32 devices in a mesh: shard: 8 (over z, core), ctx: 4 (over y, x).
Axes of the slice: x: 2, y: 2, z: 4, core: 2. Of those that a mesh axis runs over, the one named last changes fastest.
Arguments:
- tokens: bfloat16 [32, 384, 512], P('shard', 'ctx'), may hold values from -6 to 6
- lengths: int32 [32], P('shard'), may hold values from 96 to 384, as said below
- out_weight: float32 [512, 1024], P('shard'), may hold values from -0.25 to 0.25
- out_bias: float32 [1024], P('shard'), may hold values from -3 to 3
- decay_rate: float32 [512, 64], P('shard'), may hold values from 0.00026041668 to 0.05
- frequency: float32 [512, 64], P('shard'), may hold values from -0.5 to 0.5
- coef_real: float32 [512, 64], P('shard'), may hold values from -0.5 to 0.5
- coef_imag: float32 [512, 64], P('shard'), may hold values from -0.5 to 0.5
- skip: float32 [512], P('shard'), may hold values from -4 to 4
- gain: float32 [512], P('shard'), may hold values from 0.5 to 1.5
- shift: float32 [512], P('shard'), may hold values from -3 to 3
- cotangent: bfloat16 [32, 384, 512], P('shard', 'ctx'), may hold values from -6 to 6
Outputs:
- block_out: bfloat16 [32, 384, 512], P('shard', 'ctx')
- tokens_grad: bfloat16 [32, 384, 512], P('shard', 'ctx')
- out_weight_grad: float32 [512, 1024], P('shard')
- out_bias_grad: float32 [1024], P('shard')
- decay_grad: float32 [512, 64], P('shard')
- frequency_grad: float32 [512, 64], P('shard')
- coef_real_grad: float32 [512, 64], P('shard')
- coef_imag_grad: float32 [512, 64], P('shard')
- skip_grad: float32 [512], P('shard')
- gain_grad: float32 [512], P('shard')
- shift_grad: float32 [512], P('shard')
The draws below stay inside these ranges and needn't reach their ends.
Inputs may be any that keep to these rules, and one draw needn't show every extreme that they name: `lengths`: the number of valid positions of each sequence; the first sequence has all 384.
All inputs are finite; a program needn't handle non-finite values.
Results may differ from the reference program's by a relative error of at most 0.02.
Values may be sent and summed in bfloat16 or wider, within the bound.
No kernel may reach another device: no remote copies, remote signals or barrier semaphores. Data moves between devices by JAX's collectives and lax.ppermute only.
A program may use at most 128 MiB of HBM per device.

```python
import math
import jax
import jax.numpy as jnp
from jax import lax

WIDTH = 512
STATES = 64
GLU_UNITS = 1024
SEQ_LEN = 384
SEQUENCES = 32


def draw_lengths(key, part):
    drawn = jax.random.randint(key, (SEQUENCES,), SEQ_LEN // 4, SEQ_LEN + 1, dtype=jnp.int32)
    return drawn.at[0].set(SEQ_LEN)


def block_levels(key, extent, shards, smallest, top_value):
    def one(axis_at, blocks):
        heights = jax.random.uniform(jax.random.fold_in(jax.random.fold_in(key, 6), axis_at), (blocks,), jnp.float32, smallest / len(shards), top_value / len(shards))
        return jnp.repeat(jnp.exp(heights), extent[axis_at] // blocks).reshape((-1,) + (1,) * (len(extent) - axis_at - 1))

    level = one(*shards[0])
    for cut in shards[1:]:
        level = level * one(*cut)
    return level


def gaussian(stream_key, dims, scale, reach, cuts=(), kind=jnp.bfloat16):
    entries = scale * jax.random.normal(stream_key, dims, jnp.float32)
    if cuts:
        entries = entries * block_levels(stream_key, dims, cuts, -0.22, 0.18)
    return jnp.clip(entries, -reach, reach).astype(kind)


def setup_inputs(seed: int = 0) -> dict:
    key_list = jax.random.split(jax.random.key(seed), 13)
    return {
        "tokens": gaussian(key_list[0], (SEQUENCES, SEQ_LEN, WIDTH), 1.0, 6.0, ((0, 8), (1, 4))),
        "lengths": draw_lengths(jax.random.fold_in(key_list[12], 71), 0),
        "out_weight": gaussian(key_list[2], (WIDTH, GLU_UNITS), WIDTH ** -0.5, 0.25, ((0, 8),), jnp.float32),
        "out_bias": gaussian(key_list[3], (GLU_UNITS,), 0.5, 3.0, ((0, 8),), jnp.float32),
        "decay_rate": jnp.clip(jnp.exp(math.log(0.05) - 5.2574953 * jax.random.uniform(key_list[4], (WIDTH, STATES), jnp.float32) ** block_levels(key_list[4], (WIDTH, STATES), ((0, 8),), -0.2, 0.2)), 0.00026041668, 0.05),
        "frequency": jnp.clip(jax.random.uniform(key_list[5], (WIDTH, STATES), jnp.float32, -0.5, 0.5) * block_levels(key_list[5], (WIDTH, STATES), ((0, 8),), -0.4, 0.0), -0.5, 0.5),
        "coef_real": gaussian(key_list[6], (WIDTH, STATES), (2 * STATES) ** -0.5, 0.5, ((0, 8),), jnp.float32),
        "coef_imag": gaussian(key_list[7], (WIDTH, STATES), (2 * STATES) ** -0.5, 0.5, ((0, 8),), jnp.float32),
        "skip": gaussian(key_list[8], (WIDTH,), 1.0, 4.0, ((0, 8),), jnp.float32),
        "gain": jnp.clip(1.0 + 0.1 * jax.random.normal(key_list[9], (WIDTH,), jnp.float32), 0.5, 1.5),
        "shift": gaussian(key_list[10], (WIDTH,), 0.5, 3.0, ((0, 8),), jnp.float32),
        "cotangent": gaussian(key_list[11], (SEQUENCES, SEQ_LEN, WIDTH), 1.0, 6.0, ((0, 8), (1, 4))),
    }


@jax.custom_vjp
def low(v):
    return lax.optimization_barrier(v.astype(jnp.bfloat16)).astype(jnp.float32)

@jax.custom_vjp
def low_back(v):
    return v

def low_keep(v):
    return (low(v), None)

def low_pass(kept, grad):
    return (grad,)

def back_keep(v):
    return (v, None)

def back_low(kept, grad):
    return (low(grad),)
low.defvjp(low_keep, low_pass)
low_back.defvjp(back_keep, back_low)
HIGHEST = lax.Precision.HIGHEST
EPSILON = 1e-05

def conv_kernel(decay_rate, frequency, coef_real, coef_imag):
    group_size = 32
    group_total = WIDTH // group_size
    lag_steps = jnp.arange(SEQ_LEN, dtype=jnp.float32)

    def one_group(inputs):
        decay_grp, freq_grp, real_grp, imag_grp = inputs
        scale_grp = jnp.sqrt(-jnp.expm1(-2.0 * decay_grp))
        magnitude = jnp.exp(-decay_grp[:, :, None] * lag_steps)
        phase = freq_grp[:, :, None] * lag_steps
        terms = (scale_grp * real_grp)[:, :, None] * (magnitude * jnp.cos(phase)) - (scale_grp * imag_grp)[:, :, None] * (magnitude * jnp.sin(phase))
        return lax.optimization_barrier(jnp.sum(terms, axis=1))
    shaped = tuple((member.reshape(group_total, group_size, STATES) for member in (decay_rate, frequency, coef_real, coef_imag)))
    return lax.map(jax.checkpoint(one_group), shaped).reshape(WIDTH, SEQ_LEN)

def block_forward(rows, valid, out_weight, out_bias, decay_rate, frequency, coef_real, coef_imag, skip, gain, shift):
    row_mean = lax.optimization_barrier(jnp.mean(rows, axis=1, keepdims=True))
    centered = rows - row_mean
    row_var = lax.optimization_barrier(jnp.mean(centered * centered, axis=1, keepdims=True))
    normed = low(valid[:, None] * (centered * lax.rsqrt(row_var + EPSILON) * gain + shift))
    kernel = conv_kernel(decay_rate, frequency, coef_real, coef_imag)
    padded = 2 * SEQ_LEN
    spectrum = jnp.fft.rfft(normed.T, n=padded, axis=1) * jnp.fft.rfft(kernel, n=padded, axis=1)
    mixed = low_back(jnp.fft.irfft(spectrum, n=padded, axis=1)[:, :SEQ_LEN].T + skip * normed)
    hidden = low(jax.nn.gelu(mixed))
    proj = low_back(jnp.dot(hidden, low(out_weight), precision=HIGHEST) + low(out_bias))
    gated = proj[:, :WIDTH] * jax.nn.sigmoid(proj[:, WIDTH:])
    return rows + valid[:, None] * gated

def reference(tokens, lengths, out_weight, out_bias, decay_rate, frequency, coef_real, coef_imag, skip, gain, shift, cotangent):
    params = (out_weight, out_bias, decay_rate, frequency, coef_real, coef_imag, skip, gain, shift)
    positions = jnp.arange(SEQ_LEN, dtype=jnp.int32)

    def one_sequence(totals, item):
        seq_rows, seq_length, seq_cot = item
        valid = (positions < seq_length).astype(jnp.float32)
        rows_wide = seq_rows.astype(jnp.float32)

        def apply_block(row_vals, *weights):
            return block_forward(row_vals, valid, *weights)
        result, pull = jax.vjp(apply_block, rows_wide, *params)
        grads = pull(seq_cot.astype(jnp.float32))
        new_totals = tuple((total + extra for total, extra in zip(totals, grads[1:])))
        return (new_totals, (result.astype(jnp.bfloat16), grads[0].astype(jnp.bfloat16)))
    start = tuple((jnp.zeros_like(member) for member in params))
    totals, (outputs, input_grads) = lax.scan(one_sequence, start, (tokens, lengths, cotangent))
    return (outputs, input_grads, totals[0], totals[1], totals[2], totals[3], totals[4], totals[5], totals[6], totals[7], totals[8])
```

```python
import functools
import math

import jax
import jax.numpy as jnp
from jax import lax
from jax.experimental import pallas as pl
from jax.experimental.pallas import tpu as pltpu
from jax.sharding import PartitionSpec as P

EPSILON = 1e-05
LANES = 128
BOTH = ("shard", "ctx")
F32 = jnp.float32
BF16 = jnp.bfloat16
VMEM = pl.BlockSpec(memory_space=pltpu.VMEM)
SMEM = pl.BlockSpec(memory_space=pltpu.SMEM)
PARAMS = pltpu.CompilerParams(vmem_limit_bytes=56 * 1024 * 1024)


class Plan:
    def __init__(self, shards, chunks):
        layers = shards // 2
        self.shards, self.chunks = shards, chunks
        self.subs = subs = chunks // layers
        self.order = [
            (core, top * subs + sub)
            for top in range(chunks // subs)
            for core in range(2)
            for sub in range(subs)
        ]
        self.groups = [
            [(2 * z + core) * chunks + c for core, c in self.order] for z in range(layers)
        ]
        members = [(z, core, c) for z in range(layers) for core, c in self.order]

        def here(z, core, c):
            return (2 * z + core) * chunks + c

        def owner(z, core, c, turn):
            place = (z * subs + c % subs + turn) % chunks
            return (2 * (c // subs) + core) * chunks + place

        self.fetch = [(owner(*m, 0), here(*m)) for m in members]
        self.give = [[(here(*m), owner(*m, turn)) for m in members] for turn in range(chunks)]
        self.rotate = [
            [(a, (a + turn) % chunks) for a in range(chunks)] for turn in range(1, chunks)
        ]


def row_stats(rows):
    mean = jnp.mean(rows, axis=-1, keepdims=True)
    centered = rows - mean
    var = jnp.mean(centered * centered, axis=-1, keepdims=True)
    inv = lax.rsqrt(var + EPSILON)
    return centered * inv, inv


def dot(a, b, over):
    return lax.dot_general(a, b, (((over[0],), (over[1],)), ((), ())), preferred_element_type=F32)


def norm_kernel(counts, tokens, out):
    seqs, rows, width = tokens.shape
    blocks, _, chans, _ = out.shape
    pad = LANES - rows
    last = lax.broadcasted_iota(jnp.int32, (pad, width), 0) == pad - 1
    for n in range(seqs):
        xhat, _ = row_stats(tokens[n].astype(F32))
        tail = jnp.where(last, counts[n].astype(F32), 0.0)
        full = jnp.concatenate([xhat, tail], axis=0)
        out[:, n] = full.T.astype(BF16).reshape(blocks, chans, LANES)


def table_kernel(chunks, rows, pack, table, edge, taps):
    chans = pack.shape[0]
    low = lax.broadcasted_iota(jnp.int32, (1, 1, LANES), 2) < LANES // 2
    turn = jnp.where(low, 0.0, math.pi / 2)
    step = 8

    def spread(pair):
        other = pltpu.roll(pair, LANES // 2, 1)
        flag = low[0]
        return jnp.where(flag, pair, other), jnp.where(flag, other, pair)

    def complex_times(values, factor):
        other = pltpu.roll(factor, LANES // 2, 2)
        same = jnp.where(low, factor, other)
        cross = jnp.where(low, -other, factor)
        return values * same + pltpu.roll(values, LANES // 2, 2) * cross

    offsets = lax.broadcasted_iota(jnp.int32, (1, step, 1), 1).astype(F32)
    row_at = lax.broadcasted_iota(jnp.int32, (1, 2 * chunks, 1), 1)
    starts = jnp.where(row_at < chunks, rows * row_at, rows * (row_at - chunks) - LANES).astype(F32)

    def block(at, _):
        here = pl.ds(at * step, step)
        decay, freq = spread(pack[here, 0:LANES])
        real, imag = spread(pack[here, LANES : 2 * LANES])
        decay, freq = decay[:, None, :], freq[:, None, :]

        def power(by):
            return jnp.exp(-decay * by) * jnp.cos(freq * by - turn)

        part = power(offsets)
        table[here, 0:step] = part.astype(BF16)
        size = step
        while size < LANES:
            new = complex_times(part, power(jnp.full((1, 1, 1), float(size), F32)))
            table[here, size : 2 * size] = new.astype(BF16)
            part = jnp.concatenate([part, new], axis=1)
            size *= 2
        edges = power(starts)
        edge[here] = edges
        hat_same = jnp.where(low, real[:, None, :], -real[:, None, :])
        mix = hat_same * edges - imag[:, None, :] * pltpu.roll(edges, LANES // 2, 2)
        mix = jnp.where(row_at == chunks, 0.0, mix).astype(BF16)
        whole = part.astype(BF16)
        for k in range(step):
            taps[at * step + k] = dot(mix[k], whole[k], (1, 1))
        return 0

    lax.fori_loop(0, chans // step, block, 0)


def toeplitz(chunks, rows, taps):
    lane = lax.broadcasted_iota(jnp.int32, (rows, LANES), 1)
    row = lax.broadcasted_iota(jnp.int32, (rows, LANES), 0)
    upper = lane >= row

    def sheared(at):
        wide = jnp.broadcast_to(taps[at : at + 1], (rows, LANES))
        return pltpu.roll(wide, 0, 1, stride=1, stride_axis=0)

    slots = []
    for d in range(chunks):
        below = sheared(chunks + d) if d else 0.0
        slots.append(jnp.where(upper, sheared(d), below).astype(BF16))
    body = jnp.concatenate(slots, axis=1)
    return jnp.concatenate([body, jnp.zeros((LANES - rows, chunks * LANES), BF16)], axis=0)


def place(order, seqs, block, n):
    core, c = order[block]
    return (c * 2 + core) * seqs + n


def forward_kernel(chunks, rows, order, arrived, pack, taps, hidden, mixed, inputs, result, local):
    blocks, seqs, chans, _ = arrived.shape
    local[...] = pack[:, 2 * LANES :]
    total = blocks * seqs
    each = 2 * seqs
    lane = lax.broadcasted_iota(jnp.int32, (chans, LANES), 1).astype(F32)
    gain, shift = pack[:, 257:258], pack[:, 258:259]
    for b in range(blocks):
        for n in range(seqs):
            xhat = arrived[b, n].astype(F32)
            x = jnp.where(lane < xhat[:, LANES - 1 :], xhat * gain + shift, 0.0)
            inputs[pl.ds(place(order, seqs, b, n) * chans, chans), :] = x.astype(BF16).astype(F32)

    def channel(h, _):
        x = inputs[pl.ds(h, total, stride=chans), :]
        weights = toeplitz(chunks, rows, taps[h])
        out = dot(x.astype(BF16), weights, (1, 0))
        parts = []
        for d in range(chunks):
            part = out[0:each, d * LANES : (d + 1) * LANES]
            for c in range(1, d + 1):
                part += out[each * c : each * (c + 1), (d - c) * LANES : (d - c + 1) * LANES]
            parts.append(part)
        mix = jnp.concatenate(parts, axis=0) + local[pl.ds(h, 1), :][:, 0:1] * x
        mixed[h] = mix
        result[pl.ds(h, total, stride=chans), :] = jax.nn.gelu(mix)
        return 0

    lax.fori_loop(0, chans, channel, 0)
    for b in range(blocks):
        for n in range(seqs):
            at = place(order, seqs, b, n) * chans
            hidden[b, n] = result[pl.ds(at, chans), :].astype(BF16)


def glu_kernel(counts, arrived, weights, bias, tokens, cotangent, block_out, leaving, grads):
    seqs, rows, width = tokens.shape
    blocks, _, chans, _ = arrived.shape
    shards, own = weights.shape[0], width // weights.shape[0]
    w = weights[:, 0:own].reshape(width, 2 * width)
    position = lax.broadcasted_iota(jnp.int32, (rows, width), 0)
    sides, outers = [], []
    bias_sum = jnp.zeros((1, 2 * width), F32)
    for n in range(seqs):
        side = arrived[:, n].reshape(width, LANES)
        hidden = side.astype(F32).T.astype(BF16)
        proj = dot(hidden, w, (1, 0)) + bias[...]
        r, q = proj[0:rows, :width], proj[0:rows, width:]
        valid = jnp.where(position < counts[n], 1.0, 0.0)
        open_ = jax.nn.sigmoid(q)
        block_out[n] = (tokens[n].astype(F32) + valid * (r * open_)).astype(BF16)
        e = valid * cotangent[n].astype(F32)
        first = e * open_
        both = jnp.concatenate([first, first * r * (1.0 - open_)], axis=1).astype(BF16)
        bias_sum += jnp.sum(both.astype(F32), axis=0, keepdims=True)
        both = jnp.concatenate([both, jnp.zeros((LANES - rows, 2 * width), BF16)], axis=0)
        back = dot(both, w, (1, 1))
        leaving[:, n] = back.T.astype(BF16).reshape(blocks, chans, LANES)
        sides.append(side)
        outers.append(both)
    outer = dot(jnp.concatenate(sides, axis=1), jnp.concatenate(outers, axis=0), (1, 0))
    grads[:, 0:own] = outer.astype(BF16).reshape(shards, own, 2 * width)
    extra = grads.shape[1] - own
    tail = jnp.broadcast_to(bias_sum, (extra, 2 * width)).astype(BF16)
    for s in range(shards):
        grads[s, own:] = tail


def gelu_slope(x):
    c = math.sqrt(2.0 / math.pi)
    t = jnp.tanh(c * (x + 0.044715 * x * x * x))
    return 0.5 * (1.0 + t) + 0.5 * x * (1.0 - t * t) * (c * (1.0 + 3.0 * 0.044715 * x * x))


def backward_kernel(
    chunks, rows, order, arrived, first, pack, table, edge, taps, mixed,
    leaving, sums, normal, inputs, mirrored, grads, result, masks, local, ones, twos, skips, gains, shifts,
):
    blocks, seqs, chans, _ = arrived.shape
    local[...] = pack[:, 2 * LANES :]
    total = blocks * seqs
    each = 2 * seqs
    lane_row = lax.broadcasted_iota(jnp.int32, (1, LANES), 1).astype(F32)
    lane_all = lax.broadcasted_iota(jnp.int32, (chans, LANES), 1).astype(F32)
    gain_all, shift_all = pack[:, 257:258], pack[:, 258:259]
    square = (LANES, LANES)
    reach = lax.broadcasted_iota(jnp.int32, square, 0) + lax.broadcasted_iota(jnp.int32, square, 1)
    mirror = jnp.where(reach == rows - 1, 1.0, 0.0).astype(BF16)
    for b in range(blocks):
        for n in range(seqs):
            r = place(order, seqs, b, n)
            here = pl.ds(r * chans, chans)
            xhat = first[b, n].astype(F32)
            x = jnp.where(lane_all < xhat[:, LANES - 1 :], xhat * gain_all + shift_all, 0.0).astype(BF16)
            inputs[here, :] = x.astype(F32)
            mirrored[here, :] = dot(x, mirror, (1, 0))
            normal[here, :] = xhat
            grads[here, :] = arrived[b, n].astype(F32)
            masks[r : r + 1, :] = jnp.where(lane_row < xhat[0:1, LANES - 1 :], 1.0, 0.0)
    low = lax.broadcasted_iota(jnp.int32, (1, LANES), 1) < LANES // 2
    lane = lax.broadcasted_iota(jnp.int32, (rows, LANES), 1)
    row = lax.broadcasted_iota(jnp.int32, (rows, LANES), 0)
    upper = lane <= LANES - rows + row
    row_at = lax.broadcasted_iota(jnp.int32, (2 * chunks, 1), 0)
    starts = jnp.where(row_at < chunks, rows * row_at, rows * (row_at - chunks) - LANES).astype(F32)
    lags = starts + lane_row

    def channel(h, _):
        xhat = normal[pl.ds(h, total, stride=chans), :]
        valid = masks[...]
        vectors = local[pl.ds(h, 1), :]
        skip, gain = vectors[:, 0:1], vectors[:, 1:2]
        x = inputs[pl.ds(h, total, stride=chans), :]
        x_mirrored = mirrored[pl.ds(h, total, stride=chans), :].astype(BF16)
        back = grads[pl.ds(h, total, stride=chans), :]
        g = (back * gelu_slope(mixed[h])).astype(BF16).astype(F32)
        weights = toeplitz(chunks, rows, taps[h])
        empty = jnp.zeros((each, LANES), F32)
        ahead = jnp.concatenate(
            [
                jnp.concatenate(
                    [g[each * (c + d) : each * (c + d + 1)] if c + d < chunks else empty for d in range(chunks)],
                    axis=1,
                )
                for c in range(chunks)
            ],
            axis=0,
        ).astype(BF16)
        m = valid * (dot(ahead, weights, (1, 1)) + skip * g)
        result[pl.ds(h, total, stride=chans), :] = gain * m
        here = pl.ds(h, 1)
        skips[here, :] = jnp.sum(g * x, axis=0, keepdims=True)
        gains[here, :] = jnp.sum(m * xhat, axis=0, keepdims=True)
        shifts[here, :] = jnp.sum(m, axis=0, keepdims=True)
        outer = dot(x_mirrored, ahead, (0, 0))
        above, below = [], []
        for d in range(chunks):
            slid = pltpu.roll(
                outer[0:rows, d * LANES : (d + 1) * LANES],
                LANES - rows + 1, 1, stride=1, stride_axis=0,
            )
            above.append(jnp.sum(jnp.where(upper, slid, 0.0), axis=0, keepdims=True))
            if d:
                below.append(jnp.sum(jnp.where(upper, 0.0, slid), axis=0, keepdims=True))
        corr = jnp.concatenate(above + [jnp.zeros((1, LANES), F32)] + below, axis=0)
        both = jnp.concatenate([corr, corr * lags], axis=0).astype(BF16)
        turned = dot(both, table[h], (1, 0))
        factor = edge[h]
        other = pltpu.roll(factor, LANES // 2, 1)
        same = jnp.where(low, factor, other)
        cross = jnp.where(low, -other, factor)
        for k, into in enumerate((ones, twos)):
            part = turned[2 * chunks * k : 2 * chunks * (k + 1)]
            full = part * same + pltpu.roll(part, LANES // 2, 1) * cross
            into[here, :] = jnp.sum(full, axis=0, keepdims=True)
        return 0

    lax.fori_loop(0, chans, channel, 0)
    for b in range(blocks):
        for n in range(seqs):
            at = place(order, seqs, b, n) * chans
            leaving[b, n] = result[pl.ds(at, chans), :].astype(BF16)
    at = lax.broadcasted_iota(jnp.int32, (chans, LANES), 1)
    tail = jnp.zeros((chans, LANES), F32)
    for k, part in enumerate((skips, gains, shifts)):
        tail = jnp.where(at == k, jnp.sum(part[...], axis=1, keepdims=True), tail)
    sums[:, 0:LANES] = ones[...]
    sums[:, LANES : 2 * LANES] = twos[...]
    sums[:, 2 * LANES :] = tail


def final_kernel(arrived, tokens, cotangent, out):
    seqs, rows, width = tokens.shape
    for n in range(seqs):
        d = arrived[:, n].reshape(width, LANES).astype(F32).T[0:rows]
        xhat, inv = row_stats(tokens[n].astype(F32))
        mean = jnp.mean(d, axis=-1, keepdims=True)
        along = jnp.mean(d * xhat, axis=-1, keepdims=True)
        grad = (d - mean - xhat * along) * inv
        out[n] = (cotangent[n].astype(F32) + grad).astype(BF16)


def call(kernel, outs, ins, scratch=()):
    return pl.pallas_call(
        kernel,
        out_shape=[jax.ShapeDtypeStruct(*o) for o in outs],
        in_specs=ins,
        out_specs=[VMEM] * len(outs),
        scratch_shapes=list(scratch),
        compiler_params=PARAMS,
    )


def in_order(received, mine):
    count = len(received)
    twice = jnp.stack(received[::-1] * 2)
    parts = lax.dynamic_slice_in_dim(twice, count - 1 - mine, count, 0).astype(F32)
    return [parts[k] for k in range(count)]


def per_device(
    plan, tokens, lengths, out_weight, out_bias, decay_rate, frequency, coef_real, coef_imag,
    skip, gain, shift, cotangent,
):
    seqs, rows, width = tokens.shape
    chunks, subs = plan.chunks, plan.subs
    blocks = 2 * chunks
    chans = width // blocks
    own, states = decay_rate.shape
    total = blocks * seqs
    mine = lax.axis_index("ctx")
    counts = jnp.clip(lengths - mine * rows, 0, rows).astype(jnp.int32)

    def exchange(buffer):
        return lax.all_to_all(buffer, BOTH, 0, 0, axis_index_groups=plan.groups, tiled=True)

    scale = jnp.sqrt(-jnp.expm1(-2.0 * decay_rate))
    pack = jnp.concatenate(
        [decay_rate, frequency, scale * coef_real, scale * coef_imag]
        + [v[:, None] for v in (skip, gain, shift)]
        + [jnp.zeros((own, LANES - 3), F32)],
        axis=1,
    )
    sub = lax.rem(mine, subs)
    pack = lax.dynamic_slice_in_dim(pack, sub * chans, chans, 0)
    pack = lax.ppermute(pack, BOTH, plan.fetch)
    bias_row = jnp.pad(out_bias[None, :], ((0, 15), (0, 2 * width - out_bias.shape[0])))
    weights = jnp.concatenate([out_weight, bias_row], axis=0).astype(BF16)
    weights = lax.all_gather(weights, "shard")
    bias = weights[:, own, : out_bias.shape[0]].reshape(1, 2 * width).astype(F32)

    wire = ((blocks, seqs, chans, LANES), BF16)
    (first,) = call(norm_kernel, [wire], [SMEM, VMEM])(counts, tokens)
    table, edge, taps = call(
        functools.partial(table_kernel, chunks, rows),
        [
            ((chans, LANES, LANES), BF16),
            ((chans, 2 * chunks, LANES), F32),
            ((chans, 2 * chunks, LANES), F32),
        ],
        [VMEM],
    )(pack)
    first = exchange(first)
    flat = pltpu.VMEM((total * chans, LANES), F32)
    line = pltpu.VMEM((chans, LANES), F32)
    hidden, mixed = call(
        functools.partial(forward_kernel, chunks, rows, plan.order),
        [wire, ((chans, total, LANES), F32)],
        [VMEM] * 3,
        [flat, flat, line],
    )(first, pack, taps)
    hidden = exchange(hidden)
    block_out, back, grads = call(
        glu_kernel,
        [(tokens.shape, BF16), wire, ((plan.shards, own + 16, 2 * width), BF16)],
        [SMEM] + [VMEM] * 5,
    )(counts, hidden, weights, bias, tokens, cotangent)
    back = exchange(back)
    owned = lax.psum_scatter(
        grads.reshape(plan.shards * (own + 16), 2 * width), "shard", scatter_dimension=0, tiled=True
    )
    leaving, sums = call(
        functools.partial(backward_kernel, chunks, rows, plan.order),
        [wire, ((chans, 3 * LANES), F32)],
        [VMEM] * 7,
        [
            flat, flat, flat, flat, flat, pltpu.VMEM((total, LANES), F32),
            line, line, line, line, line, line,
        ],
    )(back, first, pack, table, edge, taps, mixed)
    leaving = exchange(leaving)
    (tokens_grad,) = call(final_kernel, [(tokens.shape, BF16)], [VMEM] * 3)(
        leaving, tokens, cotangent
    )

    parts = in_order([lax.ppermute(sums, BOTH, route) for route in plan.give], mine)
    totals = jnp.concatenate([sum(parts[j::subs][1:], parts[j]) for j in range(subs)], axis=0)
    one_re, one_im, two_re, two_im = (totals[:, k * states : (k + 1) * states] for k in range(4))
    hat_re, hat_im = scale * coef_real, scale * coef_imag
    grad_decay = -(hat_re * two_re - hat_im * two_im) + jnp.exp(-2.0 * decay_rate) / scale * (
        coef_real * one_re - coef_imag * one_im
    )
    grad_freq = -(hat_re * two_im + hat_im * two_re)

    parts = in_order([owned] + [lax.ppermute(owned, "ctx", route) for route in plan.rotate], mine)
    whole = sum(parts[1:], parts[0])
    segment = out_bias.shape[0]
    grad_bias = lax.dynamic_slice_in_dim(whole[own], lax.axis_index("shard") * segment, segment, 0)
    return (
        block_out,
        tokens_grad,
        whole[:own],
        grad_bias,
        grad_decay,
        grad_freq,
        scale * one_re,
        -scale * one_im,
        totals[:, 4 * states],
        totals[:, 4 * states + 1],
        totals[:, 4 * states + 2],
    )


def solution(mesh):
    plan = Plan(mesh.shape["shard"], mesh.shape["ctx"])
    rows = P("shard", "ctx", None)
    matrix = P("shard", None)
    vector = P("shard")
    in_specs = (rows, vector, matrix, vector) + (matrix,) * 4 + (vector,) * 3 + (rows,)
    out_specs = (rows, rows, matrix, vector) + (matrix,) * 4 + (vector,) * 3
    return jax.shard_map(
        functools.partial(per_device, plan),
        mesh=mesh,
        in_specs=in_specs,
        out_specs=out_specs,
        check_vma=False,
    )
```

```python
import functools
import math

import jax
import jax.numpy as jnp
from jax import lax
from jax.experimental import pallas as pl
from jax.experimental.pallas import tpu as pltpu
from jax.sharding import PartitionSpec as P

EPSILON = 1e-05
LANES = 128
GROUP = 8
COST = (2, 8, 10, 6, 1, 3, 2, 8)
BOTH = ("shard", "ctx")
F32 = jnp.float32
BF16 = jnp.bfloat16
VMEM = pl.BlockSpec(memory_space=pltpu.VMEM)
SMEM = pl.BlockSpec(memory_space=pltpu.SMEM)
HBM = pl.BlockSpec(memory_space=pltpu.HBM)
PARAMS = pltpu.CompilerParams(vmem_limit_bytes=20 * 1024 * 1024)


class Plan:
    def __init__(self, shards, chunks):
        layers = shards // 2
        self.shards, self.chunks = shards, chunks
        self.subs = subs = chunks // layers
        self.order = [
            (core, top * subs + sub)
            for top in range(chunks // subs)
            for core in range(2)
            for sub in range(subs)
        ]
        self.groups = [
            [(2 * z + core) * chunks + c for core, c in self.order] for z in range(layers)
        ]
        members = [(z, core, c) for z in range(layers) for core, c in self.order]

        def here(z, core, c):
            return (2 * z + core) * chunks + c

        def owner(z, core, c, turn):
            place = (z * subs + c % subs + turn) % chunks
            return (2 * (c // subs) + core) * chunks + place

        self.fetch = [(owner(*m, 0), here(*m)) for m in members]
        self.give = [[(here(*m), owner(*m, turn)) for m in members] for turn in range(chunks)]
        self.rotate = [
            [(a, (a + turn) % chunks) for a in range(chunks)] for turn in range(1, chunks)
        ]
        self.layers = layers
        self.climb = [
            [(s, (s + 2 * turn) % shards) for s in range(shards)] for turn in range(1, layers)
        ]
        self.across = [(s, s ^ 1) for s in range(shards)]


def row_stats(rows):
    mean = jnp.mean(rows, axis=-1, keepdims=True)
    centered = rows - mean
    var = jnp.mean(centered * centered, axis=-1, keepdims=True)
    inv = lax.rsqrt(var + EPSILON)
    return centered * inv, inv


def dot(a, b, over):
    return lax.dot_general(a, b, (((over[0],), (over[1],)), ((), ())), preferred_element_type=F32)


def pack_kernel(decay, freq, real, imag, skip, gain, shift, weight, bias, pack, scales, piece):
    own, states = decay.shape
    wide = weight.shape[1]
    rate = decay[...]
    square = rate * rate
    scale = jnp.sqrt(2.0 * rate * jnp.exp(-rate) * (1.0 + square / 6.0 * (1.0 + square / 20.0)))
    scales[...] = scale
    pack[:, 0:LANES] = jnp.concatenate([rate, freq[...]], axis=1)
    pack[:, LANES : 2 * LANES] = jnp.concatenate([scale * real[...], scale * imag[...]], axis=1)
    lane = lax.broadcasted_iota(jnp.int32, (own, LANES), 1)
    diagonal = lax.broadcasted_iota(jnp.int32, (own, own), 0) == lax.broadcasted_iota(jnp.int32, (own, own), 1)
    tail = jnp.zeros((own, LANES), F32)
    for k, vector in enumerate((skip, gain, shift)):
        column = jnp.sum(jnp.where(diagonal, vector[...], 0.0), axis=1, keepdims=True)
        tail = jnp.where(lane == k, column, tail)
    pack[:, 2 * LANES :] = tail
    piece[0:own] = weight[...].astype(BF16)
    segment = lax.broadcasted_iota(jnp.int32, (1, wide), 1) // bias.shape[1]
    repeated = jnp.concatenate([bias[...]] * (wide // bias.shape[1]), axis=1)
    row = jnp.where(segment == lax.axis_index("shard"), repeated, 0.0)
    piece[own:] = jnp.broadcast_to(row, (piece.shape[0] - own, wide)).astype(BF16)


def valid_count(lengths, n, rows):
    return jnp.clip(lengths[n] - lax.axis_index("ctx") * rows, 0, rows)


def norm_kernel(lengths, tokens, out):
    seqs, rows, width = tokens.shape
    blocks, _, chans, _ = out.shape
    pad = LANES - rows
    last = lax.broadcasted_iota(jnp.int32, (pad, width), 0) == pad - 1
    for n in range(seqs):
        xhat, _ = row_stats(tokens[n].astype(F32))
        tail = jnp.where(last, valid_count(lengths, n, rows).astype(F32), 0.0)
        full = jnp.concatenate([xhat, tail], axis=0)
        out[:, n] = full.T.astype(BF16).reshape(blocks, chans, LANES)


def swap(values):
    return pltpu.roll(values, LANES // 2, values.ndim - 1)


def table_kernel(rows, pack, table, lines, firsts):
    chans = pack.shape[0]
    low2 = lax.broadcasted_iota(jnp.int32, (1, LANES), 1) < LANES // 2
    low3 = low2[None]
    angle = jnp.where(low2, 0.0, math.pi / 2)
    step = 8
    offsets = lax.broadcasted_iota(jnp.int32, (1, step, 1), 1).astype(F32)

    def spread(pair):
        other = swap(pair)
        return jnp.where(low2, pair, other), jnp.where(low2, other, pair)

    def factors(power):
        other = swap(power)
        return jnp.where(low2, power, other), jnp.where(low2, -other, power)

    def block(at, _):
        here = pl.ds(pl.multiple_of(at * step, step), step)
        decay, freq = spread(pack[here, 0:LANES])
        real, imag = spread(pack[here, LANES : 2 * LANES])

        def power(by):
            return jnp.exp(-decay * by) * jnp.cos(freq * by - angle)

        part = jnp.exp(-decay[:, None, :] * offsets) * jnp.cos(freq[:, None, :] * offsets - angle[None])
        table[here, 0:step] = part.astype(BF16)
        size = step
        while size < LANES:
            same, cross = factors(power(float(size)))
            new = part * same[:, None, :] + swap(part) * cross[:, None, :]
            table[here, size : 2 * size] = new.astype(BF16)
            part = jnp.concatenate([part, new], axis=1)
            size *= 2
        real = jnp.where(low2, real, -real)
        whole = part.astype(BF16)
        hat = jnp.where(low2, real, -imag).astype(BF16)
        for k in range(step):
            row = jnp.broadcast_to(hat[k : k + 1], (step, LANES))
            lines[at * step + k, 0:1] = dot(row, whole[k], (1, 1))[0:1]
        one = power(1.0)
        same, cross = factors(one)
        firsts[0, here] = same
        firsts[1, here] = cross
        chunk_same, chunk_cross = factors(power(float(rows)))
        hat_re = jnp.where(low2, real, -real)
        turn_re = hat_re * same - imag * jnp.where(low2, -cross, cross)
        turn_im = hat_re * jnp.where(low2, -cross, cross) + imag * same
        for k, line in enumerate((chunk_same, chunk_cross, jnp.where(low2, turn_re, -turn_re), -turn_im)):
            lines[here, k + 1 : k + 2] = line[:, None, :]
        return 0

    lax.fori_loop(0, chans // step, block, 0)


def upper_half(rows):
    square = (rows, LANES)
    return lax.broadcasted_iota(jnp.int32, square, 1) >= lax.broadcasted_iota(jnp.int32, square, 0)


def toeplitz(upper, taps):
    slid = pltpu.roll(jnp.broadcast_to(taps, upper.shape), 0, 1, stride=1, stride_axis=0)
    body = jnp.where(upper, slid, 0.0).astype(BF16)
    return jnp.concatenate([body, jnp.zeros((LANES - upper.shape[0], LANES), BF16)], axis=0)


def mirror_matrix(rows):
    square = (LANES, LANES)
    reach = lax.broadcasted_iota(jnp.int32, square, 0) + lax.broadcasted_iota(jnp.int32, square, 1)
    return jnp.where(reach == rows - 1, 1.0, 0.0).astype(BF16)


def place(order, seqs, block, n):
    core, c = order[block]
    return (c * 2 + core) * seqs + n


def forward_kernel(
    chunks, rows, order, arrived, pack, far_table, lines, hidden, kept, inputs, mirrored, mixed, table, sem,
):
    fetch = pltpu.make_async_copy(far_table, table, sem)
    fetch.start()
    blocks, seqs, chans, _ = arrived.shape
    total = blocks * seqs
    each = 2 * seqs
    lane = lax.broadcasted_iota(jnp.int32, (1, LANES), 1).astype(F32)
    gain, shift = pack[:, 257:258], pack[:, 258:259]
    mirror = mirror_matrix(rows)
    upper = upper_half(rows)
    for b in range(blocks):
        for n in range(seqs):
            here = pl.ds(place(order, seqs, b, n) * chans, chans)
            xhat = arrived[b, n].astype(F32)
            x = jnp.where(lane < xhat[0:1, LANES - 1 :], xhat * gain + shift, 0.0).astype(BF16)
            inputs[here, :] = x.astype(F32)
            mirrored[here, :] = dot(x, mirror, (1, 0))

    def group(at, _):
        members = range(GROUP)
        mine = [pl.ds(at * GROUP + k, total, stride=chans) for k in members]
        line = [lines[at * GROUP + k] for k in members]
        ends = [dot(mirrored[mine[k], :].astype(BF16), table[at * GROUP + k], (1, 0)) for k in members]
        local = [
            dot(inputs[mine[k], :].astype(BF16), toeplitz(upper, line[k][0:1]), (1, 0)) for k in members
        ]
        for k in members:
            state = ends[k][0:each]
            carried = [jnp.zeros((each, LANES), F32)]
            for c in range(1, chunks):
                carried.append(state * line[k][3:4] + swap(state) * line[k][4:5])
                if c < chunks - 1:
                    state = state * line[k][1:2] + swap(state) * line[k][2:3]
                    state += ends[k][each * c : each * (c + 1)]
            ends[k] = jnp.concatenate(carried, axis=0).astype(BF16)
        for k in members:
            mixed[mine[k], :] = local[k] + dot(ends[k], table[at * GROUP + k], (1, 1))
        return 0

    fetch.wait()
    lax.fori_loop(0, chans // GROUP, group, 0)
    skip = pack[:, 256:257]
    for b in range(blocks):
        for n in range(seqs):
            here = pl.ds(place(order, seqs, b, n) * chans, chans)
            mix = mixed[here, :] + skip * inputs[here, :]
            kept[here, :] = mix.astype(BF16)
            hidden[b, n] = jax.nn.gelu(mix).astype(BF16)


def weight_kernel(plan, *refs):
    pieces, (w, bias) = refs[:-2], refs[-2:]
    layers = plan.layers
    width = w.shape[0]
    own = width // plan.shards
    shard = lax.axis_index("shard")
    layer, core = shard // 2, lax.rem(shard, 2)
    total = jnp.zeros((1, 2 * width), F32)
    for side in range(2):
        for turn in range(layers):
            piece = pieces[side * layers + turn]
            home = 2 * lax.rem(layer + layers - turn, layers) + lax.rem(core + side, 2)
            w[pl.ds(pl.multiple_of(home * own, own), own), :] = piece[0:own]
            total += piece[own : own + 1].astype(F32)
    bias[...] = total


def glu_kernel(lengths, arrived, tokens, cotangent, w, bias, block_out, leaving, outers):
    seqs, rows, width = tokens.shape
    blocks, _, chans, _ = arrived.shape
    position = lax.broadcasted_iota(jnp.int32, (rows, width), 0)
    for n in range(seqs):
        hidden = arrived[:, n].reshape(width, LANES).astype(F32).T.astype(BF16)
        proj = dot(hidden, w[...], (1, 0)) + bias[...]
        r, q = proj[0:rows, :width], proj[0:rows, width:]
        valid = jnp.where(position < valid_count(lengths, n, rows), 1.0, 0.0)
        open_ = jax.nn.sigmoid(q)
        block_out[n] = (tokens[n].astype(F32) + valid * (r * open_)).astype(BF16)
        e = valid * cotangent[n].astype(F32)
        first = e * open_
        both = jnp.concatenate([first, first * r * (1.0 - open_)], axis=1).astype(BF16)
        both = jnp.concatenate([both, jnp.zeros((LANES - rows, 2 * width), BF16)], axis=0)
        back = dot(both, w[...], (1, 1))
        leaving[:, n] = back.T.astype(BF16).reshape(blocks, chans, LANES)
        outers[pl.ds(n * LANES, LANES), :] = both


def outer_kernel(plan, arrived, outers, kept, sent):
    blocks, seqs, chans, _ = arrived.shape
    layers, subs = plan.layers, plan.subs
    own = chans * subs
    wide = outers.shape[1]
    core = lax.rem(lax.axis_index("shard"), 2)
    outer = outers[...]
    bias = jnp.sum(outer.astype(F32), axis=0, keepdims=True)
    tail = jnp.broadcast_to(bias, (kept.shape[1] - own, wide)).astype(BF16)
    for side, out in enumerate((sent, kept)):
        which = lax.rem(core + 1 - side, 2)
        left = jnp.concatenate(
            [
                jnp.concatenate([arrived[(2 * z + which) * subs + sub, n] for n in range(seqs)], axis=1)
                for z in range(layers)
                for sub in range(subs)
            ],
            axis=0,
        )
        out[:, 0:own] = dot(left, outer, (1, 0)).astype(BF16).reshape(layers, own, wide)
        for z in range(layers):
            out[z, own:] = tail


def gelu_slope(x):
    c = math.sqrt(2.0 / math.pi)
    t = jnp.tanh(c * (x + 0.044715 * x * x * x))
    return 0.5 * (1.0 + t) + 0.5 * x * (1.0 - t * t) * (c * (1.0 + 3.0 * 0.044715 * x * x))


def backward_kernel(
    chunks, rows, order, arrived, first, pack, far_table, lines, mixed,
    leaving, kept, tallies, grads, local, cross, table, sem,
):
    fetch = pltpu.make_async_copy(far_table, table, sem)
    fetch.start()
    blocks, seqs, chans, _ = arrived.shape
    total = blocks * seqs
    each = 2 * seqs
    lane = lax.broadcasted_iota(jnp.int32, (1, LANES), 1).astype(F32)
    skip, gain = pack[:, 256:257], pack[:, 257:258]
    mirror = mirror_matrix(rows)
    upper = upper_half(rows)
    for b in range(blocks):
        for n in range(seqs):
            here = pl.ds(place(order, seqs, b, n) * chans, chans)
            g = (arrived[b, n].astype(F32) * gelu_slope(mixed[here, :].astype(F32))).astype(BF16)
            kept[here, :] = g
            grads[here, :] = g.astype(F32)

    def group(at, _):
        members = range(GROUP)
        which = [at * GROUP + k for k in members]
        mine = [pl.ds(h, total, stride=chans) for h in which]
        line = [lines[h] for h in which]
        ends = [dot(grads[mine[k], :].astype(BF16), table[which[k]], (1, 0)) for k in members]
        for k in members:
            g = grads[mine[k], :].astype(BF16)
            local[mine[k], :] = dot(g, toeplitz(upper, line[k][0:1]), (1, 1))
        for k in members:
            parts = [jnp.zeros((each, LANES), F32)]
            state = ends[k][each * (chunks - 1) :]
            for c in range(chunks - 2, -1, -1):
                parts.append(state * line[k][3:4] + swap(state) * line[k][4:5])
                if c:
                    state = state * line[k][1:2] + swap(state) * line[k][2:3]
                    state += ends[k][each * c : each * (c + 1)]
            ends[k] = jnp.concatenate(parts[::-1], axis=0).astype(BF16)
        for k in members:
            cross[mine[k], :] = dot(ends[k], table[which[k]], (1, 1))
        return 0

    fetch.wait()
    lax.fori_loop(0, chans // GROUP, group, 0)
    gains = shifts = jnp.zeros((chans, LANES), F32)
    for b in range(blocks):
        for n in range(seqs):
            here = pl.ds(place(order, seqs, b, n) * chans, chans)
            grad = local[here, :] + skip * grads[here, :]
            grad += dot(cross[here, :].astype(BF16), mirror, (1, 0))
            xhat = first[b, n].astype(F32)
            m = jnp.where(lane < xhat[0:1, LANES - 1 :], grad, 0.0)
            gains += m * xhat
            shifts += m
            leaving[b, n] = (gain * m).astype(BF16)
    tallies[0] = gains
    tallies[1] = shifts


def moment_kernel(
    chunks, rows, order, first, pack, table, lines, firsts, kept, tallies, sums, mirrored, grads,
    cross_one_a, cross_one_b, cross_two_a, cross_two_b, local_one, local_two,
):
    blocks, seqs, chans, _ = first.shape
    total = blocks * seqs
    each = 2 * seqs
    lane = lax.broadcasted_iota(jnp.int32, (1, LANES), 1).astype(F32)
    gain, shift = pack[:, 257:258], pack[:, 258:259]
    mirror = mirror_matrix(rows)
    skips = jnp.zeros((chans, LANES), F32)
    for b in range(blocks):
        for n in range(seqs):
            here = pl.ds(place(order, seqs, b, n) * chans, chans)
            xhat = first[b, n].astype(F32)
            x = jnp.where(lane < xhat[0:1, LANES - 1 :], xhat * gain + shift, 0.0).astype(BF16)
            mirrored[here, :] = dot(x, mirror, (1, 0))
            g = kept[here, :].astype(F32)
            grads[here, :] = g
            skips += g * x.astype(F32)
    square = (rows, LANES)
    behind = lax.broadcasted_iota(jnp.int32, square, 1) <= (
        LANES - rows + lax.broadcasted_iota(jnp.int32, square, 0)
    )

    def group(place_at, _):
        members = range(GROUP)
        which = [place_at * GROUP + k for k in members]
        mine = [pl.ds(h, total, stride=chans) for h in which]
        line = [lines[h] for h in which]
        ends, outer, pairs = [], [], []
        for k in members:
            x_back, g = mirrored[mine[k], :], grads[mine[k], :]
            stack = jnp.concatenate([x_back, g, x_back * lane, g * lane], axis=0).astype(BF16)
            ends.append(dot(stack, table[which[k]], (1, 0)))
        for k in members:
            g = grads[mine[k], :].astype(BF16)
            outer.append(dot(mirrored[mine[k], :].astype(BF16), g, (0, 0)))
        for k in members:
            swapped = swap(ends[k])

            def at(kind, c, of=ends[k]):
                start = kind * total + each * c
                return of[start : start + each]

            def onward(state):
                return state * line[k][1:2] + swap(state) * line[k][2:3]

            one_a = one_b = two_a = two_b = jnp.zeros((each, LANES), F32)
            state, slope = at(0, 0), at(2, 0)
            for c in range(1, chunks):
                both = state + slope
                one_a += state * at(1, c)
                one_b += state * at(1, c, swapped)
                two_a += both * at(1, c) + state * at(3, c)
                two_b += both * at(1, c, swapped) + state * at(3, c, swapped)
                if c < chunks - 1:
                    slope = onward(slope + float(rows) * state) + at(2, c)
                    state = onward(state) + at(0, c)
            for into, value in (
                (cross_one_a, one_a), (cross_one_b, one_b), (cross_two_a, two_a), (cross_two_b, two_b),
            ):
                into[pl.ds(which[k], 1), :] = jnp.sum(value, axis=0, keepdims=True)
            slid = pltpu.roll(outer[k][0:rows], LANES - rows + 1, 1, stride=1, stride_axis=0)
            corr = jnp.sum(jnp.where(behind, slid, 0.0), axis=0, keepdims=True)
            pair = jnp.concatenate([corr, corr * lane, jnp.zeros((6, LANES), F32)], axis=0)
            pairs.append(pair.astype(BF16))
        for k in members:
            turned = dot(pairs[k], table[which[k]], (1, 0))
            local_one[pl.ds(which[k], 1), :] = turned[0:1]
            local_two[pl.ds(which[k], 1), :] = turned[1:2]
        return 0

    lax.fori_loop(0, chans // GROUP, group, 0)
    low = lax.broadcasted_iota(jnp.int32, (1, LANES), 1) < LANES // 2
    for k, (a, b, near) in enumerate(
        ((cross_one_a, cross_one_b, local_one), (cross_two_a, cross_two_b, local_two))
    ):
        far = jnp.where(low, a[...] - swap(a[...]), b[...] + swap(b[...]))
        moment = far * firsts[0] + swap(far) * firsts[1] + near[...]
        sums[0:chans, k * LANES : (k + 1) * LANES] = moment.astype(BF16)
    diagonal = lax.broadcasted_iota(jnp.int32, (chans, 2 * LANES), 0) == lax.broadcasted_iota(
        jnp.int32, (chans, 2 * LANES), 1
    )
    row = lax.broadcasted_iota(jnp.int32, (16, 2 * LANES), 0)
    tail = jnp.zeros((16, 2 * LANES), F32)
    for k, part in enumerate((skips, tallies[0], tallies[1])):
        column = jnp.sum(part, axis=1, keepdims=True)
        line = jnp.sum(jnp.where(diagonal, column, 0.0), axis=0, keepdims=True)
        tail = jnp.where(row == k, line, tail)
    sums[chans:, :] = tail.astype(BF16)


def share_kernel(layers, kept, came, *outs):
    layer = lax.axis_index("shard") // 2
    for turn, out in enumerate(outs):
        at = lax.rem(layer + turn, layers)
        out[...] = (kept[at].astype(F32) + came[at].astype(F32)).astype(BF16)


def add_kernel(*refs):
    total = refs[0][...].astype(F32)
    for ref in refs[1:-1]:
        total += ref[...].astype(F32)
    refs[-1][...] = total.astype(BF16)


def ordered(parts, slots):
    count = len(parts)
    mine = lax.axis_index("ctx")
    for turn, part in enumerate(parts):
        slots[lax.rem(mine + count - turn, count)] = part[...]


def owner_kernel(chunks, *refs):
    parts, (grad, bias, slots) = refs[:chunks], refs[chunks:]
    own, segment = grad.shape[0], bias.shape[1]
    ordered(parts, slots)
    total = slots[0].astype(F32)
    for k in range(1, chunks):
        total += slots[k].astype(F32)
    grad[...] = total[0:own]
    shard = lax.axis_index("shard")
    row = jnp.zeros((1, segment), F32)
    for s in range(total.shape[1] // segment):
        row = jnp.where(shard == s, total[own : own + 1, s * segment : (s + 1) * segment], row)
    bias[...] = row


def state_kernel(chunks, subs, *refs):
    parts, (decay, scale_in, real, imag), outs = refs[:chunks], refs[chunks : chunks + 4], refs[chunks + 4 :]
    grad_decay, grad_freq, grad_real, grad_imag, *vectors, slots = outs
    ordered(parts, slots)
    own, states = decay.shape
    chans = own // subs
    sums = []
    for sub in range(subs):
        total = slots[sub].astype(F32)
        for k in range(sub + subs, chunks, subs):
            total += slots[k].astype(F32)
        sums.append(total)
    moments = jnp.concatenate([t[0:chans] for t in sums], axis=0)
    one_re, one_im, two_re, two_im = (moments[:, k * states : (k + 1) * states] for k in range(4))
    scale = scale_in[...]
    hat_re, hat_im = scale * real[...], scale * imag[...]
    grad_decay[...] = -(hat_re * two_re - hat_im * two_im) + jnp.exp(-2.0 * decay[...]) / scale * (
        real[...] * one_re - imag[...] * one_im
    )
    grad_freq[...] = -(hat_re * two_im + hat_im * two_re)
    grad_real[...] = scale * one_re
    grad_imag[...] = -scale * one_im
    for k, vector in enumerate(vectors):
        lines = [t[chans + k : chans + k + 1, 0:chans] for t in sums]
        vector[...] = jnp.concatenate(lines, axis=1) if subs > 1 else lines[0]


def final_kernel(arrived, tokens, cotangent, out):
    seqs, rows, width = tokens.shape
    for n in range(seqs):
        d = arrived[:, n].reshape(width, LANES).astype(F32).T[0:rows]
        xhat, inv = row_stats(tokens[n].astype(F32))
        mean = jnp.mean(d, axis=-1, keepdims=True)
        along = jnp.mean(d * xhat, axis=-1, keepdims=True)
        grad = (d - mean - xhat * along) * inv
        out[n] = (cotangent[n].astype(F32) + grad).astype(BF16)


def call(kernel, micros, outs, ins, scratch=()):
    return pl.pallas_call(
        kernel,
        out_shape=[(pltpu.HBM if len(o) > 2 else jax.ShapeDtypeStruct)(*o[:2]) for o in outs],
        in_specs=ins,
        out_specs=[VMEM] * len(outs),
        scratch_shapes=list(scratch),
        compiler_params=PARAMS,
        cost_estimate=pl.CostEstimate(
            flops=int(micros * 1e9), bytes_accessed=int(micros * 3.5e6), transcendentals=0
        ),
    )


def in_hbm(*arrays):
    return [pltpu.with_memory_space_constraint(a, pltpu.HBM) for a in arrays]


def per_device(
    plan, tokens, lengths, out_weight, out_bias, decay_rate, frequency, coef_real, coef_imag,
    skip, gain, shift, cotangent,
):
    seqs, rows, width = tokens.shape
    chunks, subs = plan.chunks, plan.subs
    blocks = 2 * chunks
    chans = width // blocks
    own, states = decay_rate.shape
    total = blocks * seqs
    mine, shard = lax.axis_index("ctx"), lax.axis_index("shard")
    layer = shard // 2

    def exchange(buffer):
        return lax.all_to_all(buffer, BOTH, 0, 0, axis_index_groups=plan.groups, tiled=True)

    segment = out_bias.shape[0]
    pack, scale, piece = call(
        pack_kernel,
        2,
        [((own, 3 * LANES), F32), ((own, states), F32), ((own + 16, 2 * width), BF16)],
        [VMEM] * 9,
    )(
        *in_hbm(
            decay_rate, frequency, coef_real, coef_imag,
            skip[None], gain[None], shift[None], out_weight, out_bias[None],
        )
    )
    if subs > 1:
        pack = lax.dynamic_slice_in_dim(pack, lax.rem(mine, subs) * chans, chans, 0)
    pack = lax.ppermute(pack, BOTH, plan.fetch)

    wire = ((blocks, seqs, chans, LANES), BF16)
    (first,) = call(norm_kernel, COST[0], [wire], [SMEM, VMEM])(lengths, tokens)
    first = exchange(first)
    piece, pack = lax.optimization_barrier((piece, pack))
    near = [piece] + [lax.ppermute(piece, "shard", route) for route in plan.climb]
    table_type = ((chans, LANES, LANES), BF16, 1)
    table, lines, firsts = call(
        functools.partial(table_kernel, rows),
        COST[1],
        [table_type, ((chans, 8, LANES), F32), ((2, chans, LANES), F32)],
        [VMEM],
    )(pack)
    buffer = pltpu.VMEM((total * chans, LANES), F32)
    line = pltpu.VMEM((chans, LANES), F32)
    fetched = [pltpu.VMEM(*table_type[:2]), pltpu.SemaphoreType.DMA]
    low = ((total * chans, LANES), BF16)
    hidden, mixed = call(
        functools.partial(forward_kernel, chunks, rows, plan.order),
        COST[2],
        [wire, low],
        [VMEM, VMEM, HBM, VMEM],
        [buffer, buffer, buffer] + fetched,
    )(first, pack, table, lines)
    hidden, near = lax.optimization_barrier((hidden, near))
    across = [lax.ppermute(p, "shard", plan.across) for p in near]
    hidden = exchange(hidden)
    weight, bias = call(
        functools.partial(weight_kernel, plan),
        2,
        [((width, 2 * width), BF16), ((1, 2 * width), F32)],
        [VMEM] * (2 * plan.layers),
    )(*near, *across)
    half = ((plan.layers, own + 16, 2 * width), BF16)
    block_out, back, outers = call(
        glu_kernel,
        COST[3],
        [(tokens.shape, BF16), wire, ((seqs * LANES, 2 * width), BF16)],
        [SMEM] + [VMEM] * 5,
    )(lengths, hidden, tokens, cotangent, weight, bias)
    back = exchange(back)
    kept, sent = call(functools.partial(outer_kernel, plan), 2, [half, half], [VMEM] * 2)(hidden, outers)

    came = lax.ppermute(sent, "shard", plan.across)
    slab = ((own + 16, 2 * width), BF16)
    shares = call(
        functools.partial(share_kernel, plan.layers), COST[6], [slab] * plan.layers, [VMEM] * 2
    )(kept, came)
    back, shares = lax.optimization_barrier((back, shares))
    climbed = [lax.ppermute(v, "shard", route) for v, route in zip(shares[1:], plan.climb)]
    leaving, local_grads, tallies = call(
        functools.partial(backward_kernel, chunks, rows, plan.order),
        COST[4],
        [wire, low, ((2, chans, LANES), F32)],
        [VMEM, VMEM, VMEM, HBM, VMEM, VMEM],
        [buffer, buffer, buffer] + fetched,
    )(back, first, pack, table, lines, mixed)
    (owned,) = call(add_kernel, 1, [slab], [VMEM] * plan.layers)(shares[0], *climbed)
    tallies, owned = lax.optimization_barrier((tallies, owned))
    state = (chans + 16, 2 * LANES)
    (sums,) = call(
        functools.partial(moment_kernel, chunks, rows, plan.order),
        COST[7],
        [(state, BF16)],
        [VMEM] * 7,
        [buffer, buffer] + [line] * 6,
    )(first, pack, table, lines, firsts, local_grads, tallies)
    leaving = exchange(leaving)
    (tokens_grad,) = call(final_kernel, COST[5], [(tokens.shape, BF16)], [VMEM] * 3)(
        leaving, tokens, cotangent
    )

    parts = [lax.ppermute(sums, BOTH, route) for route in plan.give]
    wholes = [owned] + [lax.ppermute(owned, "ctx", route) for route in plan.rotate]
    tokens_grad, parts, wholes = lax.optimization_barrier((tokens_grad, parts, wholes))
    grad_weight, grad_bias = call(
        functools.partial(owner_kernel, chunks),
        2,
        [(out_weight.shape, F32), ((1, segment), F32)],
        [VMEM] * chunks,
        [pltpu.VMEM((chunks,) + slab[0], BF16)],
    )(*wholes)
    matrix, vector = ((own, states), F32), ((1, own), F32)
    grads = call(
        functools.partial(state_kernel, chunks, subs),
        2,
        [matrix] * 4 + [vector] * 3,
        [VMEM] * (chunks + 4),
        [pltpu.VMEM((chunks,) + state, BF16)],
    )(*parts, decay_rate, scale, coef_real, coef_imag)
    return (
        block_out,
        tokens_grad,
        grad_weight,
        grad_bias[0],
        *grads[:4],
        *(v[0] for v in grads[4:]),
    )


def solution(mesh):
    plan = Plan(mesh.shape["shard"], mesh.shape["ctx"])
    rows = P("shard", "ctx", None)
    matrix = P("shard", None)
    vector = P("shard")
    in_specs = (rows, vector, matrix, vector) + (matrix,) * 4 + (vector,) * 3 + (rows,)
    out_specs = (rows, rows, matrix, vector) + (matrix,) * 4 + (vector,) * 3
    return jax.shard_map(
        functools.partial(per_device, plan),
        mesh=mesh,
        in_specs=in_specs,
        out_specs=out_specs,
        check_vma=False,
    )
```

```python
import functools
import math

import jax
import jax.numpy as jnp
from jax import lax
from jax.experimental import pallas as pl
from jax.experimental.pallas import tpu as pltpu
from jax.sharding import PartitionSpec as P

EPSILON = 1e-05
LANES = 128
GROUPS = (32, 16, 16, 16)
COST = (2, 8, 10, 6, 1, 3, 2, 8)
BOTH = ("shard", "ctx")
F32 = jnp.float32
BF16 = jnp.bfloat16
VMEM = pl.BlockSpec(memory_space=pltpu.VMEM)
SMEM = pl.BlockSpec(memory_space=pltpu.SMEM)
HBM = pl.BlockSpec(memory_space=pltpu.HBM)
PARAMS = pltpu.CompilerParams(vmem_limit_bytes=20 * 1024 * 1024)


class Plan:
    def __init__(self, shards, chunks):
        layers = shards // 2
        self.shards, self.chunks = shards, chunks
        self.subs = subs = chunks // layers
        self.order = [
            (core, top * subs + sub)
            for top in range(chunks // subs)
            for core in range(2)
            for sub in range(subs)
        ]
        self.groups = [
            [(2 * z + core) * chunks + c for core, c in self.order] for z in range(layers)
        ]
        members = [(z, core, c) for z in range(layers) for core, c in self.order]

        def here(z, core, c):
            return (2 * z + core) * chunks + c

        def owner(z, core, c, turn):
            place = (z * subs + c % subs + turn) % chunks
            return (2 * (c // subs) + core) * chunks + place

        self.fetch = [(owner(*m, 0), here(*m)) for m in members]
        self.give = [[(here(*m), owner(*m, turn)) for m in members] for turn in range(chunks)]
        self.fold = [
            [(a, a ^ (1 << bit)) for a in range(chunks)] for bit in range((chunks - 1).bit_length())
        ]
        self.layers = layers
        self.climb = [
            [(s, (s + 2 * turn) % shards) for s in range(shards)] for turn in range(1, layers)
        ]
        self.across = [(s, s ^ 1) for s in range(shards)]


def row_stats(rows):
    mean = jnp.mean(rows, axis=-1, keepdims=True)
    centered = rows - mean
    var = jnp.mean(centered * centered, axis=-1, keepdims=True)
    inv = lax.rsqrt(var + EPSILON)
    return centered * inv, inv


def dot(a, b, over):
    return lax.dot_general(a, b, (((over[0],), (over[1],)), ((), ())), preferred_element_type=F32)


def pack_kernel(decay, freq, real, imag, skip, gain, shift, weight, bias, pack, scales, piece):
    own, states = decay.shape
    wide = weight.shape[1]
    rate = decay[...]
    square = rate * rate
    scale = jnp.sqrt(2.0 * rate * jnp.exp(-rate) * (1.0 + square / 6.0 * (1.0 + square / 20.0)))
    scales[...] = scale
    pack[:, 0:LANES] = jnp.concatenate([rate, freq[...]], axis=1)
    pack[:, LANES : 2 * LANES] = jnp.concatenate([scale * real[...], scale * imag[...]], axis=1)
    lane = lax.broadcasted_iota(jnp.int32, (own, LANES), 1)
    diagonal = lax.broadcasted_iota(jnp.int32, (own, own), 0) == lax.broadcasted_iota(jnp.int32, (own, own), 1)
    tail = jnp.zeros((own, LANES), F32)
    for k, vector in enumerate((skip, gain, shift)):
        column = jnp.sum(jnp.where(diagonal, vector[...], 0.0), axis=1, keepdims=True)
        tail = jnp.where(lane == k, column, tail)
    pack[:, 2 * LANES :] = tail
    piece[0:own] = weight[...].astype(BF16)
    segment = lax.broadcasted_iota(jnp.int32, (1, wide), 1) // bias.shape[1]
    repeated = jnp.concatenate([bias[...]] * (wide // bias.shape[1]), axis=1)
    row = jnp.where(segment == lax.axis_index("shard"), repeated, 0.0)
    piece[own:] = jnp.broadcast_to(row, (piece.shape[0] - own, wide)).astype(BF16)


def copying(source, target, sem):
    copy = pltpu.make_async_copy(source, target, sem)
    copy.start()
    return copy


def wait_all(copies):
    for copy in copies:
        copy.wait()


def valid_count(lengths, n, rows):
    return jnp.clip(lengths[n] - lax.axis_index("ctx") * rows, 0, rows)


def norm_kernel(lengths, tokens, out):
    seqs, rows, width = tokens.shape
    blocks, _, chans, _ = out.shape
    pad = LANES - rows
    last = lax.broadcasted_iota(jnp.int32, (pad, width), 0) == pad - 1
    for n in range(seqs):
        xhat, _ = row_stats(tokens[n].astype(F32))
        tail = jnp.where(last, valid_count(lengths, n, rows).astype(F32), 0.0)
        full = jnp.concatenate([xhat, tail], axis=0)
        out[:, n] = full.T.astype(BF16).reshape(blocks, chans, LANES)


def swap(values):
    return pltpu.roll(values, LANES // 2, values.ndim - 1)


def table_kernel(rows, pack, far_table, far_lines, firsts, table, lines, sems):
    chans = pack.shape[0]
    low2 = lax.broadcasted_iota(jnp.int32, (1, LANES), 1) < LANES // 2
    low3 = low2[None]
    angle = jnp.where(low2, 0.0, math.pi / 2)
    step = 8
    offsets = lax.broadcasted_iota(jnp.int32, (1, step, 1), 1).astype(F32)

    def spread(pair):
        other = swap(pair)
        return jnp.where(low2, pair, other), jnp.where(low2, other, pair)

    def factors(power):
        other = swap(power)
        return jnp.where(low2, power, other), jnp.where(low2, -other, power)

    def block(at, _):
        here = pl.ds(pl.multiple_of(at * step, step), step)
        decay, freq = spread(pack[here, 0:LANES])
        real, imag = spread(pack[here, LANES : 2 * LANES])

        def power(by):
            return jnp.exp(-decay * by) * jnp.cos(freq * by - angle)

        part = jnp.exp(-decay[:, None, :] * offsets) * jnp.cos(freq[:, None, :] * offsets - angle[None])
        table[here, 0:step] = part.astype(BF16)
        size = step
        while size < LANES:
            same, cross = factors(power(float(size)))
            new = part * same[:, None, :] + swap(part) * cross[:, None, :]
            table[here, size : 2 * size] = new.astype(BF16)
            part = jnp.concatenate([part, new], axis=1)
            size *= 2
        copying(table.at[here], far_table.at[here], sems.at[at])
        real = jnp.where(low2, real, -real)
        whole = part.astype(BF16)
        hat = jnp.where(low2, real, -imag).astype(BF16)
        for k in range(step):
            row = jnp.broadcast_to(hat[k : k + 1], (step, LANES))
            lines[at * step + k, 0:1] = dot(row, whole[k], (1, 1))[0:1]
        one = power(1.0)
        same, cross = factors(one)
        firsts[0, here] = same
        firsts[1, here] = cross
        chunk_same, chunk_cross = factors(power(float(rows)))
        hat_re = jnp.where(low2, real, -real)
        turn_re = hat_re * same - imag * jnp.where(low2, -cross, cross)
        turn_im = hat_re * jnp.where(low2, -cross, cross) + imag * same
        for k, line in enumerate((chunk_same, chunk_cross, jnp.where(low2, turn_re, -turn_re), -turn_im)):
            lines[here, k + 1 : k + 2] = line[:, None, :]
        return 0

    count = chans // step
    lax.fori_loop(0, count, block, 0, unroll=min(4, count))
    for at in range(count):
        here = pl.ds(at * step, step)
        pltpu.make_async_copy(table.at[here], far_table.at[here], sems.at[at]).wait()
    copying(lines, far_lines, sems.at[count]).wait()


def upper_half(rows):
    square = (rows, LANES)
    return lax.broadcasted_iota(jnp.int32, square, 1) >= lax.broadcasted_iota(jnp.int32, square, 0)


def toeplitz(upper, taps):
    slid = pltpu.roll(jnp.broadcast_to(taps, upper.shape), 0, 1, stride=1, stride_axis=0)
    body = jnp.where(upper, slid, 0.0).astype(BF16)
    return jnp.concatenate([body, jnp.zeros((LANES - upper.shape[0], LANES), BF16)], axis=0)


def mirror_matrix(rows):
    square = (LANES, LANES)
    reach = lax.broadcasted_iota(jnp.int32, square, 0) + lax.broadcasted_iota(jnp.int32, square, 1)
    return jnp.where(reach == rows - 1, 1.0, 0.0).astype(BF16)


def place(order, seqs, block, n):
    core, c = order[block]
    return (c * 2 + core) * seqs + n


def fetch_tables(size, far_table, table, far_lines, lines, sems):
    count = table.shape[0] // size
    copying(far_lines, lines, sems.at[count])
    for at in range(count):
        here = pl.ds(at * size, size)
        copying(far_table.at[here], table.at[here], sems.at[at])


def await_table(size, far_table, table, sems, at):
    here = pl.ds(at * size, size)
    pltpu.make_async_copy(far_table.at[here], table.at[here], sems.at[at]).wait()


def await_lines(size, far_lines, lines, sems):
    pltpu.make_async_copy(far_lines, lines, sems.at[lines.shape[0] // size]).wait()


def gelu_and_slope(x):
    c = math.sqrt(2.0 / math.pi)
    square = x * x
    t = jnp.tanh(c * x * (1.0 + 0.044715 * square))
    half = 0.5 * (1.0 + t)
    return x * half, half + 0.5 * x * (1.0 - t * t) * (c + 3.0 * 0.044715 * c * square)


def forward_kernel(
    chunks, rows, order, arrived, pack, far_table, far_lines, far_hidden, far_kept,
    inputs, mirrored, mixed, hidden, kept, table, lines, sems, out_sems,
):
    size = min(GROUPS[0], far_table.shape[0])
    fetch_tables(size, far_table, table, far_lines, lines, sems)
    blocks, seqs, chans, _ = arrived.shape
    total = blocks * seqs
    each = 2 * seqs
    lane = lax.broadcasted_iota(jnp.int32, (1, LANES), 1).astype(F32)
    gain, shift = pack[:, 257:258], pack[:, 258:259]
    mirror = mirror_matrix(rows)
    upper = upper_half(rows)
    for b in range(blocks):
        for n in range(seqs):
            here = pl.ds(place(order, seqs, b, n) * chans, chans)
            xhat = arrived[b, n].astype(F32)
            x = jnp.where(lane < xhat[0:1, LANES - 1 :], xhat * gain + shift, 0.0).astype(BF16)
            inputs[here, :] = x.astype(F32)
            mirrored[here, :] = dot(x, mirror, (1, 0))

    def group(at, _):
        members = range(size)
        await_table(size, far_table, table, sems, at)
        mine = [pl.ds(at * size + k, total, stride=chans) for k in members]
        line = [lines[at * size + k] for k in members]
        ends = [dot(mirrored[mine[k], :].astype(BF16), table[at * size + k], (1, 0)) for k in members]
        local = [
            dot(inputs[mine[k], :].astype(BF16), toeplitz(upper, line[k][0:1]), (1, 0)) for k in members
        ]
        for k in members:
            state = ends[k][0:each]
            carried = [jnp.zeros((each, LANES), F32)]
            for c in range(1, chunks):
                carried.append(state * line[k][3:4] + swap(state) * line[k][4:5])
                if c < chunks - 1:
                    state = state * line[k][1:2] + swap(state) * line[k][2:3]
                    state += ends[k][each * c : each * (c + 1)]
            ends[k] = jnp.concatenate(carried, axis=0).astype(BF16)
        for k in members:
            mixed[mine[k], :] = local[k] + dot(ends[k], table[at * size + k], (1, 1))
        return 0

    await_lines(size, far_lines, lines, sems)
    lax.fori_loop(0, chans // size, group, 0)
    stored = []
    skip = pack[:, 256:257]
    for b in range(blocks):
        for n in range(seqs):
            here = pl.ds(place(order, seqs, b, n) * chans, chans)
            mix = mixed[here, :] + skip * inputs[here, :]
            value, slope = gelu_and_slope(mix)
            kept[here, :] = slope.astype(BF16)
            hidden[b, n] = value.astype(BF16)
        here = pl.ds(place(order, seqs, b, 0) * chans, seqs * chans)
        stored.append(copying(hidden.at[b], far_hidden.at[b], out_sems.at[0, b]))
        stored.append(copying(kept.at[here], far_kept.at[here], out_sems.at[1, b]))
    wait_all(stored)


def glu_kernel(plan, lengths, arrived, tokens, cotangent, *refs):
    layers = plan.layers
    pieces, (block_out, leaving, outers, w) = refs[: 2 * layers], refs[2 * layers :]
    seqs, rows, width = tokens.shape
    blocks, _, chans, _ = arrived.shape
    own = width // plan.shards
    shard = lax.axis_index("shard")
    layer, core = shard // 2, lax.rem(shard, 2)
    bias = jnp.zeros((1, 2 * width), F32)
    for side in range(2):
        for turn in range(layers):
            piece = pieces[side * layers + turn]
            home = 2 * lax.rem(layer + layers - turn, layers) + lax.rem(core + side, 2)
            w[pl.ds(pl.multiple_of(home * own, own), own), :] = piece[0:own]
            bias += piece[own : own + 1].astype(F32)
    position = lax.broadcasted_iota(jnp.int32, (rows, width), 0)
    for n in range(seqs):
        hidden = arrived[:, n].reshape(width, LANES).astype(F32).T.astype(BF16)
        proj = dot(hidden, w[...], (1, 0)) + bias
        r, q = proj[0:rows, :width], proj[0:rows, width:]
        valid = jnp.where(position < valid_count(lengths, n, rows), 1.0, 0.0)
        open_ = jax.nn.sigmoid(q)
        e = valid * cotangent[n].astype(F32)
        first = e * open_
        both = jnp.concatenate([first, first * r * (1.0 - open_)], axis=1).astype(BF16)
        both = jnp.concatenate([both, jnp.zeros((LANES - rows, 2 * width), BF16)], axis=0)
        back = dot(both, w[...], (1, 1))
        leaving[:, n] = back.T.astype(BF16).reshape(blocks, chans, LANES)
        outers[pl.ds(n * LANES, LANES), :] = both
        block_out[n] = (tokens[n].astype(F32) + valid * (r * open_)).astype(BF16)


def outer_kernel(plan, arrived, outers, kept, sent):
    blocks, seqs, chans, _ = arrived.shape
    layers, subs = plan.layers, plan.subs
    own = chans * subs
    wide = outers.shape[1]
    core = lax.rem(lax.axis_index("shard"), 2)
    outer = outers[...]
    bias = jnp.sum(outer.astype(F32), axis=0, keepdims=True)
    tail = jnp.broadcast_to(bias, (kept.shape[1] - own, wide)).astype(BF16)
    for side, out in enumerate((sent, kept)):
        which = lax.rem(core + 1 - side, 2)
        left = jnp.concatenate(
            [
                jnp.concatenate([arrived[(2 * z + which) * subs + sub, n] for n in range(seqs)], axis=1)
                for z in range(layers)
                for sub in range(subs)
            ],
            axis=0,
        )
        out[:, 0:own] = dot(left, outer, (1, 0)).astype(BF16).reshape(layers, own, wide)
        for z in range(layers):
            out[z, own:] = tail


def backward_kernel(
    chunks, rows, order, arrived, first, pack, far_table, far_lines, far_slope,
    far_leaving, far_kept, tallies,
    grads, local, cross, slope, kept, leaving, table, lines, sems, more_sems,
):
    size = min(GROUPS[1], far_table.shape[0])
    blocks, seqs, chans, _ = arrived.shape
    total = blocks * seqs
    each = 2 * seqs
    lane = lax.broadcasted_iota(jnp.int32, (1, LANES), 1).astype(F32)
    skip, gain = pack[:, 256:257], pack[:, 257:258]
    mirror = mirror_matrix(rows)
    upper = upper_half(rows)
    spans = [pl.ds(place(order, seqs, b, 0) * chans, seqs * chans) for b in range(blocks)]
    fetched = [
        copying(far_slope.at[span], slope.at[span], more_sems.at[0, b]) for b, span in enumerate(spans)
    ]
    fetch_tables(size, far_table, table, far_lines, lines, sems)
    stored = []
    for b in range(blocks):
        fetched[b].wait()
        for n in range(seqs):
            here = pl.ds(place(order, seqs, b, n) * chans, chans)
            g = (arrived[b, n].astype(F32) * slope[here, :].astype(F32)).astype(BF16)
            grads[here, :] = g.astype(F32)

    def group(at, _):
        members = range(size)
        await_table(size, far_table, table, sems, at)
        which = [at * size + k for k in members]
        mine = [pl.ds(h, total, stride=chans) for h in which]
        line = [lines[h] for h in which]
        ends = [dot(grads[mine[k], :].astype(BF16), table[which[k]], (1, 0)) for k in members]
        for k in members:
            g = grads[mine[k], :].astype(BF16)
            kept[which[k]] = g
            local[mine[k], :] = dot(g, toeplitz(upper, line[k][0:1]), (1, 1))
        for k in members:
            parts = [jnp.zeros((each, LANES), F32)]
            state = ends[k][each * (chunks - 1) :]
            for c in range(chunks - 2, -1, -1):
                parts.append(state * line[k][3:4] + swap(state) * line[k][4:5])
                if c:
                    state = state * line[k][1:2] + swap(state) * line[k][2:3]
                    state += ends[k][each * c : each * (c + 1)]
            ends[k] = jnp.concatenate(parts[::-1], axis=0).astype(BF16)
        for k in members:
            cross[mine[k], :] = dot(ends[k], table[which[k]], (1, 1))
        return 0

    await_lines(size, far_lines, lines, sems)
    lax.fori_loop(0, chans // size, group, 0)
    stored.append(copying(kept, far_kept, more_sems.at[1, 0]))
    gains = shifts = jnp.zeros((chans, LANES), F32)
    for b in range(blocks):
        for n in range(seqs):
            here = pl.ds(place(order, seqs, b, n) * chans, chans)
            grad = local[here, :] + skip * grads[here, :]
            grad += dot(cross[here, :].astype(BF16), mirror, (1, 0))
            xhat = first[b, n].astype(F32)
            m = jnp.where(lane < xhat[0:1, LANES - 1 :], grad, 0.0)
            gains += m * xhat
            shifts += m
            leaving[b, n] = (gain * m).astype(BF16)
        stored.append(copying(leaving.at[b], far_leaving.at[b], more_sems.at[2, b]))
    tallies[0] = gains
    tallies[1] = shifts
    wait_all(stored)


def prefix_kernel(
    chunks, rows, order, first, pack, far_table, far_lines, far_mirrored, far_prefix,
    mirrored, kept, prefix, table, lines, sems, out_sems,
):
    size = min(GROUPS[2], far_table.shape[0])
    fetch_tables(size, far_table, table, far_lines, lines, sems)
    blocks, seqs, chans, _ = first.shape
    total = blocks * seqs
    each = 2 * seqs
    lane = lax.broadcasted_iota(jnp.int32, (1, LANES), 1).astype(F32)
    gain, shift = pack[:, 257:258], pack[:, 258:259]
    mirror = mirror_matrix(rows)
    for b in range(blocks):
        for n in range(seqs):
            here = pl.ds(place(order, seqs, b, n) * chans, chans)
            xhat = first[b, n].astype(F32)
            x = jnp.where(lane < xhat[0:1, LANES - 1 :], xhat * gain + shift, 0.0).astype(BF16)
            mirrored[here, :] = dot(x, mirror, (1, 0))

    def group(at, _):
        members = range(size)
        await_table(size, far_table, table, sems, at)
        which = [at * size + k for k in members]
        line = [lines[h] for h in which]
        ends = []
        for k in members:
            x_back = mirrored[pl.ds(which[k], total, stride=chans), :]
            kept[which[k]] = x_back.astype(BF16)
            stack = jnp.concatenate([x_back, x_back * lane], axis=0).astype(BF16)
            ends.append(dot(stack, table[which[k]], (1, 0)))
        for k in members:

            def onward(state):
                return state * line[k][1:2] + swap(state) * line[k][2:3]

            state, slope = ends[k][0:each], ends[k][total : total + each]
            states, slopes = [state], [state + slope]
            for c in range(1, chunks - 1):
                slope = onward(slope + float(rows) * state) + ends[k][total + each * c : total + each * (c + 1)]
                state = onward(state) + ends[k][each * c : each * (c + 1)]
                states.append(state)
                slopes.append(state + slope)
            prefix[which[k]] = jnp.concatenate(states + slopes, axis=0).astype(BF16)
        return 0

    await_lines(size, far_lines, lines, sems)
    lax.fori_loop(0, chans // size, group, 0)
    wait_all([copying(kept, far_mirrored, out_sems.at[0]), copying(prefix, far_prefix, out_sems.at[1])])


def moment_kernel(
    chunks, rows, far_table, far_mirrored, far_prefix, far_grads, firsts, tallies, sums,
    cross_one_a, cross_one_b, cross_two_a, cross_two_b, local_one, local_two, corrs,
    table, mirrored, prefix, grads, sems,
):
    size = min(GROUPS[3], far_table.shape[0])
    chans, total, _ = far_grads.shape
    each = total // chunks
    count = chans // size
    pairs = (
        (far_grads, grads), (far_table, table), (far_mirrored, mirrored), (far_prefix, prefix)
    )
    for at in range(count):
        here = pl.ds(at * size, size)
        for k, (far, near) in enumerate(pairs):
            copying(far.at[here], near.at[here], sems.at[k, at])
    lane = lax.broadcasted_iota(jnp.int32, (1, LANES), 1).astype(F32)
    square = (rows, LANES)
    behind = lax.broadcasted_iota(jnp.int32, square, 1) <= (
        LANES - rows + lax.broadcasted_iota(jnp.int32, square, 0)
    )

    def group(at, _):
        members = range(size)
        which = [at * size + k for k in members]
        here = pl.ds(at * size, size)
        for k, (far, near) in enumerate(pairs):
            pltpu.make_async_copy(far.at[here], near.at[here], sems.at[k, at]).wait()
        ends, outer, both = [], [], []
        for k in members:
            g = grads[which[k]]
            stack = jnp.concatenate([g, (g.astype(F32) * lane).astype(BF16)], axis=0)
            ends.append(dot(stack, table[which[k]], (1, 0)))
        for k in members:
            outer.append(dot(mirrored[which[k]], grads[which[k]], (0, 0)))
        for k in members:
            one = pl.ds(which[k], 1)
            later, later_slope = ends[k][each:total], ends[k][total + each :]
            before = prefix[which[k]].astype(F32)
            state, slope = before[0 : total - each], before[total - each :]
            swapped, swapped_slope = swap(later), swap(later_slope)
            for into, value in (
                (cross_one_a, state * later),
                (cross_one_b, state * swapped),
                (cross_two_a, slope * later + state * later_slope),
                (cross_two_b, slope * swapped + state * swapped_slope),
            ):
                into[one, :] = jnp.sum(value, axis=0, keepdims=True)
            slid = pltpu.roll(outer[k][0:rows], LANES - rows + 1, 1, stride=1, stride_axis=0)
            corr = jnp.sum(jnp.where(behind, slid, 0.0), axis=0, keepdims=True)
            corrs[one, :] = corr
            pair = jnp.concatenate([corr, corr * lane, jnp.zeros((6, LANES), F32)], axis=0)
            both.append(pair.astype(BF16))
        for k in members:
            turned = dot(both[k], table[which[k]], (1, 0))
            local_one[pl.ds(which[k], 1), :] = turned[0:1]
            local_two[pl.ds(which[k], 1), :] = turned[1:2]
        return 0

    lax.fori_loop(0, count, group, 0)
    low = lax.broadcasted_iota(jnp.int32, (1, LANES), 1) < LANES // 2
    for k, (a, b, near) in enumerate(
        ((cross_one_a, cross_one_b, local_one), (cross_two_a, cross_two_b, local_two))
    ):
        far = jnp.where(low, a[...] - swap(a[...]), b[...] + swap(b[...]))
        moment = far * firsts[0] + swap(far) * firsts[1] + near[...]
        sums[0:chans, k * LANES : (k + 1) * LANES] = moment.astype(BF16)
    diagonal = lax.broadcasted_iota(jnp.int32, (chans, 2 * LANES), 0) == lax.broadcasted_iota(
        jnp.int32, (chans, 2 * LANES), 1
    )
    row = lax.broadcasted_iota(jnp.int32, (16, 2 * LANES), 0)
    tail = jnp.zeros((16, 2 * LANES), F32)
    columns = [corrs[:, 0:1]] + [jnp.sum(tallies[k], axis=1, keepdims=True) for k in range(2)]
    for k, column in enumerate(columns):
        line = jnp.sum(jnp.where(diagonal, column, 0.0), axis=0, keepdims=True)
        tail = jnp.where(row == k, line, tail)
    sums[chans:, :] = tail.astype(BF16)


def share_kernel(layers, kept, came, *outs):
    layer = lax.axis_index("shard") // 2
    for turn, out in enumerate(outs):
        at = lax.rem(layer + turn, layers)
        out[...] = (kept[at].astype(F32) + came[at].astype(F32)).astype(BF16)


def add_kernel(*refs):
    total = refs[0][...].astype(F32)
    for ref in refs[1:-1]:
        total += ref[...].astype(F32)
    refs[-1][...] = total.astype(BF16)


def ordered(parts, slots):
    count = len(parts)
    mine = lax.axis_index("ctx")
    for turn, part in enumerate(parts):
        slots[lax.rem(mine + count - turn, count)] = part[...]


def owner_kernel(chunks, subs, *refs):
    parts, inputs, outs = refs[:chunks], refs[chunks : chunks + 6], refs[chunks + 6 :]
    one, two, decay, scale_in, real, imag = inputs
    grad_weight, grad_bias, grad_decay, grad_freq, grad_real, grad_imag, *vectors, slots = outs
    own, states = decay.shape
    grad_weight[...] = one[0:own].astype(F32) + two[0:own].astype(F32)
    line = one[own : own + 1].astype(F32) + two[own : own + 1].astype(F32)
    segment = grad_bias.shape[1]
    shard = lax.axis_index("shard")
    row = jnp.zeros((1, segment), F32)
    for s in range(line.shape[1] // segment):
        row = jnp.where(shard == s, line[:, s * segment : (s + 1) * segment], row)
    grad_bias[...] = row
    ordered(parts, slots)
    chans = own // subs
    sums = []
    for sub in range(subs):
        total = slots[sub].astype(F32)
        for k in range(sub + subs, chunks, subs):
            total += slots[k].astype(F32)
        sums.append(total)
    moments = jnp.concatenate([t[0:chans] for t in sums], axis=0)
    one_re, one_im, two_re, two_im = (moments[:, k * states : (k + 1) * states] for k in range(4))
    scale = scale_in[...]
    hat_re, hat_im = scale * real[...], scale * imag[...]
    grad_decay[...] = -(hat_re * two_re - hat_im * two_im) + jnp.exp(-2.0 * decay[...]) / scale * (
        real[...] * one_re - imag[...] * one_im
    )
    grad_freq[...] = -(hat_re * two_im + hat_im * two_re)
    grad_real[...] = scale * one_re
    grad_imag[...] = -scale * one_im
    for k, vector in enumerate(vectors):
        lines = [t[chans + k : chans + k + 1, 0:chans] for t in sums]
        vector[...] = jnp.concatenate(lines, axis=1) if subs > 1 else lines[0]


def final_kernel(arrived, tokens, cotangent, out):
    seqs, rows, width = tokens.shape
    for n in range(seqs):
        d = arrived[:, n].reshape(width, LANES).astype(F32).T[0:rows]
        xhat, inv = row_stats(tokens[n].astype(F32))
        mean = jnp.mean(d, axis=-1, keepdims=True)
        along = jnp.mean(d * xhat, axis=-1, keepdims=True)
        grad = (d - mean - xhat * along) * inv
        out[n] = (cotangent[n].astype(F32) + grad).astype(BF16)


def call(kernel, micros, outs, ins, scratch=()):
    return pl.pallas_call(
        kernel,
        out_shape=[(pltpu.HBM if len(o) > 2 else jax.ShapeDtypeStruct)(*o[:2]) for o in outs],
        in_specs=ins,
        out_specs=[HBM if len(o) > 2 else VMEM for o in outs],
        scratch_shapes=list(scratch),
        compiler_params=PARAMS,
        cost_estimate=pl.CostEstimate(
            flops=int(micros * 1e9), bytes_accessed=int(micros * 3.5e6), transcendentals=0
        ),
    )


def in_hbm(*arrays):
    return [pltpu.with_memory_space_constraint(a, pltpu.HBM) for a in arrays]


def per_device(
    plan, tokens, lengths, out_weight, out_bias, decay_rate, frequency, coef_real, coef_imag,
    skip, gain, shift, cotangent,
):
    seqs, rows, width = tokens.shape
    chunks, subs = plan.chunks, plan.subs
    blocks = 2 * chunks
    chans = width // blocks
    own, states = decay_rate.shape
    total = blocks * seqs
    mine, shard = lax.axis_index("ctx"), lax.axis_index("shard")
    layer = shard // 2

    def exchange(buffer):
        return lax.all_to_all(buffer, BOTH, 0, 0, axis_index_groups=plan.groups, tiled=True)

    segment = out_bias.shape[0]
    pack, scale, piece = call(
        pack_kernel,
        2,
        [((own, 3 * LANES), F32), ((own, states), F32), ((own + 16, 2 * width), BF16)],
        [VMEM] * 9,
    )(
        *in_hbm(
            decay_rate, frequency, coef_real, coef_imag,
            skip[None], gain[None], shift[None], out_weight, out_bias[None],
        )
    )
    if subs > 1:
        pack = lax.dynamic_slice_in_dim(pack, lax.rem(mine, subs) * chans, chans, 0)
    pack = lax.ppermute(pack, BOTH, plan.fetch)

    def here(shape, dtype=BF16):
        return pltpu.VMEM(shape, dtype)

    def sems(*shape):
        return pltpu.SemaphoreType.DMA(shape)

    wire = ((blocks, seqs, chans, LANES), BF16, 1)
    flow, like_tokens = wire[:2], (tokens.shape, BF16)
    on_wire, on_rows = here(wire[0]), here(tokens.shape)
    (first,) = call(
        norm_kernel, COST[0], [flow], [SMEM, VMEM]
    )(lengths, *in_hbm(tokens))
    first = exchange(first)
    piece, pack = lax.optimization_barrier((piece, pack))
    near = [piece] + [lax.ppermute(piece, "shard", route) for route in plan.climb]
    table_type, line_type = ((chans, LANES, LANES), BF16, 1), ((chans, 8, LANES), F32, 1)
    tables = [here(*table_type[:2]), here(*line_type[:2])]
    table, lines, firsts = call(
        functools.partial(table_kernel, rows),
        COST[1],
        [table_type, line_type, ((2, chans, LANES), F32)],
        [VMEM],
        tables + [sems(chans // 8 + 1)],
    )(pack)
    far_tables = in_hbm(table, lines)
    buffer, line = here((total * chans, LANES), F32), here((chans, LANES), F32)
    low = ((total * chans, LANES), BF16, 1)
    low_buffer = here(*low[:2])
    tables.append(sems(chans // 8 + 1))
    hidden, slope = call(
        functools.partial(forward_kernel, chunks, rows, plan.order),
        COST[2],
        [wire, low],
        [VMEM, VMEM, HBM, HBM],
        [buffer, buffer, buffer, on_wire, low_buffer] + tables + [sems(2, blocks)],
    )(first, pack, *far_tables)
    prefix_type = ((chans, 2 * (total - 2 * seqs), LANES), BF16, 1)
    by_channel = ((chans, total, LANES), BF16, 1)
    mirrored, prefix = call(
        functools.partial(prefix_kernel, chunks, rows, plan.order),
        6,
        [by_channel, prefix_type],
        [VMEM, VMEM, HBM, HBM],
        [buffer, here(*by_channel[:2]), here(*prefix_type[:2])] + tables + [sems(2)],
    )(first, pack, *far_tables)
    hidden, near = lax.optimization_barrier((hidden, near))
    across = [lax.ppermute(p, "shard", plan.across) for p in near]
    hidden = exchange(hidden)
    block_out, back, outers = call(
        functools.partial(glu_kernel, plan),
        COST[3],
        [like_tokens, flow, ((seqs * LANES, 2 * width), BF16)],
        [SMEM] + [VMEM] * (3 + 2 * plan.layers),
        [here((width, 2 * width))],
    )(lengths, hidden, *in_hbm(tokens, cotangent), *near, *across)
    back = exchange(back)
    half = ((plan.layers, own + 16, 2 * width), BF16)
    kept, sent = call(functools.partial(outer_kernel, plan), 2, [half, half], [VMEM] * 2)(
        hidden, outers
    )

    came = lax.ppermute(sent, "shard", plan.across)
    slab = ((own + 16, 2 * width), BF16)
    shares = call(
        functools.partial(share_kernel, plan.layers), COST[6], [slab] * plan.layers, [VMEM] * 2
    )(kept, came)
    climbed = [lax.ppermute(v, "shard", route) for v, route in zip(shares[1:], plan.climb)]
    leaving, local_grads, tallies = call(
        functools.partial(backward_kernel, chunks, rows, plan.order),
        COST[4],
        [wire, by_channel, ((2, chans, LANES), F32)],
        [VMEM, VMEM, VMEM, HBM, HBM, HBM],
        [buffer, buffer, buffer, low_buffer, here(*by_channel[:2]), on_wire]
        + tables
        + [sems(3, blocks)],
    )(back, first, pack, *far_tables, *in_hbm(slope))
    (owned,) = call(add_kernel, 1, [slab], [VMEM] * plan.layers)(shares[0], *climbed)
    first_sum = owned
    for route in plan.fold[:-1]:
        (owned,) = call(add_kernel, 1, [slab], [VMEM] * 2)(owned, lax.ppermute(owned, "ctx", route))
    folded = lax.ppermute(owned, "ctx", plan.fold[-1])
    tallies, first_sum = lax.optimization_barrier((tallies, first_sum))
    state = (chans + 16, 2 * LANES)
    (sums,) = call(
        functools.partial(moment_kernel, chunks, rows),
        COST[7],
        [(state, BF16)],
        [HBM] * 4 + [VMEM] * 2,
        [line] * 7
        + [tables[0], here(*by_channel[:2]), here(*prefix_type[:2]), here(*by_channel[:2])]
        + [sems(4, chans // 8)],
    )(far_tables[0], *in_hbm(mirrored, prefix, local_grads), firsts, tallies)
    leaving = exchange(leaving)
    (tokens_grad,) = call(
        final_kernel,
        COST[5],
        [like_tokens],
        [VMEM] * 3,
    )(
        leaving, *in_hbm(tokens, cotangent)
    )

    parts = [lax.ppermute(sums, BOTH, route) for route in plan.give]
    tokens_grad, parts = lax.optimization_barrier((tokens_grad, parts))
    matrix, vector = ((own, states), F32), ((1, own), F32)
    grad_weight, grad_bias, *grads = call(
        functools.partial(owner_kernel, chunks, subs),
        2,
        [(out_weight.shape, F32), ((1, segment), F32)] + [matrix] * 4 + [vector] * 3,
        [VMEM] * (chunks + 6),
        [here((chunks,) + state)],
    )(*parts, owned, folded, *in_hbm(decay_rate, scale, coef_real, coef_imag))
    return (
        block_out,
        tokens_grad,
        grad_weight,
        grad_bias[0],
        *grads[:4],
        *(v[0] for v in grads[4:]),
    )


def solution(mesh):
    plan = Plan(mesh.shape["shard"], mesh.shape["ctx"])
    rows = P("shard", "ctx", None)
    matrix = P("shard", None)
    vector = P("shard")
    in_specs = (rows, vector, matrix, vector) + (matrix,) * 4 + (vector,) * 3 + (rows,)
    out_specs = (rows, rows, matrix, vector) + (matrix,) * 4 + (vector,) * 3
    return jax.shard_map(
        functools.partial(per_device, plan),
        mesh=mesh,
        in_specs=in_specs,
        out_specs=out_specs,
        check_vma=False,
    )
```

```python
import functools
import math

import jax
import jax.numpy as jnp
from jax import lax
from jax.experimental import pallas as pl
from jax.experimental.pallas import tpu as pltpu
from jax.sharding import PartitionSpec as P

EPSILON = 1e-05
LANES = 128
GROUPS = (32, 32, 16, 16)
COST = (2, 8, 10, 6, 1, 3, 2, 8)
BOTH = ("shard", "ctx")
F32 = jnp.float32
BF16 = jnp.bfloat16
VMEM = pl.BlockSpec(memory_space=pltpu.VMEM)
SMEM = pl.BlockSpec(memory_space=pltpu.SMEM)
HBM = pl.BlockSpec(memory_space=pltpu.HBM)
PARAMS = pltpu.CompilerParams(vmem_limit_bytes=20 * 1024 * 1024)


class Plan:
    def __init__(self, shards, chunks):
        layers = shards // 2
        self.shards, self.chunks = shards, chunks
        self.subs = subs = chunks // layers
        self.order = [
            (core, top * subs + sub)
            for top in range(chunks // subs)
            for core in range(2)
            for sub in range(subs)
        ]
        self.groups = [
            [(2 * z + core) * chunks + c for core, c in self.order] for z in range(layers)
        ]
        members = [(z, core, c) for z in range(layers) for core, c in self.order]

        def here(z, core, c):
            return (2 * z + core) * chunks + c

        def owner(z, core, c, turn):
            place = (z * subs + c % subs + turn) % chunks
            return (2 * (c // subs) + core) * chunks + place

        self.fetch = [(owner(*m, 0), here(*m)) for m in members]
        self.give = [[(here(*m), owner(*m, turn)) for m in members] for turn in range(0, chunks, 2)]
        self.rotate = [
            [(a, (a + turn) % chunks) for a in range(chunks)] for turn in range(1, chunks)
        ]
        self.beside = [(a, a ^ 1) for a in range(chunks)]
        self.layers = layers
        self.climb = [
            [(s, (s + 2 * turn) % shards) for s in range(shards)] for turn in range(1, layers)
        ]
        self.across = [(s, s ^ 1) for s in range(shards)]


def row_stats(rows):
    mean = jnp.mean(rows, axis=-1, keepdims=True)
    centered = rows - mean
    var = jnp.mean(centered * centered, axis=-1, keepdims=True)
    inv = lax.rsqrt(var + EPSILON)
    return centered * inv, inv


def dot(a, b, over):
    return lax.dot_general(a, b, (((over[0],), (over[1],)), ((), ())), preferred_element_type=F32)


def pack_kernel(decay, freq, real, imag, skip, gain, shift, weight, bias, pack, scales, piece):
    own, states = decay.shape
    wide = weight.shape[1]
    rate = decay[...]
    square = rate * rate
    scale = jnp.sqrt(2.0 * rate * jnp.exp(-rate) * (1.0 + square / 6.0 * (1.0 + square / 20.0)))
    scales[...] = scale
    pack[:, 0:LANES] = jnp.concatenate([rate, freq[...]], axis=1)
    pack[:, LANES : 2 * LANES] = jnp.concatenate([scale * real[...], scale * imag[...]], axis=1)
    lane = lax.broadcasted_iota(jnp.int32, (own, LANES), 1)
    diagonal = lax.broadcasted_iota(jnp.int32, (own, own), 0) == lax.broadcasted_iota(jnp.int32, (own, own), 1)
    tail = jnp.zeros((own, LANES), F32)
    for k, vector in enumerate((skip, gain, shift)):
        column = jnp.sum(jnp.where(diagonal, vector[...], 0.0), axis=1, keepdims=True)
        tail = jnp.where(lane == k, column, tail)
    pack[:, 2 * LANES :] = tail
    piece[0:own] = weight[...].astype(BF16)
    segment = lax.broadcasted_iota(jnp.int32, (1, wide), 1) // bias.shape[1]
    repeated = jnp.concatenate([bias[...]] * (wide // bias.shape[1]), axis=1)
    row = jnp.where(segment == lax.axis_index("shard"), repeated, 0.0)
    piece[own:] = jnp.broadcast_to(row, (piece.shape[0] - own, wide)).astype(BF16)


def copying(source, target, sem):
    copy = pltpu.make_async_copy(source, target, sem)
    copy.start()
    return copy


def wait_all(copies):
    for copy in copies:
        copy.wait()


def valid_count(lengths, n, rows):
    return jnp.clip(lengths[n] - lax.axis_index("ctx") * rows, 0, rows)


def norm_kernel(tokens, out):
    seqs, rows, width = tokens.shape
    xhat, _ = row_stats(tokens[...].reshape(seqs * rows, width).astype(F32))
    out[...] = xhat.T.astype(BF16).reshape(out.shape)


def split_lanes(wide, rows, count):
    lane = lax.broadcasted_iota(jnp.int32, (1, LANES), 1)
    pieces = []
    for n in range(count):
        at, off = divmod(n * rows, LANES)
        turn = (LANES - off) % LANES
        piece = wide[:, at * LANES : (at + 1) * LANES]
        if turn:
            piece = pltpu.roll(piece, turn, 1)
        if off + rows > LANES:
            after = pltpu.roll(wide[:, (at + 1) * LANES : (at + 2) * LANES], turn, 1)
            piece = jnp.where(lane < turn, piece, after)
        pieces.append(piece)
    return pieces


def join_lanes(pieces, rows):
    lane = lax.broadcasted_iota(jnp.int32, (1, LANES), 1)
    columns = [None] * (len(pieces) * rows // LANES)
    for n, piece in enumerate(pieces):
        at, off = divmod(n * rows, LANES)
        turned = pltpu.roll(piece, off, 1) if off else piece
        columns[at] = turned if off == 0 else jnp.where(lane < off, columns[at], turned)
        if off + rows > LANES:
            columns[at + 1] = turned
    return jnp.concatenate(columns, axis=1)


def count_of(lengths, partner, order, block, n, rows):
    core, c = order[block]
    own = lax.rem(lax.axis_index("shard"), 2) == core
    return jnp.clip(jnp.where(own, lengths[n], partner[n]) - c * rows, 0, rows)


def swap(values):
    return pltpu.roll(values, LANES // 2, values.ndim - 1)


def table_kernel(rows, pack, far_table, far_lines, firsts, table, lines, sems):
    chans = pack.shape[0]
    low2 = lax.broadcasted_iota(jnp.int32, (1, LANES), 1) < LANES // 2
    low3 = low2[None]
    angle = jnp.where(low2, 0.0, math.pi / 2)
    step = 8
    offsets = lax.broadcasted_iota(jnp.int32, (1, step, 1), 1).astype(F32)

    def spread(pair):
        other = swap(pair)
        return jnp.where(low2, pair, other), jnp.where(low2, other, pair)

    def factors(power):
        other = swap(power)
        return jnp.where(low2, power, other), jnp.where(low2, -other, power)

    def block(at, _):
        here = pl.ds(pl.multiple_of(at * step, step), step)
        decay, freq = spread(pack[here, 0:LANES])
        real, imag = spread(pack[here, LANES : 2 * LANES])

        def power(by):
            return jnp.exp(-decay * by) * jnp.cos(freq * by - angle)

        part = jnp.exp(-decay[:, None, :] * offsets) * jnp.cos(freq[:, None, :] * offsets - angle[None])
        table[here, 0:step] = part.astype(BF16)
        size = step
        while size < LANES:
            same, cross = factors(power(float(size)))
            new = part * same[:, None, :] + swap(part) * cross[:, None, :]
            table[here, size : 2 * size] = new.astype(BF16)
            part = jnp.concatenate([part, new], axis=1)
            size *= 2
        copying(table.at[here], far_table.at[here], sems.at[at])
        real = jnp.where(low2, real, -real)
        whole = part.astype(BF16)
        hat = jnp.where(low2, real, -imag).astype(BF16)
        for k in range(step):
            row = jnp.broadcast_to(hat[k : k + 1], (step, LANES))
            lines[at * step + k, 0:1] = dot(row, whole[k], (1, 1))[0:1]
        one = power(1.0)
        same, cross = factors(one)
        firsts[0, here] = same
        firsts[1, here] = cross
        chunk_same, chunk_cross = factors(power(float(rows)))
        hat_re = jnp.where(low2, real, -real)
        turn_re = hat_re * same - imag * jnp.where(low2, -cross, cross)
        turn_im = hat_re * jnp.where(low2, -cross, cross) + imag * same
        for k, line in enumerate((chunk_same, chunk_cross, jnp.where(low2, turn_re, -turn_re), -turn_im)):
            lines[here, k + 1 : k + 2] = line[:, None, :]
        return 0

    count = chans // step
    lax.fori_loop(0, count, block, 0, unroll=min(4, count))
    for at in range(count):
        here = pl.ds(at * step, step)
        pltpu.make_async_copy(table.at[here], far_table.at[here], sems.at[at]).wait()
    copying(lines, far_lines, sems.at[count]).wait()


def paired(lefts, rights, over):
    outs = []
    for k in range(0, len(lefts), 2):
        rows = lefts[k].shape[0]
        left = jnp.concatenate(lefts[k : k + 2], axis=0)
        right = jnp.concatenate(rights[k : k + 2], axis=1 - over[1])
        both = dot(left, right, over)
        outs += [both[0:rows, 0:LANES], both[rows:, LANES:]]
    return outs


def upper_half(rows):
    square = (rows, LANES)
    return lax.broadcasted_iota(jnp.int32, square, 1) >= lax.broadcasted_iota(jnp.int32, square, 0)


def toeplitz(upper, taps):
    slid = pltpu.roll(jnp.broadcast_to(taps, upper.shape), 0, 1, stride=1, stride_axis=0)
    body = jnp.where(upper, slid, 0.0).astype(BF16)
    return jnp.concatenate([body, jnp.zeros((LANES - upper.shape[0], LANES), BF16)], axis=0)


def mirror_matrix(rows):
    square = (LANES, LANES)
    reach = lax.broadcasted_iota(jnp.int32, square, 0) + lax.broadcasted_iota(jnp.int32, square, 1)
    return jnp.where(reach == rows - 1, 1.0, 0.0).astype(BF16)


def place(order, seqs, block, n):
    core, c = order[block]
    return (c * 2 + core) * seqs + n


def fetch_tables(size, far_table, table, far_lines, lines, sems):
    count = table.shape[0] // size
    copying(far_lines, lines, sems.at[count])
    for at in range(count):
        here = pl.ds(at * size, size)
        copying(far_table.at[here], table.at[here], sems.at[at])


def await_table(size, far_table, table, sems, at):
    here = pl.ds(at * size, size)
    pltpu.make_async_copy(far_table.at[here], table.at[here], sems.at[at]).wait()


def await_lines(size, far_lines, lines, sems):
    pltpu.make_async_copy(far_lines, lines, sems.at[lines.shape[0] // size]).wait()


def gelu_and_slope(x):
    c = math.sqrt(2.0 / math.pi)
    square = x * x
    t = jnp.tanh(c * x * (1.0 + 0.044715 * square))
    half = 0.5 * (1.0 + t)
    return x * half, half + 0.5 * x * (1.0 - t * t) * (c + 3.0 * 0.044715 * c * square)


def forward_kernel(
    chunks, rows, order, lengths, partner, arrived, pack, far_table, far_lines, far_hidden, far_kept,
    inputs, mirrored, mixed, hidden, kept, table, lines, sems, out_sems,
):
    size = min(GROUPS[0], far_table.shape[0])
    fetch_tables(size, far_table, table, far_lines, lines, sems)
    blocks, chans, wide = arrived.shape
    seqs = wide // rows
    total = blocks * seqs
    each = 2 * seqs
    lane = lax.broadcasted_iota(jnp.int32, (1, LANES), 1)
    gain, shift = pack[:, 257:258], pack[:, 258:259]
    mirror = mirror_matrix(rows)
    upper = upper_half(rows)
    for b in range(blocks):
        for n, xhat in enumerate(split_lanes(arrived[b].astype(F32), rows, seqs)):
            here = pl.ds(place(order, seqs, b, n) * chans, chans)
            inside = lane < count_of(lengths, partner, order, b, n, rows)
            x = jnp.where(inside, xhat * gain + shift, 0.0).astype(BF16)
            inputs[here, :] = x.astype(F32)
            mirrored[here, :] = dot(x, mirror, (1, 0))

    def group(at, _):
        members = range(size)
        await_table(size, far_table, table, sems, at)
        mine = [pl.ds(at * size + k, total, stride=chans) for k in members]
        line = [lines[at * size + k] for k in members]
        powers = [table[at * size + k] for k in members]
        ends = paired([mirrored[mine[k], :].astype(BF16) for k in members], powers, (1, 0))
        local = paired(
            [inputs[mine[k], :].astype(BF16) for k in members],
            [toeplitz(upper, line[k][0:1]) for k in members],
            (1, 0),
        )
        for k in members:
            state = ends[k][0:each]
            carried = [jnp.zeros((each, LANES), F32)]
            for c in range(1, chunks):
                carried.append(state * line[k][3:4] + swap(state) * line[k][4:5])
                if c < chunks - 1:
                    state = state * line[k][1:2] + swap(state) * line[k][2:3]
                    state += ends[k][each * c : each * (c + 1)]
            ends[k] = jnp.concatenate(carried, axis=0).astype(BF16)
        far = paired(ends, [table[at * size + k] for k in members], (1, 1))
        for k in members:
            mixed[mine[k], :] = local[k] + far[k]
        return 0

    await_lines(size, far_lines, lines, sems)
    lax.fori_loop(0, chans // size, group, 0)
    stored = []
    skip = pack[:, 256:257]
    for b in range(blocks):
        values = []
        for n in range(seqs):
            here = pl.ds(place(order, seqs, b, n) * chans, chans)
            mix = mixed[here, :] + skip * inputs[here, :]
            value, slope = gelu_and_slope(mix)
            kept[here, :] = jnp.where(lane < rows, slope, 0.0).astype(BF16)
            values.append(value)
        hidden[b] = join_lanes(values, rows).astype(BF16)
        here = pl.ds(place(order, seqs, b, 0) * chans, seqs * chans)
        stored.append(copying(hidden.at[b], far_hidden.at[b], out_sems.at[0, b]))
        stored.append(copying(kept.at[here], far_kept.at[here], out_sems.at[1, b]))
    wait_all(stored)


def glu_kernel(plan, lengths, arrived, tokens, cotangent, *refs):
    layers = plan.layers
    pieces, (block_out, leaving, outers, w) = refs[: 2 * layers], refs[2 * layers :]
    seqs, rows, width = tokens.shape
    own = width // plan.shards
    shard = lax.axis_index("shard")
    layer, core = shard // 2, lax.rem(shard, 2)
    bias = jnp.zeros((1, 2 * width), F32)
    for side in range(2):
        for turn in range(layers):
            piece = pieces[side * layers + turn]
            home = 2 * lax.rem(layer + layers - turn, layers) + lax.rem(core + side, 2)
            w[pl.ds(pl.multiple_of(home * own, own), own), :] = piece[0:own]
            bias += piece[own : own + 1].astype(F32)
    position = lax.broadcasted_iota(jnp.int32, (rows, width), 0)
    hidden = arrived[...].reshape(width, seqs * rows).astype(F32).T.astype(BF16)
    for n in range(seqs):
        here = slice(n * rows, (n + 1) * rows)
        proj = dot(hidden[here], w[...], (1, 0)) + bias
        r, q = proj[:, :width], proj[:, width:]
        valid = jnp.where(position < valid_count(lengths, n, rows), 1.0, 0.0)
        open_ = jax.nn.sigmoid(q)
        e = valid * cotangent[n].astype(F32)
        first = e * open_
        outers[here, :] = jnp.concatenate([first, first * r * (1.0 - open_)], axis=1).astype(BF16)
        block_out[n] = (tokens[n].astype(F32) + valid * (r * open_)).astype(BF16)
    back = dot(outers[...], w[...], (1, 1))
    leaving[...] = back.T.astype(BF16).reshape(leaving.shape)


def outer_kernel(plan, arrived, outers, kept, sent):
    chans = arrived.shape[1]
    layers, subs = plan.layers, plan.subs
    own, wide = chans * subs, outers.shape[1]
    core = lax.rem(lax.axis_index("shard"), 2)
    outer = outers[...]
    bias = jnp.sum(outer.astype(F32), axis=0, keepdims=True)
    tail = jnp.broadcast_to(bias, (kept.shape[1] - own, wide)).astype(BF16)
    for side, out in enumerate((sent, kept)):
        which = lax.rem(core + 1 - side, 2)
        members = [(2 * z + which) * subs + sub for z in range(layers) for sub in range(subs)]
        left = jnp.concatenate([arrived[member] for member in members], axis=0)
        out[:, 0:own] = dot(left, outer, (1, 0)).astype(BF16).reshape(layers, own, wide)
        for z in range(layers):
            out[z, own:] = tail


def backward_kernel(
    chunks, rows, order, lengths, partner, arrived, first, pack, far_table, far_lines, far_slope,
    far_leaving, far_kept, tallies,
    grads, local, cross, slope, kept, leaving, table, lines, sems, more_sems,
):
    size = min(GROUPS[1], far_table.shape[0])
    blocks, chans, wide = arrived.shape
    seqs = wide // rows
    total = blocks * seqs
    each = 2 * seqs
    lane = lax.broadcasted_iota(jnp.int32, (1, LANES), 1)
    skip, gain = pack[:, 256:257], pack[:, 257:258]
    mirror = mirror_matrix(rows)
    upper = upper_half(rows)
    spans = [pl.ds(place(order, seqs, b, 0) * chans, seqs * chans) for b in range(blocks)]
    fetched = [
        copying(far_slope.at[span], slope.at[span], more_sems.at[0, b]) for b, span in enumerate(spans)
    ]
    fetch_tables(size, far_table, table, far_lines, lines, sems)
    stored = []
    for b in range(blocks):
        fetched[b].wait()
        for n, back in enumerate(split_lanes(arrived[b].astype(F32), rows, seqs)):
            here = pl.ds(place(order, seqs, b, n) * chans, chans)
            g = (back * slope[here, :].astype(F32)).astype(BF16)
            grads[here, :] = g.astype(F32)

    def group(at, _):
        members = range(size)
        await_table(size, far_table, table, sems, at)
        which = [at * size + k for k in members]
        mine = [pl.ds(h, total, stride=chans) for h in which]
        line = [lines[h] for h in which]
        powers = [table[h] for h in which]
        low = [grads[mine[k], :].astype(BF16) for k in members]
        ends = paired(low, powers, (1, 0))
        near = paired(low, [toeplitz(upper, line[k][0:1]) for k in members], (1, 1))
        for k in members:
            kept[which[k]] = low[k]
            local[mine[k], :] = near[k]
        for k in members:
            parts = [jnp.zeros((each, LANES), F32)]
            state = ends[k][each * (chunks - 1) :]
            for c in range(chunks - 2, -1, -1):
                parts.append(state * line[k][3:4] + swap(state) * line[k][4:5])
                if c:
                    state = state * line[k][1:2] + swap(state) * line[k][2:3]
                    state += ends[k][each * c : each * (c + 1)]
            ends[k] = jnp.concatenate(parts[::-1], axis=0).astype(BF16)
        far = paired(ends, powers, (1, 1))
        for k in members:
            cross[mine[k], :] = far[k]
        return 0

    await_lines(size, far_lines, lines, sems)
    lax.fori_loop(0, chans // size, group, 0)
    stored.append(copying(kept, far_kept, more_sems.at[1, 0]))
    gains = shifts = jnp.zeros((chans, LANES), F32)
    for b in range(blocks):
        inner = []
        for n, xhat in enumerate(split_lanes(first[b].astype(F32), rows, seqs)):
            here = pl.ds(place(order, seqs, b, n) * chans, chans)
            grad = local[here, :] + skip * grads[here, :]
            grad += dot(cross[here, :].astype(BF16), mirror, (1, 0))
            m = jnp.where(lane < count_of(lengths, partner, order, b, n, rows), grad, 0.0)
            gains += m * xhat
            shifts += m
            inner.append(gain * m)
        leaving[b] = join_lanes(inner, rows).astype(BF16)
        stored.append(copying(leaving.at[b], far_leaving.at[b], more_sems.at[2, b]))
    tallies[0] = gains
    tallies[1] = shifts
    wait_all(stored)


def prefix_kernel(
    chunks, rows, order, lengths, partner, first, pack, far_table, far_lines, far_mirrored, far_prefix,
    mirrored, kept, prefix, table, lines, sems, out_sems,
):
    size = min(GROUPS[2], far_table.shape[0])
    fetch_tables(size, far_table, table, far_lines, lines, sems)
    blocks, chans, wide = first.shape
    seqs = wide // rows
    total = blocks * seqs
    each = 2 * seqs
    lane = lax.broadcasted_iota(jnp.int32, (1, LANES), 1).astype(F32)
    gain, shift = pack[:, 257:258], pack[:, 258:259]
    mirror = mirror_matrix(rows)
    for b in range(blocks):
        for n, xhat in enumerate(split_lanes(first[b].astype(F32), rows, seqs)):
            here = pl.ds(place(order, seqs, b, n) * chans, chans)
            inside = lane < count_of(lengths, partner, order, b, n, rows).astype(F32)
            x = jnp.where(inside, xhat * gain + shift, 0.0).astype(BF16)
            mirrored[here, :] = dot(x, mirror, (1, 0))

    def group(at, _):
        members = range(size)
        await_table(size, far_table, table, sems, at)
        which = [at * size + k for k in members]
        line = [lines[h] for h in which]
        ends = []
        for k in members:
            x_back = mirrored[pl.ds(which[k], total, stride=chans), :]
            kept[which[k]] = x_back.astype(BF16)
            stack = jnp.concatenate([x_back, x_back * lane], axis=0).astype(BF16)
            ends.append(dot(stack, table[which[k]], (1, 0)))
        for k in members:

            def onward(state):
                return state * line[k][1:2] + swap(state) * line[k][2:3]

            state, slope = ends[k][0:each], ends[k][total : total + each]
            states, slopes = [state], [state + slope]
            for c in range(1, chunks - 1):
                slope = onward(slope + float(rows) * state) + ends[k][total + each * c : total + each * (c + 1)]
                state = onward(state) + ends[k][each * c : each * (c + 1)]
                states.append(state)
                slopes.append(state + slope)
            prefix[which[k]] = jnp.concatenate(states + slopes, axis=0).astype(BF16)
        return 0

    await_lines(size, far_lines, lines, sems)
    lax.fori_loop(0, chans // size, group, 0)
    wait_all([copying(kept, far_mirrored, out_sems.at[0]), copying(prefix, far_prefix, out_sems.at[1])])


def moment_kernel(
    chunks, rows, far_table, far_mirrored, far_prefix, far_grads, firsts, tallies, sums,
    cross_one_a, cross_one_b, cross_two_a, cross_two_b, local_one, local_two, corrs,
    table, mirrored, prefix, grads, sems,
):
    size = min(GROUPS[3], far_table.shape[0])
    chans, total, _ = far_grads.shape
    each = total // chunks
    count = chans // size
    pairs = (
        (far_grads, grads), (far_table, table), (far_mirrored, mirrored), (far_prefix, prefix)
    )
    for at in range(count):
        here = pl.ds(at * size, size)
        for k, (far, near) in enumerate(pairs):
            copying(far.at[here], near.at[here], sems.at[k, at])
    lane = lax.broadcasted_iota(jnp.int32, (1, LANES), 1).astype(F32)
    square = (rows, LANES)
    behind = lax.broadcasted_iota(jnp.int32, square, 1) <= (
        LANES - rows + lax.broadcasted_iota(jnp.int32, square, 0)
    )

    def group(at, _):
        members = range(size)
        which = [at * size + k for k in members]
        here = pl.ds(at * size, size)
        for k, (far, near) in enumerate(pairs):
            pltpu.make_async_copy(far.at[here], near.at[here], sems.at[k, at]).wait()
        ends, outer, both = [], [], []
        powers = [table[h] for h in which]
        for k in members:
            g = grads[which[k]]
            ends.append(jnp.concatenate([g, (g.astype(F32) * lane).astype(BF16)], axis=0))
        ends = paired(ends, powers, (1, 0))
        for k in members:
            outer.append(dot(mirrored[which[k]], grads[which[k]], (0, 0)))
        for k in members:
            one = pl.ds(which[k], 1)
            later, later_slope = ends[k][each:total], ends[k][total + each :]
            before = prefix[which[k]].astype(F32)
            state, slope = before[0 : total - each], before[total - each :]
            swapped, swapped_slope = swap(later), swap(later_slope)
            for into, value in (
                (cross_one_a, state * later),
                (cross_one_b, state * swapped),
                (cross_two_a, slope * later + state * later_slope),
                (cross_two_b, slope * swapped + state * swapped_slope),
            ):
                into[one, :] = jnp.sum(value, axis=0, keepdims=True)
            slid = pltpu.roll(outer[k][0:rows], LANES - rows + 1, 1, stride=1, stride_axis=0)
            corr = jnp.sum(jnp.where(behind, slid, 0.0), axis=0, keepdims=True)
            corrs[one, :] = corr
            pair = jnp.concatenate([corr, corr * lane, jnp.zeros((14, LANES), F32)], axis=0)
            both.append(pair)
        for k, turned in enumerate(paired([p.astype(BF16) for p in both], powers, (1, 0))):
            local_one[pl.ds(which[k], 1), :] = turned[0:1]
            local_two[pl.ds(which[k], 1), :] = turned[1:2]
        return 0

    lax.fori_loop(0, count, group, 0)
    low = lax.broadcasted_iota(jnp.int32, (1, LANES), 1) < LANES // 2
    for k, (a, b, near) in enumerate(
        ((cross_one_a, cross_one_b, local_one), (cross_two_a, cross_two_b, local_two))
    ):
        far = jnp.where(low, a[...] - swap(a[...]), b[...] + swap(b[...]))
        moment = far * firsts[0] + swap(far) * firsts[1] + near[...]
        sums[0:chans, k * LANES : (k + 1) * LANES] = moment.astype(BF16)
    diagonal = lax.broadcasted_iota(jnp.int32, (chans, 2 * LANES), 0) == lax.broadcasted_iota(
        jnp.int32, (chans, 2 * LANES), 1
    )
    row = lax.broadcasted_iota(jnp.int32, (16, 2 * LANES), 0)
    tail = jnp.zeros((16, 2 * LANES), F32)
    columns = [corrs[:, 0:1]] + [jnp.sum(tallies[k], axis=1, keepdims=True) for k in range(2)]
    for k, column in enumerate(columns):
        line = jnp.sum(jnp.where(diagonal, column, 0.0), axis=0, keepdims=True)
        tail = jnp.where(row == k, line, tail)
    sums[chans:, :] = tail.astype(BF16)


def share_kernel(layers, kept, came, *outs):
    layer = lax.axis_index("shard") // 2
    for turn, out in enumerate(outs):
        at = lax.rem(layer + turn, layers)
        out[...] = (kept[at].astype(F32) + came[at].astype(F32)).astype(BF16)


def add_kernel(*refs):
    total = refs[0][...].astype(F32)
    for ref in refs[1:-1]:
        total += ref[...].astype(F32)
    refs[-1][...] = total.astype(BF16)


def merge_kernel(subs, *refs):
    parts, (out, slots) = refs[:-2], refs[-2:]
    count = len(parts)
    mine = lax.axis_index("ctx")
    for turn, part in enumerate(parts):
        slots[lax.rem(mine // 2 + count - turn, count)] = part[...]
    total = slots[0].astype(F32)
    for k in range(1, count):
        total += slots[k].astype(F32)
    rows = total.shape[0]
    if subs == 1:
        out[...] = total.astype(BF16)
    else:
        out[...] = jnp.zeros(out.shape, BF16)
        out[pl.ds(pl.multiple_of(lax.rem(mine, subs) * rows, rows), rows), :] = total.astype(BF16)


def owner_kernel(chunks, subs, *refs):
    slabs, refs = refs[:chunks], refs[chunks:]
    one, two, decay, scale_in, real, imag = refs[:6]
    grad_weight, grad_bias, grad_decay, grad_freq, grad_real, grad_imag, *vectors, slots = refs[6:]
    own, states = decay.shape
    wide = grad_weight.shape[1]
    mine = lax.axis_index("ctx")
    for turn, slab in enumerate(slabs):
        slots[lax.rem(mine + chunks - turn, chunks)] = slab[...]
    slab = slots[0].astype(F32)
    for k in range(1, chunks):
        slab += slots[k].astype(F32)
    grad_weight[...] = slab[0:own]
    line = slab[own : own + 1]
    segment = grad_bias.shape[1]
    shard = lax.axis_index("shard")
    row = jnp.zeros((1, segment), F32)
    for s in range(wide // segment):
        row = jnp.where(shard == s, line[:, s * segment : (s + 1) * segment], row)
    grad_bias[...] = row
    chans = own // subs
    each = chans + 16
    total = one[...].astype(F32) + two[...].astype(F32)
    sums = [total[each * sub : each * (sub + 1)] for sub in range(subs)]
    moments = jnp.concatenate([t[0:chans] for t in sums], axis=0)
    one_re, one_im, two_re, two_im = (moments[:, k * states : (k + 1) * states] for k in range(4))
    scale = scale_in[...]
    hat_re, hat_im = scale * real[...], scale * imag[...]
    grad_decay[...] = -(hat_re * two_re - hat_im * two_im) + jnp.exp(-2.0 * decay[...]) / scale * (
        real[...] * one_re - imag[...] * one_im
    )
    grad_freq[...] = -(hat_re * two_im + hat_im * two_re)
    grad_real[...] = scale * one_re
    grad_imag[...] = -scale * one_im
    for k, vector in enumerate(vectors):
        lines = [t[chans + k : chans + k + 1, 0:chans] for t in sums]
        vector[...] = jnp.concatenate(lines, axis=1) if subs > 1 else lines[0]


def final_kernel(arrived, tokens, cotangent, out):
    seqs, rows, width = tokens.shape
    inner = arrived[...].reshape(width, seqs * rows).astype(F32).T
    for n in range(seqs):
        d = inner[n * rows : (n + 1) * rows]
        xhat, inv = row_stats(tokens[n].astype(F32))
        mean = jnp.mean(d, axis=-1, keepdims=True)
        along = jnp.mean(d * xhat, axis=-1, keepdims=True)
        grad = (d - mean - xhat * along) * inv
        out[n] = (cotangent[n].astype(F32) + grad).astype(BF16)


def call(kernel, micros, outs, ins, scratch=()):
    return pl.pallas_call(
        kernel,
        out_shape=[(pltpu.HBM if len(o) > 2 else jax.ShapeDtypeStruct)(*o[:2]) for o in outs],
        in_specs=ins,
        out_specs=[HBM if len(o) > 2 else VMEM for o in outs],
        scratch_shapes=list(scratch),
        compiler_params=PARAMS,
        cost_estimate=pl.CostEstimate(
            flops=int(micros * 1e9), bytes_accessed=int(micros * 3.5e6), transcendentals=0
        ),
    )


def in_hbm(*arrays):
    return [pltpu.with_memory_space_constraint(a, pltpu.HBM) for a in arrays]


def per_device(
    plan, tokens, lengths, out_weight, out_bias, decay_rate, frequency, coef_real, coef_imag,
    skip, gain, shift, cotangent,
):
    seqs, rows, width = tokens.shape
    chunks, subs = plan.chunks, plan.subs
    blocks = 2 * chunks
    chans = width // blocks
    own, states = decay_rate.shape
    total = blocks * seqs
    mine, shard = lax.axis_index("ctx"), lax.axis_index("shard")
    layer = shard // 2

    def exchange(buffer):
        return lax.all_to_all(buffer, BOTH, 0, 0, axis_index_groups=plan.groups, tiled=True)

    segment = out_bias.shape[0]
    pack, scale, piece = call(
        pack_kernel,
        2,
        [((own, 3 * LANES), F32), ((own, states), F32), ((own + 16, 2 * width), BF16)],
        [VMEM] * 9,
    )(
        *in_hbm(
            decay_rate, frequency, coef_real, coef_imag,
            skip[None], gain[None], shift[None], out_weight, out_bias[None],
        )
    )
    if subs > 1:
        pack = lax.dynamic_slice_in_dim(pack, lax.rem(mine, subs) * chans, chans, 0)
    pack = lax.ppermute(pack, BOTH, plan.fetch)

    def here(shape, dtype=BF16):
        return pltpu.VMEM(shape, dtype)

    def sems(*shape):
        return pltpu.SemaphoreType.DMA(shape)

    wire = ((blocks, chans, seqs * rows), BF16, 1)
    partner = lax.ppermute(lengths, "shard", plan.across)
    flow, like_tokens = wire[:2], (tokens.shape, BF16)
    on_wire = here(wire[0])
    (first,) = call(
        norm_kernel, COST[0], [flow], [VMEM]
    )(tokens)
    first = exchange(first)
    piece, pack = lax.optimization_barrier((piece, pack))
    near = [piece] + [lax.ppermute(piece, "shard", route) for route in plan.climb]
    table_type, line_type = ((chans, LANES, LANES), BF16, 1), ((chans, 8, LANES), F32, 1)
    tables = [here(*table_type[:2]), here(*line_type[:2])]
    table, lines, firsts = call(
        functools.partial(table_kernel, rows),
        COST[1],
        [table_type, line_type, ((2, chans, LANES), F32)],
        [VMEM],
        tables + [sems(chans // 8 + 1)],
    )(pack)
    far_tables = in_hbm(table, lines)
    buffer, line = here((total * chans, LANES), F32), here((chans, LANES), F32)
    low = ((total * chans, LANES), BF16, 1)
    low_buffer = here(*low[:2])
    tables.append(sems(chans // 8 + 1))
    hidden, slope = call(
        functools.partial(forward_kernel, chunks, rows, plan.order),
        COST[2],
        [wire, low],
        [SMEM, SMEM, VMEM, VMEM, HBM, HBM],
        [buffer, buffer, buffer, on_wire, low_buffer] + tables + [sems(2, blocks)],
    )(lengths, partner, first, pack, *far_tables)
    prefix_type = ((chans, 2 * (total - 2 * seqs), LANES), BF16, 1)
    by_channel = ((chans, total, LANES), BF16, 1)
    mirrored, prefix = call(
        functools.partial(prefix_kernel, chunks, rows, plan.order),
        6,
        [by_channel, prefix_type],
        [SMEM, SMEM, VMEM, VMEM, HBM, HBM],
        [buffer, here(*by_channel[:2]), here(*prefix_type[:2])] + tables + [sems(2)],
    )(lengths, partner, first, pack, *far_tables)
    hidden, near = lax.optimization_barrier((hidden, near))
    across = [lax.ppermute(p, "shard", plan.across) for p in near]
    hidden = exchange(hidden)
    hidden, mirrored, prefix = lax.optimization_barrier((hidden, mirrored, prefix))
    block_out, back, outers = call(
        functools.partial(glu_kernel, plan),
        COST[3],
        [like_tokens, flow, ((seqs * rows, 2 * width), BF16)],
        [SMEM] + [VMEM] * (3 + 2 * plan.layers),
        [here((width, 2 * width))],
    )(lengths, hidden, *in_hbm(tokens, cotangent), *near, *across)
    back = exchange(back)
    half = ((plan.layers, own + 16, 2 * width), BF16)
    kept, sent = call(functools.partial(outer_kernel, plan), 2, [half, half], [VMEM] * 2)(
        hidden, outers
    )

    came = lax.ppermute(sent, "shard", plan.across)
    slab = ((own + 16, 2 * width), BF16)
    shares = call(
        functools.partial(share_kernel, plan.layers), COST[6], [slab] * plan.layers, [VMEM] * 2
    )(kept, came)
    climbed = [lax.ppermute(v, "shard", route) for v, route in zip(shares[1:], plan.climb)]
    leaving, local_grads, tallies = call(
        functools.partial(backward_kernel, chunks, rows, plan.order),
        COST[4],
        [wire, by_channel, ((2, chans, LANES), F32)],
        [SMEM, SMEM, VMEM, VMEM, VMEM, HBM, HBM, HBM],
        [buffer, buffer, buffer, low_buffer, here(*by_channel[:2]), on_wire]
        + tables
        + [sems(3, blocks)],
    )(lengths, partner, back, first, pack, *far_tables, *in_hbm(slope))
    (owned,) = call(add_kernel, 1, [slab], [VMEM] * plan.layers)(shares[0], *climbed)
    wholes = [owned] + [lax.ppermute(owned, "ctx", route) for route in plan.rotate]
    tallies, owned = lax.optimization_barrier((tallies, owned))
    state = (chans + 16, 2 * LANES)
    (sums,) = call(
        functools.partial(moment_kernel, chunks, rows),
        COST[7],
        [(state, BF16)],
        [HBM] * 4 + [VMEM] * 2,
        [line] * 7
        + [tables[0], here(*by_channel[:2]), here(*prefix_type[:2]), here(*by_channel[:2])]
        + [sems(4, chans // 8)],
    )(far_tables[0], *in_hbm(mirrored, prefix, local_grads), firsts, tallies)
    leaving, wholes = lax.optimization_barrier((exchange(leaving), wholes))
    (tokens_grad,) = call(
        final_kernel,
        COST[5],
        [like_tokens],
        [VMEM] * 3,
    )(
        leaving, *in_hbm(tokens, cotangent)
    )

    parts = [lax.ppermute(sums, BOTH, route) for route in plan.give]
    tokens_grad, parts = lax.optimization_barrier((tokens_grad, parts))
    (part,) = call(
        functools.partial(merge_kernel, subs),
        1,
        [((subs * state[0], state[1]), BF16)],
        [VMEM] * len(parts),
        [here((len(parts),) + state)],
    )(*parts)
    matrix, vector = ((own, states), F32), ((1, own), F32)
    grad_weight, grad_bias, *grads = call(
        functools.partial(owner_kernel, chunks, subs),
        2,
        [(out_weight.shape, F32), ((1, segment), F32)] + [matrix] * 4 + [vector] * 3,
        [VMEM] * (chunks + 6),
        [here((chunks,) + slab[0])],
    )(
        *wholes, part, lax.ppermute(part, "ctx", plan.beside), decay_rate, scale, coef_real, coef_imag
    )
    return (
        block_out,
        tokens_grad,
        grad_weight,
        grad_bias[0],
        *grads[:4],
        *(v[0] for v in grads[4:]),
    )


def solution(mesh):
    plan = Plan(mesh.shape["shard"], mesh.shape["ctx"])
    rows = P("shard", "ctx", None)
    matrix = P("shard", None)
    vector = P("shard")
    in_specs = (rows, vector, matrix, vector) + (matrix,) * 4 + (vector,) * 3 + (rows,)
    out_specs = (rows, rows, matrix, vector) + (matrix,) * 4 + (vector,) * 3
    return jax.shard_map(
        functools.partial(per_device, plan),
        mesh=mesh,
        in_specs=in_specs,
        out_specs=out_specs,
        check_vma=False,
    )
```

```python
import functools
import math

import jax
import jax.numpy as jnp
from jax import lax
from jax.experimental import pallas as pl
from jax.experimental.pallas import tpu as pltpu
from jax.sharding import PartitionSpec as P

EPSILON = 1e-05
LANES = 128
GROUPS = (32, 32, 16, 16)
COST = (2, 8, 10, 6, 1, 3, 2, 8)
BOTH = ("shard", "ctx")
F32 = jnp.float32
BF16 = jnp.bfloat16
VMEM = pl.BlockSpec(memory_space=pltpu.VMEM)
SMEM = pl.BlockSpec(memory_space=pltpu.SMEM)
HBM = pl.BlockSpec(memory_space=pltpu.HBM)
PARAMS = pltpu.CompilerParams(vmem_limit_bytes=20 * 1024 * 1024)


class Plan:
    def __init__(self, shards, chunks):
        layers = shards // 2
        self.shards, self.chunks = shards, chunks
        self.subs = subs = chunks // layers
        self.order = [
            (core, top * subs + sub)
            for top in range(chunks // subs)
            for core in range(2)
            for sub in range(subs)
        ]
        self.groups = [
            [(2 * z + core) * chunks + c for core, c in self.order] for z in range(layers)
        ]
        members = [(z, core, c) for z in range(layers) for core, c in self.order]

        def here(z, core, c):
            return (2 * z + core) * chunks + c

        def owner(z, core, c, turn):
            place = (z * subs + c % subs + turn) % chunks
            return (2 * (c // subs) + core) * chunks + place

        self.fetch = [(owner(*m, 0), here(*m)) for m in members]
        self.give = [[(here(*m), owner(*m, turn)) for m in members] for turn in range(0, chunks, 2)]
        self.rotate = [
            [(a, (a + turn) % chunks) for a in range(chunks)] for turn in range(1, chunks)
        ]
        self.beside = [(a, a ^ 1) for a in range(chunks)]
        self.layers = layers
        self.climb = [
            [(s, (s + 2 * turn) % shards) for s in range(shards)] for turn in range(1, layers)
        ]
        self.across = [(s, s ^ 1) for s in range(shards)]


def row_stats(rows):
    mean = jnp.mean(rows, axis=-1, keepdims=True)
    centered = rows - mean
    var = jnp.mean(centered * centered, axis=-1, keepdims=True)
    inv = lax.rsqrt(var + EPSILON)
    return centered * inv, inv


def dot(a, b, over):
    return lax.dot_general(a, b, (((over[0],), (over[1],)), ((), ())), preferred_element_type=F32)


def pack_kernel(decay, freq, real, imag, skip, gain, shift, weight, bias, pack, scales, piece):
    own, states = decay.shape
    wide = weight.shape[1]
    rate = decay[...]
    square = rate * rate
    scale = jnp.sqrt(2.0 * rate * jnp.exp(-rate) * (1.0 + square / 6.0 * (1.0 + square / 20.0)))
    scales[...] = scale
    pack[:, 0:LANES] = jnp.concatenate([rate, freq[...]], axis=1)
    pack[:, LANES : 2 * LANES] = jnp.concatenate([scale * real[...], scale * imag[...]], axis=1)
    lane = lax.broadcasted_iota(jnp.int32, (own, LANES), 1)
    diagonal = lax.broadcasted_iota(jnp.int32, (own, own), 0) == lax.broadcasted_iota(jnp.int32, (own, own), 1)
    tail = jnp.zeros((own, LANES), F32)
    for k, vector in enumerate((skip, gain, shift)):
        column = jnp.sum(jnp.where(diagonal, vector[...], 0.0), axis=1, keepdims=True)
        tail = jnp.where(lane == k, column, tail)
    pack[:, 2 * LANES :] = tail
    segment = bias.shape[1]
    flat = LANES * lax.broadcasted_iota(jnp.int32, (own, LANES), 0) + lane
    repeated = jnp.concatenate([bias[...]] * (LANES // segment), axis=1)
    piece[:, 0:wide] = weight[...].astype(BF16)
    here = flat // segment == lax.axis_index("shard")
    piece[:, wide:] = jnp.where(here, repeated, 0.0).astype(BF16)


def copying(source, target, sem):
    copy = pltpu.make_async_copy(source, target, sem)
    copy.start()
    return copy


def wait_all(copies):
    for copy in copies:
        copy.wait()


def valid_count(lengths, n, rows):
    return jnp.clip(lengths[n] - lax.axis_index("ctx") * rows, 0, rows)


def norm_kernel(tokens, out):
    seqs, rows, width = tokens.shape
    xhat, _ = row_stats(tokens[...].reshape(seqs * rows, width).astype(F32))
    out[...] = xhat.T.astype(BF16).reshape(out.shape)


def split_lanes(wide, rows, count):
    lane = lax.broadcasted_iota(jnp.int32, (1, LANES), 1)
    pieces = []
    for n in range(count):
        at, off = divmod(n * rows, LANES)
        turn = (LANES - off) % LANES
        piece = wide[:, at * LANES : (at + 1) * LANES]
        if turn:
            piece = pltpu.roll(piece, turn, 1)
        if off + rows > LANES:
            after = pltpu.roll(wide[:, (at + 1) * LANES : (at + 2) * LANES], turn, 1)
            piece = jnp.where(lane < turn, piece, after)
        pieces.append(piece)
    return pieces


def join_lanes(pieces, rows):
    lane = lax.broadcasted_iota(jnp.int32, (1, LANES), 1)
    columns = [None] * (len(pieces) * rows // LANES)
    for n, piece in enumerate(pieces):
        at, off = divmod(n * rows, LANES)
        turned = pltpu.roll(piece, off, 1) if off else piece
        columns[at] = turned if off == 0 else jnp.where(lane < off, columns[at], turned)
        if off + rows > LANES:
            columns[at + 1] = turned
    return jnp.concatenate(columns, axis=1)


def count_of(lengths, partner, order, block, n, rows):
    core, c = order[block]
    own = lax.rem(lax.axis_index("shard"), 2) == core
    return jnp.clip(jnp.where(own, lengths[n], partner[n]) - c * rows, 0, rows)


def swap(values):
    return pltpu.roll(values, LANES // 2, values.ndim - 1)


def table_kernel(rows, pack, far_table, far_lines, firsts, table, lines, sems):
    chans = pack.shape[0]
    low2 = lax.broadcasted_iota(jnp.int32, (1, LANES), 1) < LANES // 2
    low3 = low2[None]
    angle = jnp.where(low2, 0.0, math.pi / 2)
    step = 8
    offsets = lax.broadcasted_iota(jnp.int32, (1, step, 1), 1).astype(F32)

    def spread(pair):
        other = swap(pair)
        return jnp.where(low2, pair, other), jnp.where(low2, other, pair)

    def factors(power):
        other = swap(power)
        return jnp.where(low2, power, other), jnp.where(low2, -other, power)

    def block(at, _):
        here = pl.ds(pl.multiple_of(at * step, step), step)
        decay, freq = spread(pack[here, 0:LANES])
        real, imag = spread(pack[here, LANES : 2 * LANES])

        def power(by):
            return jnp.exp(-decay * by) * jnp.cos(freq * by - angle)

        part = jnp.exp(-decay[:, None, :] * offsets) * jnp.cos(freq[:, None, :] * offsets - angle[None])
        table[here, 0:step] = part.astype(BF16)
        size = step
        while size < LANES:
            same, cross = factors(power(float(size)))
            new = part * same[:, None, :] + swap(part) * cross[:, None, :]
            table[here, size : 2 * size] = new.astype(BF16)
            part = jnp.concatenate([part, new], axis=1)
            size *= 2
        copying(table.at[here], far_table.at[here], sems.at[at])
        real = jnp.where(low2, real, -real)
        whole = part.astype(BF16)
        hat = jnp.where(low2, real, -imag).astype(BF16)
        for k in range(step):
            row = jnp.broadcast_to(hat[k : k + 1], (step, LANES))
            lines[at * step + k, 0:1] = dot(row, whole[k], (1, 1))[0:1]
        one = power(1.0)
        same, cross = factors(one)
        firsts[0, here] = same
        firsts[1, here] = cross
        chunk_same, chunk_cross = factors(power(float(rows)))
        hat_re = jnp.where(low2, real, -real)
        turn_re = hat_re * same - imag * jnp.where(low2, -cross, cross)
        turn_im = hat_re * jnp.where(low2, -cross, cross) + imag * same
        for k, line in enumerate((chunk_same, chunk_cross, jnp.where(low2, turn_re, -turn_re), -turn_im)):
            lines[here, k + 1 : k + 2] = line[:, None, :]
        return 0

    count = chans // step
    lax.fori_loop(0, count, block, 0, unroll=min(8, count))
    for at in range(count):
        here = pl.ds(at * step, step)
        pltpu.make_async_copy(table.at[here], far_table.at[here], sems.at[at]).wait()
    copying(lines, far_lines, sems.at[count]).wait()


def paired(lefts, rights, over):
    outs = []
    for k in range(0, len(lefts), 2):
        rows = lefts[k].shape[0]
        left = jnp.concatenate(lefts[k : k + 2], axis=0)
        right = jnp.concatenate(rights[k : k + 2], axis=1 - over[1])
        both = dot(left, right, over)
        outs += [both[0:rows, 0:LANES], both[rows:, LANES:]]
    return outs


def upper_half(rows):
    square = (rows, LANES)
    return lax.broadcasted_iota(jnp.int32, square, 1) >= lax.broadcasted_iota(jnp.int32, square, 0)


def toeplitz(upper, taps):
    slid = pltpu.roll(jnp.broadcast_to(taps, upper.shape), 0, 1, stride=1, stride_axis=0)
    body = jnp.where(upper, slid, 0.0).astype(BF16)
    return jnp.concatenate([body, jnp.zeros((LANES - upper.shape[0], LANES), BF16)], axis=0)


def mirror_matrix(rows):
    square = (LANES, LANES)
    reach = lax.broadcasted_iota(jnp.int32, square, 0) + lax.broadcasted_iota(jnp.int32, square, 1)
    return jnp.where(reach == rows - 1, 1.0, 0.0).astype(BF16)


def place(order, seqs, block, n):
    core, c = order[block]
    return (c * 2 + core) * seqs + n


def fetch_tables(size, far_table, table, far_lines, lines, sems):
    count = table.shape[0] // size
    copying(far_lines, lines, sems.at[count])
    for at in range(count):
        here = pl.ds(at * size, size)
        copying(far_table.at[here], table.at[here], sems.at[at])


def await_table(size, far_table, table, sems, at):
    here = pl.ds(at * size, size)
    pltpu.make_async_copy(far_table.at[here], table.at[here], sems.at[at]).wait()


def await_lines(size, far_lines, lines, sems):
    pltpu.make_async_copy(far_lines, lines, sems.at[lines.shape[0] // size]).wait()


def gelu_and_slope(x):
    c = math.sqrt(2.0 / math.pi)
    square = x * x
    t = jnp.tanh(c * x * (1.0 + 0.044715 * square))
    half = 0.5 * (1.0 + t)
    return x * half, half + 0.5 * x * (1.0 - t * t) * (c + 3.0 * 0.044715 * c * square)


def forward_kernel(
    chunks, rows, order, lengths, partner, arrived, pack, far_table, far_lines, far_hidden, far_kept,
    inputs, mirrored, mixed, hidden, kept, table, lines, sems, out_sems,
):
    size = min(GROUPS[0], far_table.shape[0])
    fetch_tables(size, far_table, table, far_lines, lines, sems)
    blocks, chans, wide = arrived.shape
    seqs = wide // rows
    total = blocks * seqs
    each = 2 * seqs
    lane = lax.broadcasted_iota(jnp.int32, (1, LANES), 1)
    gain, shift = pack[:, 257:258], pack[:, 258:259]
    mirror = mirror_matrix(rows)
    upper = upper_half(rows)
    for b in range(blocks):
        for n, xhat in enumerate(split_lanes(arrived[b].astype(F32), rows, seqs)):
            here = pl.ds(place(order, seqs, b, n) * chans, chans)
            inside = lane < count_of(lengths, partner, order, b, n, rows)
            x = jnp.where(inside, xhat * gain + shift, 0.0).astype(BF16)
            inputs[here, :] = x.astype(F32)
            mirrored[here, :] = dot(x, mirror, (1, 0))

    def group(at, _):
        members = range(size)
        await_table(size, far_table, table, sems, at)
        mine = [pl.ds(at * size + k, total, stride=chans) for k in members]
        line = [lines[at * size + k] for k in members]
        powers = [table[at * size + k] for k in members]
        ends = paired([mirrored[mine[k], :].astype(BF16) for k in members], powers, (1, 0))
        local = paired(
            [inputs[mine[k], :].astype(BF16) for k in members],
            [toeplitz(upper, line[k][0:1]) for k in members],
            (1, 0),
        )
        for k in members:
            state = ends[k][0:each]
            carried = [jnp.zeros((each, LANES), F32)]
            for c in range(1, chunks):
                carried.append(state * line[k][3:4] + swap(state) * line[k][4:5])
                if c < chunks - 1:
                    state = state * line[k][1:2] + swap(state) * line[k][2:3]
                    state += ends[k][each * c : each * (c + 1)]
            ends[k] = jnp.concatenate(carried, axis=0).astype(BF16)
        far = paired(ends, [table[at * size + k] for k in members], (1, 1))
        for k in members:
            mixed[mine[k], :] = local[k] + far[k]
        return 0

    await_lines(size, far_lines, lines, sems)
    lax.fori_loop(0, chans // size, group, 0)
    stored = []
    skip = pack[:, 256:257]
    for b in range(blocks):
        values = []
        for n in range(seqs):
            here = pl.ds(place(order, seqs, b, n) * chans, chans)
            mix = mixed[here, :] + skip * inputs[here, :]
            value, slope = gelu_and_slope(mix)
            kept[here, :] = jnp.where(lane < rows, slope, 0.0).astype(BF16)
            values.append(value)
        hidden[b] = join_lanes(values, rows).astype(BF16)
        here = pl.ds(place(order, seqs, b, 0) * chans, seqs * chans)
        stored.append(copying(hidden.at[b], far_hidden.at[b], out_sems.at[0, b]))
        stored.append(copying(kept.at[here], far_kept.at[here], out_sems.at[1, b]))
    wait_all(stored)


def glu_kernel(plan, lengths, arrived, tokens, cotangent, *refs):
    layers = plan.layers
    pieces, (block_out, leaving, outers, w) = refs[: 2 * layers], refs[2 * layers :]
    seqs, rows, width = tokens.shape
    own = width // plan.shards
    shard = lax.axis_index("shard")
    layer, core = shard // 2, lax.rem(shard, 2)
    bias = jnp.zeros((16, LANES), F32)
    for side in range(2):
        for turn in range(layers):
            piece = pieces[side * layers + turn]
            home = 2 * lax.rem(layer + layers - turn, layers) + lax.rem(core + side, 2)
            w[pl.ds(pl.multiple_of(home * own, own), own), :] = piece[:, 0 : 2 * width]
            bias += piece[0:16, 2 * width :].astype(F32)
    bias = jnp.concatenate([bias[k : k + 1] for k in range(2 * width // LANES)], axis=1)
    position = lax.broadcasted_iota(jnp.int32, (rows, width), 0)
    hidden = arrived[...].reshape(width, seqs * rows).astype(F32).T.astype(BF16)
    for n in range(seqs):
        here = slice(n * rows, (n + 1) * rows)
        proj = dot(hidden[here], w[...], (1, 0)) + bias
        r, q = proj[:, :width], proj[:, width:]
        valid = jnp.where(position < valid_count(lengths, n, rows), 1.0, 0.0)
        open_ = jax.nn.sigmoid(q)
        e = valid * cotangent[n].astype(F32)
        first = e * open_
        outers[here, :] = jnp.concatenate([first, first * r * (1.0 - open_)], axis=1).astype(BF16)
        block_out[n] = (tokens[n].astype(F32) + valid * (r * open_)).astype(BF16)
    back = dot(outers[...], w[...], (1, 1))
    leaving[...] = back.T.astype(BF16).reshape(leaving.shape)


def outer_kernel(plan, arrived, outers, kept, sent):
    chans = arrived.shape[1]
    layers, subs = plan.layers, plan.subs
    own, wide = chans * subs, outers.shape[1]
    core = lax.rem(lax.axis_index("shard"), 2)
    outer = outers[...]
    bias = jnp.sum(outer.astype(F32), axis=0, keepdims=True)
    tail = [bias[:, k * LANES : (k + 1) * LANES] for k in range(wide // LANES)]
    tail.append(jnp.zeros((own - len(tail), LANES), F32))
    tail = jnp.concatenate(tail, axis=0).astype(BF16)
    for side, out in enumerate((sent, kept)):
        which = lax.rem(core + 1 - side, 2)
        members = [(2 * z + which) * subs + sub for z in range(layers) for sub in range(subs)]
        left = jnp.concatenate([arrived[member] for member in members], axis=0)
        out[:, :, 0:wide] = dot(left, outer, (1, 0)).astype(BF16).reshape(layers, own, wide)
        for z in range(layers):
            out[z, :, wide:] = tail


def backward_kernel(
    chunks, rows, order, lengths, partner, arrived, first, pack, far_table, far_lines, far_slope,
    far_leaving, far_kept, tallies,
    grads, local, cross, slope, kept, leaving, table, lines, sems, more_sems,
):
    size = min(GROUPS[1], far_table.shape[0])
    blocks, chans, wide = arrived.shape
    seqs = wide // rows
    total = blocks * seqs
    each = 2 * seqs
    lane = lax.broadcasted_iota(jnp.int32, (1, LANES), 1)
    skip, gain = pack[:, 256:257], pack[:, 257:258]
    mirror = mirror_matrix(rows)
    upper = upper_half(rows)
    spans = [pl.ds(place(order, seqs, b, 0) * chans, seqs * chans) for b in range(blocks)]
    fetched = [
        copying(far_slope.at[span], slope.at[span], more_sems.at[0, b]) for b, span in enumerate(spans)
    ]
    fetch_tables(size, far_table, table, far_lines, lines, sems)
    stored = []
    for b in range(blocks):
        fetched[b].wait()
        for n, back in enumerate(split_lanes(arrived[b].astype(F32), rows, seqs)):
            here = pl.ds(place(order, seqs, b, n) * chans, chans)
            g = (back * slope[here, :].astype(F32)).astype(BF16)
            grads[here, :] = g.astype(F32)

    def group(at, _):
        members = range(size)
        await_table(size, far_table, table, sems, at)
        which = [at * size + k for k in members]
        mine = [pl.ds(h, total, stride=chans) for h in which]
        line = [lines[h] for h in which]
        powers = [table[h] for h in which]
        low = [grads[mine[k], :].astype(BF16) for k in members]
        ends = paired(low, powers, (1, 0))
        near = paired(low, [toeplitz(upper, line[k][0:1]) for k in members], (1, 1))
        for k in members:
            kept[which[k]] = low[k]
            local[mine[k], :] = near[k]
        for k in members:
            parts = [jnp.zeros((each, LANES), F32)]
            state = ends[k][each * (chunks - 1) :]
            for c in range(chunks - 2, -1, -1):
                parts.append(state * line[k][3:4] + swap(state) * line[k][4:5])
                if c:
                    state = state * line[k][1:2] + swap(state) * line[k][2:3]
                    state += ends[k][each * c : each * (c + 1)]
            ends[k] = jnp.concatenate(parts[::-1], axis=0).astype(BF16)
        far = paired(ends, powers, (1, 1))
        for k in members:
            cross[mine[k], :] = far[k]
        return 0

    await_lines(size, far_lines, lines, sems)
    lax.fori_loop(0, chans // size, group, 0)
    stored.append(copying(kept, far_kept, more_sems.at[1, 0]))
    gains = shifts = jnp.zeros((chans, LANES), F32)
    for b in range(blocks):
        inner = []
        for n, xhat in enumerate(split_lanes(first[b].astype(F32), rows, seqs)):
            here = pl.ds(place(order, seqs, b, n) * chans, chans)
            grad = local[here, :] + skip * grads[here, :]
            grad += dot(cross[here, :].astype(BF16), mirror, (1, 0))
            m = jnp.where(lane < count_of(lengths, partner, order, b, n, rows), grad, 0.0)
            gains += m * xhat
            shifts += m
            inner.append(gain * m)
        leaving[b] = join_lanes(inner, rows).astype(BF16)
        stored.append(copying(leaving.at[b], far_leaving.at[b], more_sems.at[2, b]))
    tallies[0] = gains
    tallies[1] = shifts
    wait_all(stored)


def prefix_kernel(
    chunks, rows, order, lengths, partner, first, pack, far_table, far_lines, far_mirrored, far_prefix,
    mirrored, kept, prefix, table, lines, sems, out_sems,
):
    size = min(GROUPS[2], far_table.shape[0])
    fetch_tables(size, far_table, table, far_lines, lines, sems)
    blocks, chans, wide = first.shape
    seqs = wide // rows
    total = blocks * seqs
    each = 2 * seqs
    lane = lax.broadcasted_iota(jnp.int32, (1, LANES), 1).astype(F32)
    gain, shift = pack[:, 257:258], pack[:, 258:259]
    mirror = mirror_matrix(rows)
    for b in range(blocks):
        for n, xhat in enumerate(split_lanes(first[b].astype(F32), rows, seqs)):
            here = pl.ds(place(order, seqs, b, n) * chans, chans)
            inside = lane < count_of(lengths, partner, order, b, n, rows).astype(F32)
            x = jnp.where(inside, xhat * gain + shift, 0.0).astype(BF16)
            mirrored[here, :] = dot(x, mirror, (1, 0))

    def group(at, _):
        members = range(size)
        await_table(size, far_table, table, sems, at)
        which = [at * size + k for k in members]
        line = [lines[h] for h in which]
        ends = []
        for k in members:
            x_back = mirrored[pl.ds(which[k], total, stride=chans), :]
            kept[which[k]] = x_back.astype(BF16)
            stack = jnp.concatenate([x_back, x_back * lane], axis=0).astype(BF16)
            ends.append(dot(stack, table[which[k]], (1, 0)))
        for k in members:

            def onward(state):
                return state * line[k][1:2] + swap(state) * line[k][2:3]

            state, slope = ends[k][0:each], ends[k][total : total + each]
            states, slopes = [state], [state + slope]
            for c in range(1, chunks - 1):
                slope = onward(slope + float(rows) * state) + ends[k][total + each * c : total + each * (c + 1)]
                state = onward(state) + ends[k][each * c : each * (c + 1)]
                states.append(state)
                slopes.append(state + slope)
            prefix[which[k]] = jnp.concatenate(states + slopes, axis=0).astype(BF16)
        return 0

    await_lines(size, far_lines, lines, sems)
    lax.fori_loop(0, chans // size, group, 0)
    wait_all([copying(kept, far_mirrored, out_sems.at[0]), copying(prefix, far_prefix, out_sems.at[1])])


def moment_kernel(
    chunks, rows, far_table, far_mirrored, far_prefix, far_grads, firsts, tallies, sums,
    cross_one_a, cross_one_b, cross_two_a, cross_two_b, local_one, local_two, corrs,
    table, mirrored, prefix, grads, sems,
):
    size = min(GROUPS[3], far_table.shape[0])
    chans, total, _ = far_grads.shape
    each = total // chunks
    count = chans // size
    pairs = (
        (far_grads, grads), (far_table, table), (far_mirrored, mirrored), (far_prefix, prefix)
    )
    for at in range(count):
        here = pl.ds(at * size, size)
        for k, (far, near) in enumerate(pairs):
            copying(far.at[here], near.at[here], sems.at[k, at])
    lane = lax.broadcasted_iota(jnp.int32, (1, LANES), 1).astype(F32)
    square = (rows, LANES)
    behind = lax.broadcasted_iota(jnp.int32, square, 1) <= (
        LANES - rows + lax.broadcasted_iota(jnp.int32, square, 0)
    )

    def group(at, _):
        members = range(size)
        which = [at * size + k for k in members]
        here = pl.ds(at * size, size)
        for k, (far, near) in enumerate(pairs):
            pltpu.make_async_copy(far.at[here], near.at[here], sems.at[k, at]).wait()
        ends, outer, both = [], [], []
        powers = [table[h] for h in which]
        for k in members:
            g = grads[which[k]]
            ends.append(jnp.concatenate([g, (g.astype(F32) * lane).astype(BF16)], axis=0))
        ends = paired(ends, powers, (1, 0))
        for k in members:
            outer.append(dot(mirrored[which[k]], grads[which[k]], (0, 0)))
        for k in members:
            one = pl.ds(which[k], 1)
            later, later_slope = ends[k][each:total], ends[k][total + each :]
            before = prefix[which[k]].astype(F32)
            state, slope = before[0 : total - each], before[total - each :]
            swapped, swapped_slope = swap(later), swap(later_slope)
            for into, value in (
                (cross_one_a, state * later),
                (cross_one_b, state * swapped),
                (cross_two_a, slope * later + state * later_slope),
                (cross_two_b, slope * swapped + state * swapped_slope),
            ):
                into[one, :] = jnp.sum(value, axis=0, keepdims=True)
            slid = pltpu.roll(outer[k][0:rows], LANES - rows + 1, 1, stride=1, stride_axis=0)
            corr = jnp.sum(jnp.where(behind, slid, 0.0), axis=0, keepdims=True)
            corrs[one, :] = corr
            pair = jnp.concatenate([corr, corr * lane, jnp.zeros((14, LANES), F32)], axis=0)
            both.append(pair)
        for k, turned in enumerate(paired([p.astype(BF16) for p in both], powers, (1, 0))):
            local_one[pl.ds(which[k], 1), :] = turned[0:1]
            local_two[pl.ds(which[k], 1), :] = turned[1:2]
        return 0

    lax.fori_loop(0, count, group, 0)
    low = lax.broadcasted_iota(jnp.int32, (1, LANES), 1) < LANES // 2
    for k, (a, b, near) in enumerate(
        ((cross_one_a, cross_one_b, local_one), (cross_two_a, cross_two_b, local_two))
    ):
        far = jnp.where(low, a[...] - swap(a[...]), b[...] + swap(b[...]))
        moment = far * firsts[0] + swap(far) * firsts[1] + near[...]
        sums[0:chans, k * LANES : (k + 1) * LANES] = moment.astype(BF16)
    diagonal = lax.broadcasted_iota(jnp.int32, (chans, 2 * LANES), 0) == lax.broadcasted_iota(
        jnp.int32, (chans, 2 * LANES), 1
    )
    row = lax.broadcasted_iota(jnp.int32, (16, 2 * LANES), 0)
    tail = jnp.zeros((16, 2 * LANES), F32)
    columns = [corrs[:, 0:1]] + [jnp.sum(tallies[k], axis=1, keepdims=True) for k in range(2)]
    for k, column in enumerate(columns):
        line = jnp.sum(jnp.where(diagonal, column, 0.0), axis=0, keepdims=True)
        tail = jnp.where(row == k, line, tail)
    sums[chans:, :] = tail.astype(BF16)


def share_kernel(layers, kept, came, *outs):
    layer = lax.axis_index("shard") // 2
    for turn, out in enumerate(outs):
        at = lax.rem(layer + turn, layers)
        out[...] = (kept[at].astype(F32) + came[at].astype(F32)).astype(BF16)


def add_kernel(*refs):
    total = refs[0][...].astype(F32)
    for ref in refs[1:-1]:
        total += ref[...].astype(F32)
    refs[-1][...] = total.astype(BF16)


def merge_kernel(subs, *refs):
    parts, (out, slots) = refs[:-2], refs[-2:]
    count = len(parts)
    mine = lax.axis_index("ctx")
    for turn, part in enumerate(parts):
        slots[lax.rem(mine // 2 + count - turn, count)] = part[...]
    total = slots[0].astype(F32)
    for k in range(1, count):
        total += slots[k].astype(F32)
    rows = total.shape[0]
    if subs == 1:
        out[...] = total.astype(BF16)
    else:
        out[...] = jnp.zeros(out.shape, BF16)
        out[pl.ds(pl.multiple_of(lax.rem(mine, subs) * rows, rows), rows), :] = total.astype(BF16)


def owner_kernel(chunks, subs, *refs):
    slabs, refs = refs[:chunks], refs[chunks:]
    one, two, decay, scale_in, real, imag = refs[:6]
    grad_weight, grad_bias, grad_decay, grad_freq, grad_real, grad_imag, *vectors, slots = refs[6:]
    own, states = decay.shape
    wide = grad_weight.shape[1]
    mine = lax.axis_index("ctx")
    for turn, slab in enumerate(slabs):
        slots[lax.rem(mine + chunks - turn, chunks)] = slab[...]
    slab = slots[0].astype(F32)
    for k in range(1, chunks):
        slab += slots[k].astype(F32)
    grad_weight[...] = slab[:, 0:wide]
    segment = grad_bias.shape[1]
    shard = lax.axis_index("shard")
    row = jnp.zeros((1, segment), F32)
    for s in range(wide // segment):
        at, off = divmod(s * segment, LANES)
        row = jnp.where(shard == s, slab[at : at + 1, wide + off : wide + off + segment], row)
    grad_bias[...] = row
    chans = own // subs
    each = chans + 16
    total = one[...].astype(F32) + two[...].astype(F32)
    sums = [total[each * sub : each * (sub + 1)] for sub in range(subs)]
    moments = jnp.concatenate([t[0:chans] for t in sums], axis=0)
    one_re, one_im, two_re, two_im = (moments[:, k * states : (k + 1) * states] for k in range(4))
    scale = scale_in[...]
    hat_re, hat_im = scale * real[...], scale * imag[...]
    grad_decay[...] = -(hat_re * two_re - hat_im * two_im) + jnp.exp(-2.0 * decay[...]) / scale * (
        real[...] * one_re - imag[...] * one_im
    )
    grad_freq[...] = -(hat_re * two_im + hat_im * two_re)
    grad_real[...] = scale * one_re
    grad_imag[...] = -scale * one_im
    for k, vector in enumerate(vectors):
        lines = [t[chans + k : chans + k + 1, 0:chans] for t in sums]
        vector[...] = jnp.concatenate(lines, axis=1) if subs > 1 else lines[0]


def final_kernel(arrived, tokens, cotangent, out):
    seqs, rows, width = tokens.shape
    inner = arrived[...].reshape(width, seqs * rows).astype(F32).T
    for n in range(seqs):
        d = inner[n * rows : (n + 1) * rows]
        xhat, inv = row_stats(tokens[n].astype(F32))
        mean = jnp.mean(d, axis=-1, keepdims=True)
        along = jnp.mean(d * xhat, axis=-1, keepdims=True)
        grad = (d - mean - xhat * along) * inv
        out[n] = (cotangent[n].astype(F32) + grad).astype(BF16)


def call(kernel, micros, outs, ins, scratch=()):
    return pl.pallas_call(
        kernel,
        out_shape=[(pltpu.HBM if len(o) > 2 else jax.ShapeDtypeStruct)(*o[:2]) for o in outs],
        in_specs=ins,
        out_specs=[HBM if len(o) > 2 else VMEM for o in outs],
        scratch_shapes=list(scratch),
        compiler_params=PARAMS,
        cost_estimate=pl.CostEstimate(
            flops=int(micros * 1e9), bytes_accessed=int(micros * 3.5e6), transcendentals=0
        ),
    )


def in_hbm(*arrays):
    return [pltpu.with_memory_space_constraint(a, pltpu.HBM) for a in arrays]


def per_device(
    plan, tokens, lengths, out_weight, out_bias, decay_rate, frequency, coef_real, coef_imag,
    skip, gain, shift, cotangent,
):
    seqs, rows, width = tokens.shape
    chunks, subs = plan.chunks, plan.subs
    blocks = 2 * chunks
    chans = width // blocks
    own, states = decay_rate.shape
    total = blocks * seqs
    mine, shard = lax.axis_index("ctx"), lax.axis_index("shard")
    layer = shard // 2

    def exchange(buffer):
        return lax.all_to_all(buffer, BOTH, 0, 0, axis_index_groups=plan.groups, tiled=True)

    segment = out_bias.shape[0]
    pack, scale, piece = call(
        pack_kernel,
        2,
        [((own, 3 * LANES), F32), ((own, states), F32), ((own, 2 * width + LANES), BF16)],
        [VMEM] * 9,
    )(
        *in_hbm(
            decay_rate, frequency, coef_real, coef_imag,
            skip[None], gain[None], shift[None], out_weight, out_bias[None],
        )
    )
    if subs > 1:
        pack = lax.dynamic_slice_in_dim(pack, lax.rem(mine, subs) * chans, chans, 0)
    pack = lax.ppermute(pack, BOTH, plan.fetch)

    def here(shape, dtype=BF16):
        return pltpu.VMEM(shape, dtype)

    def sems(*shape):
        return pltpu.SemaphoreType.DMA(shape)

    wire = ((blocks, chans, seqs * rows), BF16, 1)
    partner = lax.ppermute(lengths, "shard", plan.across)
    flow, like_tokens = wire[:2], (tokens.shape, BF16)
    on_wire = here(wire[0])
    (first,) = call(
        norm_kernel, COST[0], [flow], [VMEM]
    )(tokens)
    first = exchange(first)
    piece, pack = lax.optimization_barrier((piece, pack))
    near = [piece] + [lax.ppermute(piece, "shard", route) for route in plan.climb]
    table_type, line_type = ((chans, LANES, LANES), BF16, 1), ((chans, 8, LANES), F32, 1)
    tables = [here(*table_type[:2]), here(*line_type[:2])]
    table, lines, firsts = call(
        functools.partial(table_kernel, rows),
        COST[1],
        [table_type, line_type, ((2, chans, LANES), F32)],
        [VMEM],
        tables + [sems(chans // 8 + 1)],
    )(pack)
    far_tables = in_hbm(table, lines)
    buffer, line = here((total * chans, LANES), F32), here((chans, LANES), F32)
    low = ((total * chans, LANES), BF16, 1)
    low_buffer = here(*low[:2])
    tables.append(sems(chans // 8 + 1))
    hidden, slope = call(
        functools.partial(forward_kernel, chunks, rows, plan.order),
        COST[2],
        [wire, low],
        [SMEM, SMEM, VMEM, VMEM, HBM, HBM],
        [buffer, buffer, buffer, on_wire, low_buffer] + tables + [sems(2, blocks)],
    )(lengths, partner, first, pack, *far_tables)
    prefix_type = ((chans, 2 * (total - 2 * seqs), LANES), BF16, 1)
    by_channel = ((chans, total, LANES), BF16, 1)
    mirrored, prefix = call(
        functools.partial(prefix_kernel, chunks, rows, plan.order),
        6,
        [by_channel, prefix_type],
        [SMEM, SMEM, VMEM, VMEM, HBM, HBM],
        [buffer, here(*by_channel[:2]), here(*prefix_type[:2])] + tables + [sems(2)],
    )(lengths, partner, first, pack, *far_tables)
    hidden, near = lax.optimization_barrier((hidden, near))
    across = [lax.ppermute(p, "shard", plan.across) for p in near]
    hidden = exchange(hidden)
    hidden, mirrored, prefix = lax.optimization_barrier((hidden, mirrored, prefix))
    block_out, back, outers = call(
        functools.partial(glu_kernel, plan),
        COST[3],
        [like_tokens, flow, ((seqs * rows, 2 * width), BF16)],
        [SMEM] + [VMEM] * (3 + 2 * plan.layers),
        [here((width, 2 * width))],
    )(lengths, hidden, *in_hbm(tokens, cotangent), *near, *across)
    back = exchange(back)
    half = ((plan.layers, own, 2 * width + LANES), BF16)
    kept, sent = call(functools.partial(outer_kernel, plan), 2, [half, half], [VMEM] * 2)(
        hidden, outers
    )

    came = lax.ppermute(sent, "shard", plan.across)
    slab = ((own, 2 * width + LANES), BF16)
    shares = call(
        functools.partial(share_kernel, plan.layers), COST[6], [slab] * plan.layers, [VMEM] * 2
    )(kept, came)
    climbed = [lax.ppermute(v, "shard", route) for v, route in zip(shares[1:], plan.climb)]
    leaving, local_grads, tallies = call(
        functools.partial(backward_kernel, chunks, rows, plan.order),
        COST[4],
        [wire, by_channel, ((2, chans, LANES), F32)],
        [SMEM, SMEM, VMEM, VMEM, VMEM, HBM, HBM, HBM],
        [buffer, buffer, buffer, low_buffer, here(*by_channel[:2]), on_wire]
        + tables
        + [sems(3, blocks)],
    )(lengths, partner, back, first, pack, *far_tables, *in_hbm(slope))
    (owned,) = call(add_kernel, 1, [slab], [VMEM] * plan.layers)(shares[0], *climbed)
    wholes = [owned] + [lax.ppermute(owned, "ctx", route) for route in plan.rotate]
    tallies, owned = lax.optimization_barrier((tallies, owned))
    state = (chans + 16, 2 * LANES)
    (sums,) = call(
        functools.partial(moment_kernel, chunks, rows),
        COST[7],
        [(state, BF16)],
        [HBM] * 4 + [VMEM] * 2,
        [line] * 7
        + [tables[0], here(*by_channel[:2]), here(*prefix_type[:2]), here(*by_channel[:2])]
        + [sems(4, chans // 8)],
    )(far_tables[0], *in_hbm(mirrored, prefix, local_grads), firsts, tallies)
    leaving = exchange(leaving)
    (tokens_grad,) = call(
        final_kernel,
        COST[5],
        [like_tokens],
        [VMEM] * 3,
    )(
        leaving, *in_hbm(tokens, cotangent)
    )

    parts = [lax.ppermute(sums, BOTH, route) for route in plan.give]
    tokens_grad, parts = lax.optimization_barrier((tokens_grad, parts))
    (part,) = call(
        functools.partial(merge_kernel, subs),
        1,
        [((subs * state[0], state[1]), BF16)],
        [VMEM] * len(parts),
        [here((len(parts),) + state)],
    )(*parts)
    matrix, vector = ((own, states), F32), ((1, own), F32)
    grad_weight, grad_bias, *grads = call(
        functools.partial(owner_kernel, chunks, subs),
        2,
        [(out_weight.shape, F32), ((1, segment), F32)] + [matrix] * 4 + [vector] * 3,
        [VMEM] * (chunks + 6),
        [here((chunks,) + slab[0])],
    )(
        *wholes, part, lax.ppermute(part, "ctx", plan.beside), decay_rate, scale, coef_real, coef_imag
    )
    return (
        block_out,
        tokens_grad,
        grad_weight,
        grad_bias[0],
        *grads[:4],
        *(v[0] for v in grads[4:]),
    )


def solution(mesh):
    plan = Plan(mesh.shape["shard"], mesh.shape["ctx"])
    rows = P("shard", "ctx", None)
    matrix = P("shard", None)
    vector = P("shard")
    in_specs = (rows, vector, matrix, vector) + (matrix,) * 4 + (vector,) * 3 + (rows,)
    out_specs = (rows, rows, matrix, vector) + (matrix,) * 4 + (vector,) * 3
    return jax.shard_map(
        functools.partial(per_device, plan),
        mesh=mesh,
        in_specs=in_specs,
        out_specs=out_specs,
        check_vma=False,
    )
```

```python
import functools
import math

import jax
import jax.numpy as jnp
from jax import lax
from jax.experimental import pallas as pl
from jax.experimental.pallas import tpu as pltpu
from jax.sharding import PartitionSpec as P

EPSILON = 1e-05
LANES = 128
GROUPS = (32, 32, 16, 16)
COST = (2, 8, 10, 6, 1, 3, 2, 8)
BOTH = ("shard", "ctx")
F32 = jnp.float32
BF16 = jnp.bfloat16
VMEM = pl.BlockSpec(memory_space=pltpu.VMEM)
SMEM = pl.BlockSpec(memory_space=pltpu.SMEM)
HBM = pl.BlockSpec(memory_space=pltpu.HBM)
PARAMS = pltpu.CompilerParams(vmem_limit_bytes=20 * 1024 * 1024)


class Plan:
    def __init__(self, shards, chunks):
        layers = shards // 2
        self.shards, self.chunks = shards, chunks
        self.subs = subs = chunks // layers
        self.order = [
            (core, top * subs + sub)
            for top in range(chunks // subs)
            for core in range(2)
            for sub in range(subs)
        ]
        self.groups = [
            [(2 * z + core) * chunks + c for core, c in self.order] for z in range(layers)
        ]
        members = [(z, core, c) for z in range(layers) for core, c in self.order]

        def here(z, core, c):
            return (2 * z + core) * chunks + c

        def owner(z, core, c, turn):
            place = ((layers - 1 - z) * subs + c % subs + turn) % chunks
            return (2 * (c // subs) + core) * chunks + place

        self.fetch = [(owner(*m, 0), here(*m)) for m in members]
        self.give = [[(here(*m), owner(*m, turn)) for m in members] for turn in range(0, chunks, 2)]
        self.rotate = [
            [(a, (a + turn) % chunks) for a in range(chunks)] for turn in range(1, chunks)
        ]
        self.beside = [(a, a ^ 1) for a in range(chunks)]
        self.layers = layers
        self.climb = [
            [(s, (s + 2 * turn) % shards) for s in range(shards)] for turn in range(1, layers)
        ]
        self.across = [(s, s ^ 1) for s in range(shards)]


def row_stats(rows):
    mean = jnp.mean(rows, axis=-1, keepdims=True)
    centered = rows - mean
    var = jnp.mean(centered * centered, axis=-1, keepdims=True)
    inv = lax.rsqrt(var + EPSILON)
    return centered * inv, inv


def dot(a, b, over):
    return lax.dot_general(a, b, (((over[0],), (over[1],)), ((), ())), preferred_element_type=F32)


def pack_kernel(decay, freq, real, imag, skip, gain, shift, weight, bias, pack, scales, piece):
    own, states = decay.shape
    wide = weight.shape[1]
    rate = decay[...]
    square = rate * rate
    scale = jnp.sqrt(2.0 * rate * jnp.exp(-rate) * (1.0 + square / 6.0 * (1.0 + square / 20.0)))
    scales[...] = scale
    pack[:, 0:LANES] = jnp.concatenate([rate, freq[...]], axis=1)
    pack[:, LANES : 2 * LANES] = jnp.concatenate([scale * real[...], scale * imag[...]], axis=1)
    lane = lax.broadcasted_iota(jnp.int32, (own, LANES), 1)
    diagonal = lax.broadcasted_iota(jnp.int32, (own, own), 0) == lax.broadcasted_iota(jnp.int32, (own, own), 1)
    tail = jnp.zeros((own, LANES), F32)
    for k, vector in enumerate((skip, gain, shift)):
        column = jnp.sum(jnp.where(diagonal, vector[...], 0.0), axis=1, keepdims=True)
        tail = jnp.where(lane == k, column, tail)
    pack[:, 2 * LANES :] = tail
    segment = bias.shape[1]
    flat = LANES * lax.broadcasted_iota(jnp.int32, (own, LANES), 0) + lane
    repeated = jnp.concatenate([bias[...]] * (LANES // segment), axis=1)
    piece[:, 0:wide] = weight[...].astype(BF16)
    here = flat // segment == lax.axis_index("shard")
    piece[:, wide:] = jnp.where(here, repeated, 0.0).astype(BF16)


def copying(source, target, sem):
    copy = pltpu.make_async_copy(source, target, sem)
    copy.start()
    return copy


def wait_all(copies):
    for copy in copies:
        copy.wait()


def valid_count(lengths, n, rows):
    return jnp.clip(lengths[n] - lax.axis_index("ctx") * rows, 0, rows)


def norm_kernel(tokens, out):
    seqs, rows, width = tokens.shape
    xhat, _ = row_stats(tokens[...].reshape(seqs * rows, width).astype(F32))
    out[...] = xhat.T.astype(BF16).reshape(out.shape)


def split_lanes(wide, rows, count):
    lane = lax.broadcasted_iota(jnp.int32, (1, LANES), 1)
    pieces = []
    for n in range(count):
        at, off = divmod(n * rows, LANES)
        turn = (LANES - off) % LANES
        piece = wide[:, at * LANES : (at + 1) * LANES]
        if turn:
            piece = pltpu.roll(piece, turn, 1)
        if off + rows > LANES:
            after = pltpu.roll(wide[:, (at + 1) * LANES : (at + 2) * LANES], turn, 1)
            piece = jnp.where(lane < turn, piece, after)
        pieces.append(piece)
    return pieces


def join_lanes(pieces, rows):
    lane = lax.broadcasted_iota(jnp.int32, (1, LANES), 1)
    columns = [None] * (len(pieces) * rows // LANES)
    for n, piece in enumerate(pieces):
        at, off = divmod(n * rows, LANES)
        turned = pltpu.roll(piece, off, 1) if off else piece
        columns[at] = turned if off == 0 else jnp.where(lane < off, columns[at], turned)
        if off + rows > LANES:
            columns[at + 1] = turned
    return jnp.concatenate(columns, axis=1)


def count_of(lengths, partner, order, block, n, rows):
    core, c = order[block]
    own = lax.rem(lax.axis_index("shard"), 2) == core
    return jnp.clip(jnp.where(own, lengths[n], partner[n]) - c * rows, 0, rows)


def swap(values):
    return pltpu.roll(values, LANES // 2, values.ndim - 1)


def table_kernel(rows, pack, far_table, far_lines, firsts, table, lines, sems):
    chans = pack.shape[0]
    low2 = lax.broadcasted_iota(jnp.int32, (1, LANES), 1) < LANES // 2
    low3 = low2[None]
    angle = jnp.where(low2, 0.0, math.pi / 2)
    step = 8
    offsets = lax.broadcasted_iota(jnp.int32, (1, step, 1), 1).astype(F32)

    def spread(pair):
        other = swap(pair)
        return jnp.where(low2, pair, other), jnp.where(low2, other, pair)

    def factors(power):
        other = swap(power)
        return jnp.where(low2, power, other), jnp.where(low2, -other, power)

    def block(at, _):
        here = pl.ds(pl.multiple_of(at * step, step), step)
        decay, freq = spread(pack[here, 0:LANES])
        real, imag = spread(pack[here, LANES : 2 * LANES])

        def power(by):
            return jnp.exp(-decay * by) * jnp.cos(freq * by - angle)

        part = jnp.exp(-decay[:, None, :] * offsets) * jnp.cos(freq[:, None, :] * offsets - angle[None])
        table[here, 0:step] = part.astype(BF16)
        size = step
        while size < LANES:
            same, cross = factors(power(float(size)))
            new = part * same[:, None, :] + swap(part) * cross[:, None, :]
            table[here, size : 2 * size] = new.astype(BF16)
            part = jnp.concatenate([part, new], axis=1)
            size *= 2
        copying(table.at[here], far_table.at[here], sems.at[at])
        real = jnp.where(low2, real, -real)
        whole = part.astype(BF16)
        hat = jnp.where(low2, real, -imag).astype(BF16)
        for k in range(step):
            row = jnp.broadcast_to(hat[k : k + 1], (step, LANES))
            lines[at * step + k, 0:1] = dot(row, whole[k], (1, 1))[0:1]
        one = power(1.0)
        same, cross = factors(one)
        firsts[0, here] = same
        firsts[1, here] = cross
        chunk_same, chunk_cross = factors(power(float(rows)))
        hat_re = jnp.where(low2, real, -real)
        turn_re = hat_re * same - imag * jnp.where(low2, -cross, cross)
        turn_im = hat_re * jnp.where(low2, -cross, cross) + imag * same
        for k, line in enumerate((chunk_same, chunk_cross, jnp.where(low2, turn_re, -turn_re), -turn_im)):
            lines[here, k + 1 : k + 2] = line[:, None, :]
        return 0

    count = chans // step
    lax.fori_loop(0, count, block, 0, unroll=min(8, count))
    for at in range(count):
        here = pl.ds(at * step, step)
        pltpu.make_async_copy(table.at[here], far_table.at[here], sems.at[at]).wait()
    copying(lines, far_lines, sems.at[count]).wait()


def paired(lefts, rights, over):
    outs = []
    for k in range(0, len(lefts), 2):
        rows = lefts[k].shape[0]
        left = jnp.concatenate(lefts[k : k + 2], axis=0)
        right = jnp.concatenate(rights[k : k + 2], axis=1 - over[1])
        both = dot(left, right, over)
        outs += [both[0:rows, 0:LANES], both[rows:, LANES:]]
    return outs


def upper_half(rows):
    square = (rows, LANES)
    return lax.broadcasted_iota(jnp.int32, square, 1) >= lax.broadcasted_iota(jnp.int32, square, 0)


def toeplitz(upper, taps):
    slid = pltpu.roll(jnp.broadcast_to(taps, upper.shape), 0, 1, stride=1, stride_axis=0)
    body = jnp.where(upper, slid, 0.0).astype(BF16)
    return jnp.concatenate([body, jnp.zeros((LANES - upper.shape[0], LANES), BF16)], axis=0)


def mirror_matrix(rows):
    square = (LANES, LANES)
    reach = lax.broadcasted_iota(jnp.int32, square, 0) + lax.broadcasted_iota(jnp.int32, square, 1)
    return jnp.where(reach == rows - 1, 1.0, 0.0).astype(BF16)


def place(order, seqs, block, n):
    core, c = order[block]
    return (c * 2 + core) * seqs + n


def fetch_tables(size, far_table, table, far_lines, lines, sems):
    count = table.shape[0] // size
    copying(far_lines, lines, sems.at[count])
    for at in range(count):
        here = pl.ds(at * size, size)
        copying(far_table.at[here], table.at[here], sems.at[at])


def await_table(size, far_table, table, sems, at):
    here = pl.ds(at * size, size)
    pltpu.make_async_copy(far_table.at[here], table.at[here], sems.at[at]).wait()


def await_lines(size, far_lines, lines, sems):
    pltpu.make_async_copy(far_lines, lines, sems.at[lines.shape[0] // size]).wait()


def gelu_and_slope(x):
    c = math.sqrt(2.0 / math.pi)
    square = x * x
    t = jnp.tanh(c * x * (1.0 + 0.044715 * square))
    half = 0.5 * (1.0 + t)
    return x * half, half + 0.5 * x * (1.0 - t * t) * (c + 3.0 * 0.044715 * c * square)


def forward_kernel(
    chunks, rows, order, lengths, partner, arrived, pack, far_table, far_lines, far_hidden, far_kept,
    inputs, mirrored, mixed, hidden, kept, table, lines, sems, out_sems,
):
    size = min(GROUPS[0], far_table.shape[0])
    fetch_tables(size, far_table, table, far_lines, lines, sems)
    blocks, chans, wide = arrived.shape
    seqs = wide // rows
    total = blocks * seqs
    each = 2 * seqs
    lane = lax.broadcasted_iota(jnp.int32, (1, LANES), 1)
    gain, shift = pack[:, 257:258], pack[:, 258:259]
    mirror = mirror_matrix(rows)
    upper = upper_half(rows)
    for b in range(blocks):
        for n, xhat in enumerate(split_lanes(arrived[b].astype(F32), rows, seqs)):
            here = pl.ds(place(order, seqs, b, n) * chans, chans)
            inside = lane < count_of(lengths, partner, order, b, n, rows)
            x = jnp.where(inside, xhat * gain + shift, 0.0).astype(BF16)
            inputs[here, :] = x.astype(F32)
            mirrored[here, :] = dot(x, mirror, (1, 0))

    def group(at, _):
        members = range(size)
        await_table(size, far_table, table, sems, at)
        mine = [pl.ds(at * size + k, total, stride=chans) for k in members]
        line = [lines[at * size + k] for k in members]
        powers = [table[at * size + k] for k in members]
        ends = paired([mirrored[mine[k], :].astype(BF16) for k in members], powers, (1, 0))
        local = paired(
            [inputs[mine[k], :].astype(BF16) for k in members],
            [toeplitz(upper, line[k][0:1]) for k in members],
            (1, 0),
        )
        for k in members:
            state = ends[k][0:each]
            carried = [jnp.zeros((each, LANES), F32)]
            for c in range(1, chunks):
                carried.append(state * line[k][3:4] + swap(state) * line[k][4:5])
                if c < chunks - 1:
                    state = state * line[k][1:2] + swap(state) * line[k][2:3]
                    state += ends[k][each * c : each * (c + 1)]
            ends[k] = jnp.concatenate(carried, axis=0).astype(BF16)
        far = paired(ends, [table[at * size + k] for k in members], (1, 1))
        for k in members:
            mixed[mine[k], :] = local[k] + far[k]
        return 0

    await_lines(size, far_lines, lines, sems)
    lax.fori_loop(0, chans // size, group, 0)
    stored = []
    skip = pack[:, 256:257]
    for b in range(blocks):
        values = []
        for n in range(seqs):
            here = pl.ds(place(order, seqs, b, n) * chans, chans)
            mix = mixed[here, :] + skip * inputs[here, :]
            value, slope = gelu_and_slope(mix)
            kept[here, :] = jnp.where(lane < rows, slope, 0.0).astype(BF16)
            values.append(value)
        hidden[b] = join_lanes(values, rows).astype(BF16)
        here = pl.ds(place(order, seqs, b, 0) * chans, seqs * chans)
        stored.append(copying(hidden.at[b], far_hidden.at[b], out_sems.at[0, b]))
        stored.append(copying(kept.at[here], far_kept.at[here], out_sems.at[1, b]))
    wait_all(stored)


def glu_kernel(plan, lengths, arrived, tokens, cotangent, *refs):
    layers = plan.layers
    pieces, (block_out, leaving, outers, w) = refs[: 2 * layers], refs[2 * layers :]
    seqs, rows, width = tokens.shape
    own = width // plan.shards
    shard = lax.axis_index("shard")
    layer, core = shard // 2, lax.rem(shard, 2)
    bias = jnp.zeros((16, LANES), F32)
    for side in range(2):
        for turn in range(layers):
            piece = pieces[side * layers + turn]
            home = 2 * lax.rem(layer + layers - turn, layers) + lax.rem(core + side, 2)
            w[pl.ds(pl.multiple_of(home * own, own), own), :] = piece[:, 0 : 2 * width]
            bias += piece[0:16, 2 * width :].astype(F32)
    bias = jnp.concatenate([bias[k : k + 1] for k in range(2 * width // LANES)], axis=1)
    position = lax.broadcasted_iota(jnp.int32, (rows, width), 0)
    hidden = arrived[...].reshape(width, seqs * rows).astype(F32).T.astype(BF16)
    for n in range(seqs):
        here = slice(n * rows, (n + 1) * rows)
        proj = dot(hidden[here], w[...], (1, 0)) + bias
        r, q = proj[:, :width], proj[:, width:]
        valid = jnp.where(position < valid_count(lengths, n, rows), 1.0, 0.0)
        open_ = jax.nn.sigmoid(q)
        e = valid * cotangent[n].astype(F32)
        first = e * open_
        outers[here, :] = jnp.concatenate([first, first * r * (1.0 - open_)], axis=1).astype(BF16)
        block_out[n] = (tokens[n].astype(F32) + valid * (r * open_)).astype(BF16)
    back = dot(outers[...], w[...], (1, 1))
    leaving[...] = back.T.astype(BF16).reshape(leaving.shape)


def outer_kernel(plan, arrived, outers, kept, sent):
    chans = arrived.shape[1]
    layers, subs = plan.layers, plan.subs
    own, wide = chans * subs, outers.shape[1]
    core = lax.rem(lax.axis_index("shard"), 2)
    outer = outers[...]
    bias = jnp.sum(outer.astype(F32), axis=0, keepdims=True)
    tail = [bias[:, k * LANES : (k + 1) * LANES] for k in range(wide // LANES)]
    tail.append(jnp.zeros((own - len(tail), LANES), F32))
    tail = jnp.concatenate(tail, axis=0).astype(BF16)
    for side, out in enumerate((sent, kept)):
        which = lax.rem(core + 1 - side, 2)
        members = [(2 * z + which) * subs + sub for z in range(layers) for sub in range(subs)]
        left = jnp.concatenate([arrived[member] for member in members], axis=0)
        out[:, :, 0:wide] = dot(left, outer, (1, 0)).astype(BF16).reshape(layers, own, wide)
        for z in range(layers):
            out[z, :, wide:] = tail


def backward_kernel(
    chunks, rows, order, lengths, partner, arrived, first, pack, far_table, far_lines, far_slope,
    far_leaving, far_kept, tallies,
    grads, local, cross, slope, kept, leaving, table, lines, sems, more_sems,
):
    size = min(GROUPS[1], far_table.shape[0])
    blocks, chans, wide = arrived.shape
    seqs = wide // rows
    total = blocks * seqs
    each = 2 * seqs
    lane = lax.broadcasted_iota(jnp.int32, (1, LANES), 1)
    skip, gain = pack[:, 256:257], pack[:, 257:258]
    mirror = mirror_matrix(rows)
    upper = upper_half(rows)
    spans = [pl.ds(place(order, seqs, b, 0) * chans, seqs * chans) for b in range(blocks)]
    fetched = [
        copying(far_slope.at[span], slope.at[span], more_sems.at[0, b]) for b, span in enumerate(spans)
    ]
    fetch_tables(size, far_table, table, far_lines, lines, sems)
    stored = []
    for b in range(blocks):
        fetched[b].wait()
        for n, back in enumerate(split_lanes(arrived[b].astype(F32), rows, seqs)):
            here = pl.ds(place(order, seqs, b, n) * chans, chans)
            g = (back * slope[here, :].astype(F32)).astype(BF16)
            grads[here, :] = g.astype(F32)

    def group(at, _):
        members = range(size)
        await_table(size, far_table, table, sems, at)
        which = [at * size + k for k in members]
        mine = [pl.ds(h, total, stride=chans) for h in which]
        line = [lines[h] for h in which]
        powers = [table[h] for h in which]
        low = [grads[mine[k], :].astype(BF16) for k in members]
        ends = paired(low, powers, (1, 0))
        near = paired(low, [toeplitz(upper, line[k][0:1]) for k in members], (1, 1))
        for k in members:
            kept[which[k]] = low[k]
            local[mine[k], :] = near[k]
        for k in members:
            parts = [jnp.zeros((each, LANES), F32)]
            state = ends[k][each * (chunks - 1) :]
            for c in range(chunks - 2, -1, -1):
                parts.append(state * line[k][3:4] + swap(state) * line[k][4:5])
                if c:
                    state = state * line[k][1:2] + swap(state) * line[k][2:3]
                    state += ends[k][each * c : each * (c + 1)]
            ends[k] = jnp.concatenate(parts[::-1], axis=0).astype(BF16)
        far = paired(ends, powers, (1, 1))
        for k in members:
            cross[mine[k], :] = far[k]
        return 0

    await_lines(size, far_lines, lines, sems)
    lax.fori_loop(0, chans // size, group, 0)
    stored.append(copying(kept, far_kept, more_sems.at[1, 0]))
    gains = shifts = jnp.zeros((chans, LANES), F32)
    for b in range(blocks):
        inner = []
        for n, xhat in enumerate(split_lanes(first[b].astype(F32), rows, seqs)):
            here = pl.ds(place(order, seqs, b, n) * chans, chans)
            grad = local[here, :] + skip * grads[here, :]
            grad += dot(cross[here, :].astype(BF16), mirror, (1, 0))
            m = jnp.where(lane < count_of(lengths, partner, order, b, n, rows), grad, 0.0)
            gains += m * xhat
            shifts += m
            inner.append(gain * m)
        leaving[b] = join_lanes(inner, rows).astype(BF16)
        stored.append(copying(leaving.at[b], far_leaving.at[b], more_sems.at[2, b]))
    tallies[0] = gains
    tallies[1] = shifts
    wait_all(stored)


def prefix_kernel(
    chunks, rows, order, lengths, partner, first, pack, far_table, far_lines, far_mirrored, far_prefix,
    mirrored, kept, prefix, table, lines, sems, out_sems,
):
    size = min(GROUPS[2], far_table.shape[0])
    fetch_tables(size, far_table, table, far_lines, lines, sems)
    blocks, chans, wide = first.shape
    seqs = wide // rows
    total = blocks * seqs
    each = 2 * seqs
    lane = lax.broadcasted_iota(jnp.int32, (1, LANES), 1).astype(F32)
    gain, shift = pack[:, 257:258], pack[:, 258:259]
    mirror = mirror_matrix(rows)
    for b in range(blocks):
        for n, xhat in enumerate(split_lanes(first[b].astype(F32), rows, seqs)):
            here = pl.ds(place(order, seqs, b, n) * chans, chans)
            inside = lane < count_of(lengths, partner, order, b, n, rows).astype(F32)
            x = jnp.where(inside, xhat * gain + shift, 0.0).astype(BF16)
            mirrored[here, :] = dot(x, mirror, (1, 0))

    def group(at, _):
        members = range(size)
        await_table(size, far_table, table, sems, at)
        which = [at * size + k for k in members]
        line = [lines[h] for h in which]
        ends = []
        for k in members:
            x_back = mirrored[pl.ds(which[k], total, stride=chans), :]
            kept[which[k]] = x_back.astype(BF16)
            stack = jnp.concatenate([x_back, x_back * lane], axis=0).astype(BF16)
            ends.append(dot(stack, table[which[k]], (1, 0)))
        for k in members:

            def onward(state):
                return state * line[k][1:2] + swap(state) * line[k][2:3]

            state, slope = ends[k][0:each], ends[k][total : total + each]
            states, slopes = [state], [state + slope]
            for c in range(1, chunks - 1):
                slope = onward(slope + float(rows) * state) + ends[k][total + each * c : total + each * (c + 1)]
                state = onward(state) + ends[k][each * c : each * (c + 1)]
                states.append(state)
                slopes.append(state + slope)
            prefix[which[k]] = jnp.concatenate(states + slopes, axis=0).astype(BF16)
        return 0

    await_lines(size, far_lines, lines, sems)
    lax.fori_loop(0, chans // size, group, 0)
    wait_all([copying(kept, far_mirrored, out_sems.at[0]), copying(prefix, far_prefix, out_sems.at[1])])


def moment_kernel(
    chunks, rows, far_table, far_mirrored, far_prefix, far_grads, firsts, tallies, sums,
    cross_one_a, cross_one_b, cross_two_a, cross_two_b, local_one, local_two, corrs,
    table, mirrored, prefix, grads, sems,
):
    size = min(GROUPS[3], far_table.shape[0])
    chans, total, _ = far_grads.shape
    each = total // chunks
    count = chans // size
    pairs = (
        (far_grads, grads), (far_table, table), (far_mirrored, mirrored), (far_prefix, prefix)
    )
    for at in range(count):
        here = pl.ds(at * size, size)
        for k, (far, near) in enumerate(pairs):
            copying(far.at[here], near.at[here], sems.at[k, at])
    lane = lax.broadcasted_iota(jnp.int32, (1, LANES), 1).astype(F32)
    square = (rows, LANES)
    behind = lax.broadcasted_iota(jnp.int32, square, 1) <= (
        LANES - rows + lax.broadcasted_iota(jnp.int32, square, 0)
    )

    def group(at, _):
        members = range(size)
        which = [at * size + k for k in members]
        here = pl.ds(at * size, size)
        for k, (far, near) in enumerate(pairs):
            pltpu.make_async_copy(far.at[here], near.at[here], sems.at[k, at]).wait()
        ends, outer, both = [], [], []
        powers = [table[h] for h in which]
        for k in members:
            g = grads[which[k]]
            ends.append(jnp.concatenate([g, (g.astype(F32) * lane).astype(BF16)], axis=0))
        ends = paired(ends, powers, (1, 0))
        for k in members:
            outer.append(dot(mirrored[which[k]], grads[which[k]], (0, 0)))
        for k in members:
            one = pl.ds(which[k], 1)
            later, later_slope = ends[k][each:total], ends[k][total + each :]
            before = prefix[which[k]].astype(F32)
            state, slope = before[0 : total - each], before[total - each :]
            swapped, swapped_slope = swap(later), swap(later_slope)
            for into, value in (
                (cross_one_a, state * later),
                (cross_one_b, state * swapped),
                (cross_two_a, slope * later + state * later_slope),
                (cross_two_b, slope * swapped + state * swapped_slope),
            ):
                into[one, :] = jnp.sum(value, axis=0, keepdims=True)
            slid = pltpu.roll(outer[k][0:rows], LANES - rows + 1, 1, stride=1, stride_axis=0)
            corr = jnp.sum(jnp.where(behind, slid, 0.0), axis=0, keepdims=True)
            corrs[one, :] = corr
            pair = jnp.concatenate([corr, corr * lane, jnp.zeros((14, LANES), F32)], axis=0)
            both.append(pair)
        for k, turned in enumerate(paired([p.astype(BF16) for p in both], powers, (1, 0))):
            local_one[pl.ds(which[k], 1), :] = turned[0:1]
            local_two[pl.ds(which[k], 1), :] = turned[1:2]
        return 0

    lax.fori_loop(0, count, group, 0)
    low = lax.broadcasted_iota(jnp.int32, (1, LANES), 1) < LANES // 2
    for k, (a, b, near) in enumerate(
        ((cross_one_a, cross_one_b, local_one), (cross_two_a, cross_two_b, local_two))
    ):
        far = jnp.where(low, a[...] - swap(a[...]), b[...] + swap(b[...]))
        moment = far * firsts[0] + swap(far) * firsts[1] + near[...]
        sums[0:chans, k * LANES : (k + 1) * LANES] = moment.astype(BF16)
    diagonal = lax.broadcasted_iota(jnp.int32, (chans, 2 * LANES), 0) == lax.broadcasted_iota(
        jnp.int32, (chans, 2 * LANES), 1
    )
    row = lax.broadcasted_iota(jnp.int32, (16, 2 * LANES), 0)
    tail = jnp.zeros((16, 2 * LANES), F32)
    columns = [corrs[:, 0:1]] + [jnp.sum(tallies[k], axis=1, keepdims=True) for k in range(2)]
    for k, column in enumerate(columns):
        line = jnp.sum(jnp.where(diagonal, column, 0.0), axis=0, keepdims=True)
        tail = jnp.where(row == k, line, tail)
    sums[chans:, :] = tail.astype(BF16)


def share_kernel(layers, kept, came, *outs):
    layer = lax.axis_index("shard") // 2
    for turn, out in enumerate(outs):
        at = lax.rem(layer + turn, layers)
        out[...] = (kept[at].astype(F32) + came[at].astype(F32)).astype(BF16)


def add_kernel(*refs):
    total = refs[0][...].astype(F32)
    for ref in refs[1:-1]:
        total += ref[...].astype(F32)
    refs[-1][...] = total.astype(BF16)


def merge_kernel(subs, *refs):
    parts, (out, slots) = refs[:-2], refs[-2:]
    count = len(parts)
    mine = lax.axis_index("ctx")
    for turn, part in enumerate(parts):
        slots[lax.rem(mine // 2 + count - turn, count)] = part[...]
    total = slots[0].astype(F32)
    for k in range(1, count):
        total += slots[k].astype(F32)
    rows = total.shape[0]
    if subs == 1:
        out[...] = total.astype(BF16)
    else:
        out[...] = jnp.zeros(out.shape, BF16)
        out[pl.ds(pl.multiple_of(lax.rem(mine, subs) * rows, rows), rows), :] = total.astype(BF16)


def owner_kernel(chunks, subs, *refs):
    slabs, refs = refs[:chunks], refs[chunks:]
    one, two, decay, scale_in, real, imag = refs[:6]
    grad_weight, grad_bias, grad_decay, grad_freq, grad_real, grad_imag, *vectors, slots = refs[6:]
    own, states = decay.shape
    wide = grad_weight.shape[1]
    mine = lax.axis_index("ctx")
    for turn, slab in enumerate(slabs):
        slots[lax.rem(mine + chunks - turn, chunks)] = slab[...]
    slab = slots[0].astype(F32)
    for k in range(1, chunks):
        slab += slots[k].astype(F32)
    grad_weight[...] = slab[:, 0:wide]
    segment = grad_bias.shape[1]
    shard = lax.axis_index("shard")
    row = jnp.zeros((1, segment), F32)
    for s in range(wide // segment):
        at, off = divmod(s * segment, LANES)
        row = jnp.where(shard == s, slab[at : at + 1, wide + off : wide + off + segment], row)
    grad_bias[...] = row
    chans = own // subs
    each = chans + 16
    total = one[...].astype(F32) + two[...].astype(F32)
    sums = [total[each * sub : each * (sub + 1)] for sub in range(subs)]
    moments = jnp.concatenate([t[0:chans] for t in sums], axis=0)
    one_re, one_im, two_re, two_im = (moments[:, k * states : (k + 1) * states] for k in range(4))
    scale = scale_in[...]
    hat_re, hat_im = scale * real[...], scale * imag[...]
    grad_decay[...] = -(hat_re * two_re - hat_im * two_im) + jnp.exp(-2.0 * decay[...]) / scale * (
        real[...] * one_re - imag[...] * one_im
    )
    grad_freq[...] = -(hat_re * two_im + hat_im * two_re)
    grad_real[...] = scale * one_re
    grad_imag[...] = -scale * one_im
    for k, vector in enumerate(vectors):
        lines = [t[chans + k : chans + k + 1, 0:chans] for t in sums]
        vector[...] = jnp.concatenate(lines, axis=1) if subs > 1 else lines[0]


def final_kernel(arrived, tokens, cotangent, out):
    seqs, rows, width = tokens.shape
    inner = arrived[...].reshape(width, seqs * rows).astype(F32).T
    for n in range(seqs):
        d = inner[n * rows : (n + 1) * rows]
        xhat, inv = row_stats(tokens[n].astype(F32))
        mean = jnp.mean(d, axis=-1, keepdims=True)
        along = jnp.mean(d * xhat, axis=-1, keepdims=True)
        grad = (d - mean - xhat * along) * inv
        out[n] = (cotangent[n].astype(F32) + grad).astype(BF16)


def call(kernel, micros, outs, ins, scratch=()):
    return pl.pallas_call(
        kernel,
        out_shape=[(pltpu.HBM if len(o) > 2 else jax.ShapeDtypeStruct)(*o[:2]) for o in outs],
        in_specs=ins,
        out_specs=[HBM if len(o) > 2 else VMEM for o in outs],
        scratch_shapes=list(scratch),
        compiler_params=PARAMS,
        cost_estimate=pl.CostEstimate(
            flops=int(micros * 1e9), bytes_accessed=int(micros * 3.5e6), transcendentals=0
        ),
    )


def in_hbm(*arrays):
    return [pltpu.with_memory_space_constraint(a, pltpu.HBM) for a in arrays]


def per_device(
    plan, tokens, lengths, out_weight, out_bias, decay_rate, frequency, coef_real, coef_imag,
    skip, gain, shift, cotangent,
):
    seqs, rows, width = tokens.shape
    chunks, subs = plan.chunks, plan.subs
    blocks = 2 * chunks
    chans = width // blocks
    own, states = decay_rate.shape
    total = blocks * seqs
    mine, shard = lax.axis_index("ctx"), lax.axis_index("shard")
    layer = shard // 2

    def exchange(buffer):
        return lax.all_to_all(buffer, BOTH, 0, 0, axis_index_groups=plan.groups, tiled=True)

    segment = out_bias.shape[0]
    pack, scale, piece = call(
        pack_kernel,
        2,
        [((own, 3 * LANES), F32), ((own, states), F32), ((own, 2 * width + LANES), BF16)],
        [VMEM] * 9,
    )(
        *in_hbm(
            decay_rate, frequency, coef_real, coef_imag,
            skip[None], gain[None], shift[None], out_weight, out_bias[None],
        )
    )
    if subs > 1:
        pack = lax.dynamic_slice_in_dim(pack, lax.rem(mine, subs) * chans, chans, 0)
    pack = lax.ppermute(pack, BOTH, plan.fetch)

    def here(shape, dtype=BF16):
        return pltpu.VMEM(shape, dtype)

    def sems(*shape):
        return pltpu.SemaphoreType.DMA(shape)

    wire = ((blocks, chans, seqs * rows), BF16, 1)
    partner = lax.ppermute(lengths, "shard", plan.across)
    flow, like_tokens = wire[:2], (tokens.shape, BF16)
    on_wire = here(wire[0])
    (first,) = call(
        norm_kernel, COST[0], [flow], [VMEM]
    )(tokens)
    first = exchange(first)
    piece, pack = lax.optimization_barrier((piece, pack))
    near = [piece] + [lax.ppermute(piece, "shard", route) for route in plan.climb]
    table_type, line_type = ((chans, LANES, LANES), BF16, 1), ((chans, 8, LANES), F32, 1)
    tables = [here(*table_type[:2]), here(*line_type[:2])]
    table, lines, firsts = call(
        functools.partial(table_kernel, rows),
        COST[1],
        [table_type, line_type, ((2, chans, LANES), F32)],
        [VMEM],
        tables + [sems(chans // 8 + 1)],
    )(pack)
    far_tables = in_hbm(table, lines)
    buffer, line = here((total * chans, LANES), F32), here((chans, LANES), F32)
    low = ((total * chans, LANES), BF16, 1)
    low_buffer = here(*low[:2])
    tables.append(sems(chans // 8 + 1))
    hidden, slope = call(
        functools.partial(forward_kernel, chunks, rows, plan.order),
        COST[2],
        [wire, low],
        [SMEM, SMEM, VMEM, VMEM, HBM, HBM],
        [buffer, buffer, buffer, on_wire, low_buffer] + tables + [sems(2, blocks)],
    )(lengths, partner, first, pack, *far_tables)
    prefix_type = ((chans, 2 * (total - 2 * seqs), LANES), BF16, 1)
    by_channel = ((chans, total, LANES), BF16, 1)
    mirrored, prefix = call(
        functools.partial(prefix_kernel, chunks, rows, plan.order),
        6,
        [by_channel, prefix_type],
        [SMEM, SMEM, VMEM, VMEM, HBM, HBM],
        [buffer, here(*by_channel[:2]), here(*prefix_type[:2])] + tables + [sems(2)],
    )(lengths, partner, first, pack, *far_tables)
    hidden, near = lax.optimization_barrier((hidden, near))
    across = [lax.ppermute(p, "shard", plan.across) for p in near]
    hidden = exchange(hidden)
    hidden, mirrored, prefix = lax.optimization_barrier((hidden, mirrored, prefix))
    block_out, back, outers = call(
        functools.partial(glu_kernel, plan),
        COST[3],
        [like_tokens, flow, ((seqs * rows, 2 * width), BF16)],
        [SMEM] + [VMEM] * (3 + 2 * plan.layers),
        [here((width, 2 * width))],
    )(lengths, hidden, *in_hbm(tokens, cotangent), *near, *across)
    back = exchange(back)
    half = ((plan.layers, own, 2 * width + LANES), BF16)
    kept, sent = call(functools.partial(outer_kernel, plan), 2, [half, half], [VMEM] * 2)(
        hidden, outers
    )

    came = lax.ppermute(sent, "shard", plan.across)
    slab = ((own, 2 * width + LANES), BF16)
    shares = call(
        functools.partial(share_kernel, plan.layers), COST[6], [slab] * plan.layers, [VMEM] * 2
    )(kept, came)
    climbed = [lax.ppermute(v, "shard", route) for v, route in zip(shares[1:], plan.climb)]
    leaving, local_grads, tallies = call(
        functools.partial(backward_kernel, chunks, rows, plan.order),
        COST[4],
        [wire, by_channel, ((2, chans, LANES), F32)],
        [SMEM, SMEM, VMEM, VMEM, VMEM, HBM, HBM, HBM],
        [buffer, buffer, buffer, low_buffer, here(*by_channel[:2]), on_wire]
        + tables
        + [sems(3, blocks)],
    )(lengths, partner, back, first, pack, *far_tables, *in_hbm(slope))
    (owned,) = call(add_kernel, 1, [slab], [VMEM] * plan.layers)(shares[0], *climbed)
    wholes = [owned] + [lax.ppermute(owned, "ctx", route) for route in plan.rotate]
    tallies, owned = lax.optimization_barrier((tallies, owned))
    state = (chans + 16, 2 * LANES)
    (sums,) = call(
        functools.partial(moment_kernel, chunks, rows),
        COST[7],
        [(state, BF16)],
        [HBM] * 4 + [VMEM] * 2,
        [line] * 7
        + [tables[0], here(*by_channel[:2]), here(*prefix_type[:2]), here(*by_channel[:2])]
        + [sems(4, chans // 8)],
    )(far_tables[0], *in_hbm(mirrored, prefix, local_grads), firsts, tallies)
    leaving = exchange(leaving)
    (tokens_grad,) = call(
        final_kernel,
        COST[5],
        [like_tokens],
        [VMEM] * 3,
    )(
        leaving, *in_hbm(tokens, cotangent)
    )

    parts = [lax.ppermute(sums, BOTH, route) for route in plan.give]
    tokens_grad, parts = lax.optimization_barrier((tokens_grad, parts))
    (part,) = call(
        functools.partial(merge_kernel, subs),
        1,
        [((subs * state[0], state[1]), BF16)],
        [VMEM] * len(parts),
        [here((len(parts),) + state)],
    )(*parts)
    matrix, vector = ((own, states), F32), ((1, own), F32)
    grad_weight, grad_bias, *grads = call(
        functools.partial(owner_kernel, chunks, subs),
        2,
        [(out_weight.shape, F32), ((1, segment), F32)] + [matrix] * 4 + [vector] * 3,
        [VMEM] * (chunks + 6),
        [here((chunks,) + slab[0])],
    )(
        *wholes, part, lax.ppermute(part, "ctx", plan.beside), decay_rate, scale, coef_real, coef_imag
    )
    return (
        block_out,
        tokens_grad,
        grad_weight,
        grad_bias[0],
        *grads[:4],
        *(v[0] for v in grads[4:]),
    )


def solution(mesh):
    plan = Plan(mesh.shape["shard"], mesh.shape["ctx"])
    rows = P("shard", "ctx", None)
    matrix = P("shard", None)
    vector = P("shard")
    in_specs = (rows, vector, matrix, vector) + (matrix,) * 4 + (vector,) * 3 + (rows,)
    out_specs = (rows, rows, matrix, vector) + (matrix,) * 4 + (vector,) * 3
    return jax.shard_map(
        functools.partial(per_device, plan),
        mesh=mesh,
        in_specs=in_specs,
        out_specs=out_specs,
        check_vma=False,
    )
```
